32 devices in a mesh: dp: 4 (over y, x), seq: 8 (over z, core).
Axes of the slice: x: 2, y: 2, z: 4, core: 2. Of those that a mesh axis runs over, the one named last changes fastest.
Arguments:
- tokens: bfloat16 [32768, 512], P(('dp', 'seq')), may hold values from -6 to 6
- counts: int32 [4, 8], P('dp'), may hold values from 1 to 2048, 8192 in all within a row
- w_query: bfloat16 [512, 512], replicated, may hold values from -0.25 to 0.25
- b_query: float32 [512], replicated, may hold values from -3 to 3
- w_key: bfloat16 [512, 512], replicated, may hold values from -0.25 to 0.25
- w_value: bfloat16 [512, 512], replicated, may hold values from -0.25 to 0.25
- b_value: float32 [512], replicated, may hold values from -3 to 3
- w_out: bfloat16 [512, 512], replicated, may hold values from -3 to 3
- b_out: float32 [512], replicated, may hold values from -2 to 2
- gain_one: float32 [512], replicated, may hold values from 0.25 to 1.75
- shift_one: float32 [512], replicated, may hold values from -2 to 2
- w_up: bfloat16 [512, 1024], replicated, may hold values from -0.25 to 0.25
- b_up: float32 [1024], replicated, may hold values from -3 to 3
- w_down: bfloat16 [1024, 512], replicated, may hold values from -0.1875 to 0.1875
- b_down: float32 [512], replicated, may hold values from -2 to 2
- gain_two: float32 [512], replicated, may hold values from 0.25 to 1.75
- shift_two: float32 [512], replicated, may hold values from -2 to 2
- cotangent: bfloat16 [32768, 512], P(('dp', 'seq')), may hold values from -6 to 6
Outputs:
- layer_out: bfloat16 [32768, 512], P(('dp', 'seq'))
- input_grad: float32 [32768, 512], P(('dp', 'seq'))
- grad_w_query: float32 [512, 512], replicated
- grad_b_query: float32 [512], replicated
- grad_w_key: float32 [512, 512], replicated
- grad_w_value: float32 [512, 512], replicated
- grad_b_value: float32 [512], replicated
- grad_w_out: float32 [512, 512], replicated
- grad_b_out: float32 [512], replicated
- grad_gain_one: float32 [512], replicated
- grad_shift_one: float32 [512], replicated
- grad_w_up: float32 [512, 1024], replicated
- grad_b_up: float32 [1024], replicated
- grad_w_down: float32 [1024, 512], replicated
- grad_b_down: float32 [512], replicated
- grad_gain_two: float32 [512], replicated
- grad_shift_two: float32 [512], replicated
The draws below stay inside these ranges and needn't reach their ends.
Inputs may be any that keep to these rules, and one draw needn't show every extreme that they name: counts[g] lists the samples of the 8 datasets of group g, laid end to end over the group's 8192 rows in the order of the devices of seq; they sum to 8192 and the largest is 2048.
All inputs are finite; a program needn't handle non-finite values.
Results may differ from the reference program's by a relative error of at most 0.023.
Values may be sent and summed in bfloat16 or wider, within the bound.
No kernel may reach another device: no remote copies, remote signals or barrier semaphores. Data moves between devices by JAX's collectives and lax.ppermute only.
A program may use at most 256 MiB of HBM per device.

```python
import math
from functools import partial
import jax
import jax.numpy as jnp
import numpy as np
from jax import lax

D = 512
H = 4
HD = 128
FF = 1024
TOK_DEV = 1024
MAXLEN = 2048
DSETS = 8
GROUP = 8192
TOKENS = 32768
N_DP = 4
N_SEQ = 8


def level_of(key, dims, shards, smallest, largest):
    factor_of = 1.0
    for position, blocks in shards:
        steps = jax.random.uniform(jax.random.fold_in(jax.random.fold_in(key, 6), position), (blocks,), jnp.float32, smallest / len(shards), largest / len(shards))
        factor_of = factor_of * jnp.repeat(jnp.exp(steps), dims[position] // blocks).reshape((-1,) + (1,) * (len(dims) - 1 - position))
    return factor_of


def length_profile(amount, total, bound, lean):
    weights = [(1 << 20) // math.isqrt(standing ** lean) + 1 for standing in range(2, amount + 1)]
    surplus, holding = total - bound - (amount - 1), [1] * (amount - 1)
    while surplus > 0:
        free = [i for i in range(amount - 1) if holding[i] < bound]
        mass, remaining = sum([weights[i] for i in free]), surplus
        for i in free:
            extra = min(bound - holding[i], max(1, remaining * weights[i] // mass), surplus)
            holding[i] = holding[i] + extra
            surplus = surplus - extra
    return np.array([bound] + holding)


def uneven_parts(rng, number_of, total, bound, slope):
    if number_of == 2:
        one = jax.random.randint(rng, (), max(1, total - bound), min(bound, total - 1) + 1)
        return jnp.stack([one, total - one])
    sizes = jnp.asarray(length_profile(number_of, total, bound, slope), jnp.int32)
    pairs = (number_of - 1) // 2
    source_of, sink = sizes[1:1 + 2 * pairs:2], sizes[2:2 + 2 * pairs:2]
    margin = jnp.minimum(source_of - 1, bound - sink)
    shifted = jax.random.randint(jax.random.fold_in(rng, 1), (pairs,), 0, 1 << 20) % (margin + 1)
    sizes = sizes.at[1:1 + 2 * pairs:2].set(source_of - shifted).at[2:2 + 2 * pairs:2].set(sink + shifted)
    return sizes[jax.random.permutation(jax.random.fold_in(rng, 2), number_of)]


def bell_draw(own_key, dims, scale, reach, shards=(), kind=jnp.bfloat16):
    entries = scale * jax.random.normal(own_key, dims, jnp.float32)
    if shards:
        entries = entries * level_of(own_key, dims, shards, -0.22, 0.18)
    return jnp.clip(entries, -reach, reach).astype(kind)


def setup_inputs(seed: int = 0) -> dict:
    splits = jax.random.split(jax.random.key(seed), 19)
    return {
        "tokens": bell_draw(splits[0], (TOKENS, D), 1.0, 6.0, ((0, 32),)),
        "counts": jax.vmap(lambda own: uneven_parts(own, DSETS, GROUP, MAXLEN, 2))(jax.random.split(splits[1], N_DP)).reshape((N_DP, DSETS)).astype(jnp.int32),
        "w_query": bell_draw(splits[2], (D, D), D ** -0.5, 0.25),
        "b_query": bell_draw(splits[3], (D,), 0.5, 3.0, (), jnp.float32),
        "w_key": bell_draw(splits[4], (D, D), D ** -0.5, 0.25),
        "w_value": bell_draw(splits[5], (D, D), D ** -0.5, 0.25),
        "b_value": bell_draw(splits[6], (D,), 0.5, 3.0, (), jnp.float32),
        "w_out": bell_draw(splits[7], (D, D), (max(1, D // 128)) ** -0.5, 3.0),
        "b_out": bell_draw(splits[8], (D,), 0.3, 2.0, (), jnp.float32),
        "gain_one": jnp.clip(1.0 + 0.15 * jax.random.normal(splits[9], (D,), jnp.float32), 0.25, 1.75),
        "shift_one": bell_draw(splits[10], (D,), 0.3, 2.0, (), jnp.float32),
        "w_up": bell_draw(splits[11], (D, FF), D ** -0.5, 0.25),
        "b_up": bell_draw(splits[12], (FF,), 0.5, 3.0, (), jnp.float32),
        "w_down": bell_draw(splits[13], (FF, D), FF ** -0.5, 0.1875),
        "b_down": bell_draw(splits[14], (D,), 0.3, 2.0, (), jnp.float32),
        "gain_two": jnp.clip(1.0 + 0.15 * jax.random.normal(splits[15], (D,), jnp.float32), 0.25, 1.75),
        "shift_two": bell_draw(splits[16], (D,), 0.3, 2.0, (), jnp.float32),
        "cotangent": bell_draw(splits[17], (TOKENS, D), 1.0, 6.0, ((0, 32),)),
    }


NEG = -1e+30
EPS = 1e-05
HI = lax.Precision.HIGHEST

@jax.custom_vjp
def low(v):
    return lax.optimization_barrier(v.astype(jnp.bfloat16)).astype(jnp.float32)

@jax.custom_vjp
def low_back(v):
    return v

def low_keep(v):
    return (low(v), None)

def low_pass(kept, grad):
    return (grad,)

def back_keep(v):
    return (v, None)

def back_low(kept, grad):
    return (low(grad),)
low.defvjp(low_keep, low_pass)
low_back.defvjp(back_keep, back_low)

def matmul(left, right):
    return jnp.dot(left, right, precision=HI, preferred_element_type=jnp.float32)

def layer_norm(rows, gain, shift):
    centre = rows - lax.optimization_barrier(jnp.mean(rows, axis=-1, keepdims=True))
    spread = lax.optimization_barrier(jnp.mean(centre * centre, axis=-1, keepdims=True))
    return centre * lax.rsqrt(spread + EPS) * gain + shift

def seg_group(count_row, rows):
    ends = jnp.cumsum(count_row)
    places = jnp.arange(rows, dtype=jnp.int32)
    return lax.optimization_barrier(jnp.sum((places[:, None] >= ends[None, :]).astype(jnp.int32), axis=1))

def group_attend(item):
    query_blocks, seg_blocks, keys, values, segment = item
    scale = 1.0 / math.sqrt(HD)

    @jax.checkpoint
    def block(pair):
        query_blk, seg_blk = pair
        raw = jnp.einsum('qhd,khd->qhk', query_blk, keys, precision=HI)
        scores = low_back(raw) * scale
        allowed = (seg_blk[:, None] == segment[None, :])[:, None, :]
        scores = jnp.where(allowed, scores, NEG)
        top = lax.optimization_barrier(jnp.max(scores, axis=-1, keepdims=True))
        expo = jnp.where(allowed, jnp.exp(scores - top), 0.0)
        prob = expo / lax.optimization_barrier(jnp.sum(expo, axis=-1, keepdims=True))
        return jnp.einsum('qhk,khd->qhd', low(prob), values, precision=HI)
    return lax.map(block, (query_blocks, seg_blocks))

def forward(segments, xf, w_query, b_query, w_key, w_value, b_value, w_out, b_out, gain_one, shift_one, w_up, b_up, w_down, b_down, gain_two, shift_two):
    query = low(low_back(matmul(xf, w_query) + b_query))
    key = low(low_back(matmul(xf, w_key)))
    value = low(low_back(matmul(xf, w_value) + b_value))
    group_rows = N_SEQ * TOK_DEV
    attended = lax.map(group_attend, (query.reshape(N_DP, N_SEQ, TOK_DEV, H, HD), segments.reshape(N_DP, N_SEQ, TOK_DEV), key.reshape(N_DP, group_rows, H, HD), value.reshape(N_DP, group_rows, H, HD), segments))
    attended = attended.reshape(N_DP * group_rows, H * HD)
    att_low = low(low_back(attended))
    first_sum = xf + low_back(matmul(att_low, w_out) + b_out)
    normed = layer_norm(first_sum, gain_one, shift_one)
    pre = low_back(matmul(low(normed), w_up) + b_up)
    act = low(jax.nn.gelu(pre, approximate=False))
    second_sum = normed + low_back(matmul(act, w_down) + b_down)
    return layer_norm(second_sum, gain_two, shift_two)

def reference(tokens, counts, w_query, b_query, w_key, w_value, b_value, w_out, b_out, gain_one, shift_one, w_up, b_up, w_down, b_down, gain_two, shift_two, cotangent):
    segments = jax.vmap(lambda row: seg_group(row, N_SEQ * TOK_DEV))(counts)
    floats = [arr.astype(jnp.float32) for arr in (tokens, w_query, b_query, w_key, w_value, b_value, w_out, b_out, gain_one, shift_one, w_up, b_up, w_down, b_down, gain_two, shift_two)]
    layer, back = jax.vjp(partial(forward, segments), *floats)
    grads = back(cotangent.astype(jnp.float32))
    return (layer.astype(jnp.bfloat16), grads[0], grads[1], grads[2], grads[3], grads[4], grads[5], grads[6], grads[7], grads[8], grads[9], grads[10], grads[11], grads[12], grads[13], grads[14], grads[15])
```

```python
import functools
import math

import jax
import jax.numpy as jnp
from jax import lax
from jax.experimental import pallas as pl
from jax.experimental.pallas import tpu as pltpu
from jax.sharding import PartitionSpec as P

H = 4
HD = 128
EPS = 1e-05
BIG = 1e30
T = 256
LANES = 128
SCALE = 1.0 / math.sqrt(HD)
LOG2E = 1.0 / math.log(2.0)
LN2 = math.log(2.0)
F32 = jnp.float32
BF16 = jnp.bfloat16
VMEM_LIMIT = 58 * 1024 * 1024

NN = (((1,), (0,)), ((), ()))
NT = (((1,), (1,)), ((), ()))
TN = (((0,), (0,)), ((), ()))


def dot(left, right, dims=NN):
    return lax.dot_general(left, right, dims, preferred_element_type=F32)


def head(h):
    return slice(h * HD, (h + 1) * HD)


def query_mask(bcol_ref, start):
    place = start + lax.broadcasted_iota(jnp.int32, (LANES, T), 1)
    inside = jnp.logical_and(place >= bcol_ref[:, 0:1], place < bcol_ref[:, 1:2])
    return jnp.where(inside, 1.0, 0.0).astype(BF16)


def key_mask(brow_ref, start):
    place = start + lax.broadcasted_iota(jnp.int32, (T, LANES), 0)
    inside = jnp.logical_and(place >= brow_ref[0:1, :], place < brow_ref[1:2, :])
    return jnp.where(inside, 0.0, -BIG).astype(BF16)


def tile_range(lo, hi, start, tiles):
    first = jnp.clip((lo - start) // T, 0, tiles)
    last = jnp.clip((hi - start + T - 1) // T, 0, tiles)
    return first, last


def meta_parts(meta_ref, nq):
    los = [meta_ref[i] for i in range(nq)]
    his = [meta_ref[nq + i] for i in range(nq)]
    return los, his, lambda b: meta_ref[2 * nq + b]


def attend(meta_ref, first_block, blocks, nq, qt_ref, k_ref, vt_ref, km_ref, qm_ref, acc_ref, load, finish):
    def query_tile(i, carry):
        q0 = pl.multiple_of(i * T, T)
        lo = meta_ref[i]
        hi = meta_ref[nq + i]
        tops, totals = load(q0)

        def block(b, state):
            first, last = tile_range(lo, hi, meta_ref[2 * nq + first_block + b], nq)

            def step(t, inner):
                kk = b * nq + t
                k0 = pl.multiple_of(kk * T, T)
                tops, totals = inner
                new_tops, new_totals = [], []
                for h in range(H):
                    kx = jnp.concatenate([k_ref[pl.ds(k0, T), head(h)], km_ref[kk]], axis=1)
                    qx = jnp.concatenate([qt_ref[head(h), pl.ds(q0, T)], qm_ref[i]], axis=0)
                    s = dot(kx, qx)
                    top = jnp.maximum(tops[h], jnp.max(s, axis=0, keepdims=True))
                    decay = jnp.exp2(tops[h] - top)
                    p = jnp.exp2(s - top)
                    new_totals.append(totals[h] * decay + jnp.sum(p, axis=0, keepdims=True))
                    new_tops.append(top)
                    acc_ref[head(h), pl.ds(q0, T)] = acc_ref[head(h), pl.ds(q0, T)] * decay + dot(
                        vt_ref[kk, head(h), :], p.astype(BF16)
                    )
                return tuple(new_tops), tuple(new_totals)

            return lax.fori_loop(first, last, step, state)

        state = lax.fori_loop(0, blocks, block, (tops, totals))
        finish(q0, *state)
        return carry

    lax.fori_loop(0, nq, query_tile, 0)


def project_keys(meta_ref, brow_ref, b, local, nq, x_ref, wk_ref, wv_ref, bv_ref, k_ref, v_ref, vt_ref, km_ref):
    start = meta_ref[2 * nq + b]
    first, last = tile_range(meta_ref[0], meta_ref[2 * nq - 1], start, nq)

    def step(t, carry):
        r0 = pl.multiple_of(t * T, T)
        kk = local * nq + t
        k0 = pl.multiple_of(kk * T, T)
        x = x_ref[pl.ds(r0, T), :]
        k_ref[pl.ds(k0, T), :] = dot(x, wk_ref[...]).astype(BF16)
        v = (dot(x, wv_ref[...]) + bv_ref[...]).astype(BF16)
        v_ref[pl.ds(k0, T), :] = v
        vt_ref[kk] = v.T
        km_ref[kk] = key_mask(brow_ref, start + r0)
        return carry

    lax.fori_loop(first, last, step, 0)


def attend_chip_kernel(
    nq,
    meta_ref, brow_ref, bcol_ref, x_ref, xp_ref, wq_ref, bq_ref, wk_ref, wv_ref, bv_ref,
    qt_ref, k_ref, v_ref, top_ref, total_ref, acc_ref,
    vt_ref, km_ref, qm_ref,
):
    own = meta_ref[2 * nq]

    def make_query(i, carry):
        q0 = pl.multiple_of(i * T, T)
        q = (dot(x_ref[pl.ds(q0, T), :], wq_ref[...]) + bq_ref[...]) * (SCALE * LOG2E)
        qt_ref[:, pl.ds(q0, T)] = q.astype(BF16).T
        qm_ref[i] = query_mask(bcol_ref, own + q0)
        return carry

    lax.fori_loop(0, nq, make_query, 0)
    project_keys(meta_ref, brow_ref, 0, 0, nq, x_ref, wk_ref, wv_ref, bv_ref, k_ref, v_ref, vt_ref, km_ref)
    project_keys(meta_ref, brow_ref, 1, 1, nq, xp_ref, wk_ref, wv_ref, bv_ref, k_ref, v_ref, vt_ref, km_ref)
    acc_ref[...] = jnp.zeros_like(acc_ref)

    def load(q0):
        return (
            tuple(jnp.full((1, T), -BIG, F32) for _ in range(H)),
            tuple(jnp.zeros((1, T), F32) for _ in range(H)),
        )

    def finish(q0, tops, totals):
        for h in range(H):
            top_ref[h : h + 1, pl.ds(q0, T)] = tops[h]
            total_ref[h : h + 1, pl.ds(q0, T)] = totals[h]

    attend(meta_ref, 0, 2, nq, qt_ref, k_ref, vt_ref, km_ref, qm_ref, acc_ref, load, finish)


def attend_far_kernel(
    nq,
    meta_ref, brow_ref, bcol_ref, xn_ref, xf_ref, xw_ref, wk_ref, wv_ref, bv_ref,
    qt_ref, top_ref, total_ref, acc_in_ref,
    k_ref, v_ref, att_ref, attt_ref, lse_ref,
    vt_ref, km_ref, qm_ref,
):
    own = meta_ref[2 * nq]

    def make_mask(i, carry):
        qm_ref[i] = query_mask(bcol_ref, own + i * T)
        return carry

    lax.fori_loop(0, nq, make_mask, 0)
    for local, rows in enumerate((xn_ref, xf_ref, xw_ref)):
        project_keys(
            meta_ref, brow_ref, 2 + local, local, nq, rows, wk_ref, wv_ref, bv_ref, k_ref, v_ref, vt_ref, km_ref
        )
    attt_ref[...] = acc_in_ref[...]

    def load(q0):
        return (
            tuple(top_ref[h : h + 1, pl.ds(q0, T)] for h in range(H)),
            tuple(total_ref[h : h + 1, pl.ds(q0, T)] for h in range(H)),
        )

    def finish(q0, tops, totals):
        for h in range(H):
            lse_ref[h : h + 1, pl.ds(q0, T)] = tops[h] + jnp.log2(totals[h])
            att = attt_ref[head(h), pl.ds(q0, T)] / totals[h]
            attt_ref[head(h), pl.ds(q0, T)] = att
            att_ref[pl.ds(q0, T), head(h)] = att.T.astype(BF16)

    attend(meta_ref, 2, 3, nq, qt_ref, k_ref, vt_ref, km_ref, qm_ref, attt_ref, load, finish)


def column_sum(rows):
    return jnp.sum(rows, axis=0, keepdims=True)


def middle_kernel(
    x_ref, cot_ref, att_ref, attt_ref, wo_ref, wu_ref, wd_ref, vec_ref, bup_ref,
    layer_ref, dfirst_ref, dot_ref, delta_ref, grads_ref, small_ref,
    gd_ref, gu_ref, go_ref,
):
    step = pl.program_id(0)
    width = x_ref.shape[1]
    hidden = wu_ref.shape[1]
    b_out, gain_one, shift_one = vec_ref[0:1, :], vec_ref[1:2, :], vec_ref[2:3, :]
    b_down, gain_two, shift_two = vec_ref[3:4, :], vec_ref[4:5, :], vec_ref[5:6, :]

    @pl.when(step == 0)
    def _():
        gd_ref[...] = jnp.zeros_like(gd_ref)
        gu_ref[...] = jnp.zeros_like(gu_ref)
        go_ref[...] = jnp.zeros_like(go_ref)
        small_ref[...] = jnp.zeros_like(small_ref)

    def mean(rows):
        return jnp.mean(rows, axis=-1, keepdims=True)

    def norm(rows):
        centre = rows - mean(rows)
        inverse = lax.rsqrt(mean(centre * centre) + EPS)
        return centre * inverse, inverse

    def norm_back(grad, n, inverse):
        return inverse * (grad - mean(grad) - n * mean(grad * n))

    att = att_ref[...]
    first_sum = x_ref[...].astype(F32) + dot(att, wo_ref[...]) + b_out
    n_one, inv_one = norm(first_sum)
    normed = n_one * gain_one + shift_one
    normed_low = normed.astype(BF16)
    pre = dot(normed_low, wu_ref[...]) + bup_ref[...]
    cdf = 0.5 * (1.0 + lax.erf(pre * math.sqrt(0.5)))
    act_low = (pre * cdf).astype(BF16)
    slope = cdf + pre * (jnp.exp(-0.5 * pre * pre) * (1.0 / math.sqrt(2.0 * math.pi)))
    second_sum = normed + dot(act_low, wd_ref[...]) + b_down
    n_two, inv_two = norm(second_sum)
    layer_ref[...] = (n_two * gain_two + shift_two).astype(BF16)
    cot = cot_ref[...].astype(F32)
    d_sum = norm_back(cot * gain_two, n_two, inv_two)
    d_ffn = d_sum.astype(BF16)
    gd_ref[...] += dot(act_low, d_ffn, TN)
    d_pre = (dot(d_ffn, wd_ref[...], NT) * slope).astype(BF16)
    gu_ref[...] += dot(normed_low, d_pre, TN)
    d_normed = d_sum + dot(d_pre, wu_ref[...], NT)
    d_first = norm_back(d_normed * gain_one, n_one, inv_one)
    dfirst_ref[...] = d_first
    d_branch = d_first.astype(BF16)
    go_ref[...] += dot(att, d_branch, TN)
    d_att = dot(wo_ref[...], d_branch, NT).astype(BF16)
    dot_ref[...] = d_att
    for h in range(H):
        delta_ref[h : h + 1, :] = column_sum(d_att[head(h), :].astype(F32) * attt_ref[head(h), :])
    up = column_sum(d_pre.astype(F32))
    sums = [
        column_sum(d_branch.astype(F32)),
        column_sum(d_normed * n_one),
        column_sum(d_normed),
        column_sum(d_ffn.astype(F32)),
        column_sum(cot * n_two),
        column_sum(cot),
    ]
    for at in range(0, hidden, width):
        sums.append(up[:, at : at + width])
    for number, row in enumerate(sums):
        small_ref[number : number + 1, :] += row

    @pl.when(step == pl.num_programs(0) - 1)
    def _():
        grads_ref[0:hidden, :] = gd_ref[...].astype(BF16)
        for part in range(hidden // width):
            at = hidden + part * width
            grads_ref[at : at + width, :] = gu_ref[:, part * width : (part + 1) * width].astype(BF16)
        grads_ref[2 * hidden : 2 * hidden + width, :] = go_ref[...].astype(BF16)


def attend_back(
    meta_ref, brow_ref, b, local, nq, x_ref, k_ref, v_ref, qt_ref, dot_ref, lse_ref, delta_ref,
    wk_ref, wv_ref, kt_ref, km_ref, qm_ref, dk_ref, dv_ref, dq_ref, dwk_ref, dwv_ref, bv_ref, write,
):
    start = meta_ref[2 * nq + b]
    first, last = tile_range(meta_ref[0], meta_ref[2 * nq - 1], start, nq)

    def key_tile(t, carry):
        r0 = pl.multiple_of(t * T, T)
        k0 = pl.multiple_of((local * nq + t) * T, T)
        row = start + r0
        q_first = sum((meta_ref[nq + i] <= row).astype(jnp.int32) for i in range(nq))
        q_last = sum((meta_ref[i] < row + T).astype(jnp.int32) for i in range(nq))
        km_ref[...] = key_mask(brow_ref, row)
        kt_ref[...] = k_ref[pl.ds(k0, T), :].T
        dk_ref[...] = jnp.zeros_like(dk_ref)
        dv_ref[...] = jnp.zeros_like(dv_ref)

        def query_tile(i, inner):
            q0 = pl.multiple_of(i * T, T)
            for h in range(H):
                kx = jnp.concatenate([k_ref[pl.ds(k0, T), head(h)], km_ref[...]], axis=1)
                qt = qt_ref[head(h), pl.ds(q0, T)]
                qx = jnp.concatenate([qt, qm_ref[i]], axis=0)
                d_att = dot_ref[head(h), pl.ds(q0, T)]
                p = jnp.exp2(dot(kx, qx) - lse_ref[h : h + 1, pl.ds(q0, T)])
                dp = dot(v_ref[pl.ds(k0, T), head(h)], d_att)
                ds = (p * (dp - delta_ref[h : h + 1, pl.ds(q0, T)])).astype(BF16)
                dv_ref[head(h), :] += dot(d_att, p.astype(BF16), NT)
                dk_ref[head(h), :] += dot(qt, ds, NT)
                dq_ref[head(h), pl.ds(q0, T)] += dot(kt_ref[head(h), :], ds)
            return inner

        lax.fori_loop(q_first, q_last, query_tile, 0)
        x = x_ref[pl.ds(r0, T), :]
        dk = (dk_ref[...] * LN2).astype(BF16)
        dv = dv_ref[...].astype(BF16)
        dwk_ref[...] += dot(dk, x)
        dwv_ref[...] += dot(dv, x)
        bv_ref[:, 0:1] += jnp.sum(dv.astype(F32), axis=1, keepdims=True)
        write(r0, dot(wk_ref[...], dk) + dot(wv_ref[...], dv))
        return carry

    lax.fori_loop(first, last, key_tile, 0)


def back_far_kernel(
    nq,
    meta_ref, brow_ref, bcol_ref, xn_ref, xf_ref, xw_ref, k_ref, v_ref, qt_ref, dot_ref, lse_ref, delta_ref,
    wk_ref, wv_ref,
    pn_ref, pf_ref, pw_ref, dq_ref, dwk_ref, dwv_ref, bv_ref,
    kt_ref, km_ref, qm_ref, dk_ref, dv_ref,
):
    own = meta_ref[2 * nq]

    def make_mask(i, carry):
        qm_ref[i] = query_mask(bcol_ref, own + i * T)
        return carry

    lax.fori_loop(0, nq, make_mask, 0)
    for ref in (dq_ref, dwk_ref, dwv_ref, bv_ref):
        ref[...] = jnp.zeros_like(ref)
    for local, (rows, out) in enumerate(((xn_ref, pn_ref), (xf_ref, pf_ref), (xw_ref, pw_ref))):
        out[...] = jnp.zeros_like(out)

        def write(r0, grad, out=out):
            out[pl.ds(r0, T), :] = grad.T.astype(BF16)

        attend_back(
            meta_ref, brow_ref, 2 + local, local, nq, rows, k_ref, v_ref, qt_ref, dot_ref, lse_ref, delta_ref,
            wk_ref, wv_ref, kt_ref, km_ref, qm_ref, dk_ref, dv_ref, dq_ref, dwk_ref, dwv_ref, bv_ref, write,
        )


def back_chip_kernel(
    nq,
    meta_ref, brow_ref, bcol_ref, x_ref, xp_ref, k_ref, v_ref, qt_ref, dot_ref, lse_ref, delta_ref,
    wk_ref, wv_ref, wq_ref, dq_in_ref, dwk_in_ref, dwv_in_ref, bv_in_ref, dfirst_ref, small_ref,
    pp_ref, ig_ref, grads_ref,
    kt_ref, km_ref, qm_ref, dk_ref, dv_ref, dq_ref, dwk_ref, dwv_ref, bv_ref,
):
    own = meta_ref[2 * nq]
    width = x_ref.shape[1]

    def make_mask(i, carry):
        qm_ref[i] = query_mask(bcol_ref, own + i * T)
        return carry

    lax.fori_loop(0, nq, make_mask, 0)
    for ref, source in (
        (dq_ref, dq_in_ref), (dwk_ref, dwk_in_ref), (dwv_ref, dwv_in_ref), (bv_ref, bv_in_ref), (ig_ref, dfirst_ref)
    ):
        ref[...] = source[...]
    pp_ref[...] = jnp.zeros_like(pp_ref)

    def write_partner(r0, grad):
        pp_ref[pl.ds(r0, T), :] = grad.T.astype(BF16)

    def write_own(r0, grad):
        ig_ref[pl.ds(r0, T), :] += grad.T

    for b, (rows, write) in enumerate(((x_ref, write_own), (xp_ref, write_partner))):
        attend_back(
            meta_ref, brow_ref, b, b, nq, rows, k_ref, v_ref, qt_ref, dot_ref, lse_ref, delta_ref,
            wk_ref, wv_ref, kt_ref, km_ref, qm_ref, dk_ref, dv_ref, dq_ref, dwk_ref, dwv_ref, bv_ref, write,
        )
    grads_ref[width : 2 * width, :] = dwk_ref[...].T.astype(BF16)
    grads_ref[2 * width : 3 * width, :] = dwv_ref[...].T.astype(BF16)
    dwk_ref[...] = jnp.zeros_like(dwk_ref)

    def query_tile(i, carry):
        q0 = pl.multiple_of(i * T, T)
        dq = (dq_ref[:, pl.ds(q0, T)] * SCALE).astype(BF16)
        dwk_ref[...] += dot(dq, x_ref[pl.ds(q0, T), :])
        bv_ref[:, 1:2] += jnp.sum(dq.astype(F32), axis=1, keepdims=True)
        ig_ref[pl.ds(q0, T), :] += dot(wq_ref[...], dq).T
        return carry

    lax.fori_loop(0, nq, query_tile, 0)
    grads_ref[0:width, :] = dwk_ref[...].T.astype(BF16)
    rows = jnp.concatenate([bv_ref[...].T[0:8, :], small_ref[...]], axis=0)
    grads_ref[3 * width : 3 * width + 16, :] = rows.astype(BF16)
    grads_ref[3 * width + 16 :, :] = jnp.zeros((grads_ref.shape[0] - 3 * width - 16, width), BF16)


def vmem(count):
    return [pl.BlockSpec(memory_space=pltpu.VMEM)] * count


def call(kernel, inputs, outputs, scratch, flops, grid=None, in_specs=None, out_specs=None):
    extra = {} if grid is None else {"grid": grid}
    if in_specs is None:
        in_specs = [pl.BlockSpec(memory_space=pltpu.SMEM)] + vmem(len(inputs) - 1)
        out_specs = vmem(len(outputs))
    moved = sum(math.prod(a.shape) * a.dtype.itemsize for a in list(inputs) + list(outputs))
    return pl.pallas_call(
        kernel,
        out_shape=outputs,
        in_specs=in_specs,
        out_specs=out_specs,
        scratch_shapes=scratch,
        compiler_params=pltpu.CompilerParams(vmem_limit_bytes=VMEM_LIMIT),
        cost_estimate=pl.CostEstimate(flops=flops, bytes_accessed=moved, transcendentals=0),
        **extra,
    )(*inputs)


def struct(shape, dtype):
    return jax.ShapeDtypeStruct(shape, dtype)


def sum_everywhere(rows, dp, seq):
    dp_masks = [seq * (1 << j) for j in range(dp.bit_length() - 1)]
    seq_masks = [1 << j for j in range(seq.bit_length() - 1)]
    steps = [(seq_masks[0], seq_masks[0])]
    for j in range(len(dp_masks)):
        steps.append((dp_masks[j], dp_masks[(j + 1) % len(dp_masks)]))
    for mask in seq_masks[1:]:
        steps.append((mask, mask))
    core = lax.axis_index("seq") % 2
    index = lax.axis_index("dp") * seq + lax.axis_index("seq")
    taken = []
    for even, odd in steps:
        pairs = [(i, i ^ (even if i % 2 == 0 else odd)) for i in range(dp * seq)]
        bit = jnp.where(core == 0, index // even, index // odd) % 2
        half = rows.shape[0] // 2
        mine = lax.dynamic_slice_in_dim(rows, bit * half, half, 0)
        other = lax.dynamic_slice_in_dim(rows, (1 - bit) * half, half, 0)
        rows = mine + lax.ppermute(other, ("dp", "seq"), pairs)
        taken.append((pairs, bit))
    for pairs, bit in taken[::-1]:
        got = lax.ppermute(rows, ("dp", "seq"), pairs)
        half = rows.shape[0]
        whole = jnp.zeros((2 * half, rows.shape[1]), rows.dtype)
        whole = lax.dynamic_update_slice_in_dim(whole, rows, bit * half, 0)
        rows = lax.dynamic_update_slice_in_dim(whole, got, (1 - bit) * half, 0)
    return rows


def shards(
    tokens, counts, w_query, b_query, w_key, w_value, b_value, w_out, b_out, gain_one, shift_one,
    w_up, b_up, w_down, b_down, gain_two, shift_two, cotangent,
):
    shard, width = tokens.shape
    hidden = w_up.shape[1]
    nq = shard // T
    seq = lax.axis_size("seq")
    dp = lax.axis_size("dp")
    position = lax.axis_index("seq")

    def swap(rows):
        return lax.ppermute(rows, "seq", [(i, i ^ 1) for i in range(seq)])

    def near(rows):
        pairs = [(i, i + 1) for i in range(1, seq - 1, 2)]
        return lax.ppermute(rows, "seq", pairs + [(b, a) for a, b in pairs])

    def far(rows, back=False):
        pairs = [(i, i + 2) for i in range(0, seq - 2, 2)] + [(i, i - 2) for i in range(3, seq, 2)]
        return lax.ppermute(rows, "seq", [(b, a) for a, b in pairs] if back else pairs)

    x_near = near(tokens)
    x_far = far(tokens)
    x_partner = swap(tokens)
    x_forward = swap(x_near)

    side = jnp.where(position % 2 == 0, -1, 1)
    places = position + jnp.stack([0 * side, -side, side, 2 * side, -2 * side])
    blocks = jnp.where(jnp.logical_and(places >= 0, places < seq), places * shard, 1 << 28)
    ends = jnp.cumsum(counts[0])
    starts = ends - counts[0]
    firsts = position * shard + T * jnp.arange(nq, dtype=jnp.int32)
    lasts = firsts + (T - 1)
    lo = jnp.max(jnp.where(starts[None, :] <= firsts[:, None], starts[None, :], 0), axis=1)
    hi = jnp.min(jnp.where(ends[None, :] > lasts[:, None], ends[None, :], seq * shard), axis=1)
    meta = jnp.concatenate([lo, hi, blocks]).astype(jnp.int32)
    bounds = jnp.zeros((8, LANES), jnp.int32)
    bounds = bounds.at[0, : starts.shape[0]].set(starts).at[1, : starts.shape[0]].set(ends)
    bounds_t = bounds.T

    row = lambda v: v.reshape(1, -1)
    tile_mask = pltpu.VMEM((nq, LANES, T), BF16)

    def keys_scratch(blocks):
        return [pltpu.VMEM((blocks * nq, width, T), BF16), pltpu.VMEM((blocks * nq, T, LANES), BF16), tile_mask]

    unit = 2 * shard * width * width
    qt, k_chip, v_chip, top, total, acc = call(
        functools.partial(attend_chip_kernel, nq),
        (meta, bounds, bounds_t, tokens, x_partner, w_query, row(b_query), w_key, w_value, row(b_value)),
        (
            struct((width, shard), BF16), struct((2 * shard, width), BF16), struct((2 * shard, width), BF16),
            struct((8, shard), F32), struct((8, shard), F32), struct((width, shard), F32),
        ),
        keys_scratch(2),
        13 * unit,
    )
    k_far, v_far, att, att_t, lse = call(
        functools.partial(attend_far_kernel, nq),
        (meta, bounds, bounds_t, x_near, x_far, x_forward, w_key, w_value, row(b_value), qt, top, total, acc),
        (
            struct((3 * shard, width), BF16), struct((3 * shard, width), BF16), struct((shard, width), BF16),
            struct((width, shard), F32), struct((8, shard), F32),
        ),
        keys_scratch(3),
        10 * unit,
    )

    vectors = jnp.stack([b_out, gain_one, shift_one, b_down, gain_two, shift_two, b_out, b_out])
    by_row = lambda columns: pl.BlockSpec((T, columns), lambda i: (i, 0))
    by_column = lambda rows: pl.BlockSpec((rows, T), lambda i: (0, i))
    whole = lambda a: pl.BlockSpec(a.shape, lambda i: (0, 0))
    early_rows = 2 * hidden + width
    ins = (tokens, cotangent, att, att_t, w_out, w_up, w_down, vectors, row(b_up))
    outs = (
        struct((shard, width), BF16), struct((shard, width), F32), struct((width, shard), BF16),
        struct((8, shard), F32), struct((early_rows, width), BF16), struct((8, width), F32),
    )
    layer, d_first, d_att, delta, early, small = call(
        middle_kernel,
        ins,
        outs,
        [pltpu.VMEM((hidden, width), F32), pltpu.VMEM((width, hidden), F32), pltpu.VMEM((width, width), F32)],
        15 * unit,
        grid=(nq,),
        in_specs=[by_row(width), by_row(width), by_row(width), by_column(width)] + [whole(a) for a in ins[4:]],
        out_specs=[by_row(width), by_row(width), by_column(width), by_column(8), whole(outs[4]), whole(outs[5])],
    )
    early = sum_everywhere(early, dp, seq)

    back_scratch = [
        pltpu.VMEM((width, T), BF16), pltpu.VMEM((T, LANES), BF16), tile_mask,
        pltpu.VMEM((width, T), F32), pltpu.VMEM((width, T), F32),
    ]
    part = struct((shard, width), BF16)
    p_near, p_far, p_forward, dq, dwk, dwv, bv = call(
        functools.partial(back_far_kernel, nq),
        (meta, bounds, bounds_t, x_near, x_far, x_forward, k_far, v_far, qt, d_att, lse, delta, w_key, w_value),
        (
            part, part, part, struct((width, shard), F32), struct((width, width), F32),
            struct((width, width), F32), struct((width, LANES), F32),
        ),
        back_scratch,
        20 * unit,
    )
    p_near = near(p_near + swap(p_forward))
    p_far = far(p_far, back=True)
    granule = 8 * dp * seq
    late_rows = (3 * width + 16 + granule - 1) // granule * granule
    p_partner, input_grad, late = call(
        functools.partial(back_chip_kernel, nq),
        (
            meta, bounds, bounds_t, tokens, x_partner, k_chip, v_chip, qt, d_att, lse, delta,
            w_key, w_value, w_query, dq, dwk, dwv, bv, d_first, small,
        ),
        (part, struct((shard, width), F32), struct((late_rows, width), BF16)),
        back_scratch
        + [
            pltpu.VMEM((width, shard), F32), pltpu.VMEM((width, width), F32), pltpu.VMEM((width, width), F32),
            pltpu.VMEM((width, LANES), F32),
        ],
        30 * unit,
    )
    p_partner = swap(p_partner)
    late = sum_everywhere(late, dp, seq)
    input_grad = input_grad + p_partner.astype(F32) + p_near.astype(F32) + p_far.astype(F32)

    early = early.astype(F32)
    late = late.astype(F32)
    g_w_down = early[:hidden]
    g_w_up = jnp.concatenate([early[at : at + width] for at in range(hidden, 2 * hidden, width)], axis=1)
    g_w_out = early[2 * hidden :]
    biases = late[3 * width :]
    g_b_up = biases[14 : 14 + hidden // width].reshape(hidden)
    return (
        layer, input_grad,
        late[:width], biases[1], late[width : 2 * width], late[2 * width : 3 * width], biases[0],
        g_w_out, biases[8], biases[9], biases[10], g_w_up, g_b_up, g_w_down, biases[11], biases[12], biases[13],
    )


def solution(mesh):
    rows = P(("dp", "seq"), None)
    return jax.shard_map(
        shards,
        mesh=mesh,
        in_specs=(rows, P("dp", None)) + (P(),) * 15 + (rows,),
        out_specs=(rows, rows) + (P(),) * 15,
        check_vma=False,
    )
```

```python
import functools
import math

import jax
import jax.numpy as jnp
from jax import lax
from jax.experimental import pallas as pl
from jax.experimental.pallas import tpu as pltpu
from jax.sharding import PartitionSpec as P

H = 4
HD = 128
EPS = 1e-05
BIG = 1e30
T = 256
LANES = 128
SCALE = 1.0 / math.sqrt(HD)
LOG2E = 1.0 / math.log(2.0)
LN2 = math.log(2.0)
F32 = jnp.float32
BF16 = jnp.bfloat16

NN = (((1,), (0,)), ((), ()))
NT = (((1,), (1,)), ((), ()))
TN = (((0,), (0,)), ((), ()))


def dot(left, right, dims=NN):
    return lax.dot_general(left, right, dims, preferred_element_type=F32)


def head(h):
    return slice(h * HD, (h + 1) * HD)


def query_mask(bcol_ref, start):
    place = start + lax.broadcasted_iota(jnp.int32, (LANES, T), 1)
    inside = jnp.logical_and(place >= bcol_ref[:, 0:1], place < bcol_ref[:, 1:2])
    return jnp.where(inside, 1.0, 0.0).astype(BF16)


def key_mask(brow_ref, start):
    place = start + lax.broadcasted_iota(jnp.int32, (T, LANES), 0)
    inside = jnp.logical_and(place >= brow_ref[0:1, :], place < brow_ref[1:2, :])
    return jnp.where(inside, 0.0, -BIG).astype(BF16)


def tile_range(lo, hi, start, tiles):
    first = jnp.clip((lo - start) // T, 0, tiles)
    last = jnp.clip((hi - start + T - 1) // T, 0, tiles)
    return first, last


class Meta:
    def __init__(self, ref, nq):
        self.ref, self.nq = ref, nq
        self.chip, self.side, self.forward, self.own_tile, self.near_tile = (ref[2 * nq + j] for j in range(5))
        self.partner_tile = nq - self.own_tile
        self.far_tile = nq - self.near_tile
        self.own = self.chip + self.own_tile * T

    def lo(self, i):
        return self.ref[i]

    def hi(self, i):
        return self.ref[self.nq + i]

    @property
    def all_keys(self):
        return self.ref[0], self.ref[2 * self.nq - 1]


LIMIT_SQUARED = 9000.0


def head_pick(width):
    shape = (width, LANES)
    same = lax.broadcasted_iota(jnp.int32, shape, 0) // HD == lax.broadcasted_iota(jnp.int32, shape, 1)
    return jnp.where(same, 1.0, 0.0).astype(BF16)


def keep_norms(norm_ref, rows):
    squares = dot((rows * rows).astype(BF16), head_pick(rows.shape[1]))
    norm_ref[0:1, :] = jnp.maximum(norm_ref[0:1, :], jnp.max(squares, axis=0, keepdims=True))


def attend(meta, segments, qt_ref, k_ref, vt_ref, km_ref, qm_ref, acc_ref, top_ref, total_ref, safe, finish):
    nq = meta.nq

    def query_tile(i, carry):
        q0 = pl.multiple_of(i * T, T)
        qs = pl.ds(q0, T)

        def scores(h, k0):
            ks = pl.ds(k0, 2 * T)
            kx = jnp.concatenate([k_ref[ks, head(h)], km_ref[ks, :]], axis=1)
            qx = jnp.concatenate([qt_ref[head(h), qs], qm_ref[i]], axis=0)
            return dot(kx, qx)

        def weigh(h, k0, p):
            values = jnp.concatenate([vt_ref[head(h), pl.ds(k0, 2 * T)], jnp.ones((16, 2 * T), BF16)], axis=0)
            return dot(values, p)

        def plain(k0):
            ps = [jnp.exp2(scores(h, k0)).astype(BF16) for h in range(H)]
            sums = [weigh(h, k0, ps[h]) for h in range(H)]
            acc_ref[:, qs] += jnp.concatenate([out[0:HD] for out in sums], axis=0)
            for h in range(H):
                total_ref[h : h + 1, qs] += sums[h][HD : HD + 1]

        def guarded(k0):
            for h in range(H):
                s = scores(h, k0)
                old = top_ref[h : h + 1, qs]
                top = jnp.maximum(old, jnp.max(s, axis=0, keepdims=True))
                decay = jnp.exp2(old - top)
                out = weigh(h, k0, jnp.exp2(s - top).astype(BF16))
                acc_ref[head(h), qs] = acc_ref[head(h), qs] * decay + out[0:HD]
                total_ref[h : h + 1, qs] = total_ref[h : h + 1, qs] * decay + out[HD : HD + 1]
                top_ref[h : h + 1, qs] = top

        def walk(body):
            for start, tile, tiles in segments:
                first, last = tile_range(meta.lo(i), meta.hi(i), start, tiles)

                def step(j, inner):
                    body(pl.multiple_of((tile + first + 2 * j) * T, T))
                    return inner

                lax.fori_loop(0, (last - first + 1) // 2, step, 0)

        @pl.when(safe)
        def _():
            walk(plain)

        @pl.when(jnp.logical_not(safe))
        def _():
            walk(guarded)

        finish(q0)
        return carry

    lax.fori_loop(0, nq, query_tile, 0)


def project_keys(meta, brow_ref, start, tile, x_ref, wk_ref, wv_ref, bv_ref, k_ref, v_ref, vt_ref, km_ref, norm_ref):
    lo, hi = meta.all_keys
    first, last = tile_range(lo, hi + T, start, meta.nq)

    def step(t, carry):
        r0 = pl.multiple_of(t * T, T)
        ks = pl.ds(pl.multiple_of((tile + t) * T, T), T)
        x = x_ref[pl.ds(r0, T), :]
        k = dot(x, wk_ref[...])
        v = (dot(x, wv_ref[...]) + bv_ref[...]).astype(BF16)
        k_ref[ks, :] = k.astype(BF16)
        v_ref[ks, :] = v
        vt_ref[:, ks] = v.T
        km_ref[ks, :] = key_mask(brow_ref, start + r0)
        keep_norms(norm_ref, k)
        return carry

    lax.fori_loop(first, last, step, 0)


def blank_tile(tile, k_ref, vt_ref, km_ref):
    ks = slice(tile * T, (tile + 1) * T)
    k_ref[ks, :] = jnp.zeros((T, k_ref.shape[1]), BF16)
    vt_ref[:, ks] = jnp.zeros((vt_ref.shape[0], T), BF16)
    km_ref[ks, :] = jnp.full((T, LANES), -BIG, BF16)


def bounded(query_norms, key_norms):
    return jnp.max(query_norms * key_norms) <= LIMIT_SQUARED


def load(sources, targets, sems):
    copies = [pltpu.make_async_copy(src, dst, sems.at[n]) for n, (src, dst) in enumerate(zip(sources, targets))]
    for copy in copies:
        copy.start()
    return [copy.wait for copy in copies]


def attend_chip_kernel(
    nq,
    meta_ref, brow_ref, bcol_ref, bq_ref, bv_ref, *refs,
):
    sources, refs = refs[:5], refs[5:]
    (qt_ref, k_ref, v_ref, top_ref, total_ref, acc_ref, norm_ref, qm_ref), refs = refs[:8], refs[8:]
    vt_ref, km_ref, kn_ref, x_ref, wq_ref, wk_ref, wv_ref, xp_ref, sems = refs
    waits = load(sources, (x_ref, wq_ref, wk_ref, wv_ref, xp_ref), sems)
    meta = Meta(meta_ref, nq)
    waits[0]()
    waits[1]()
    norm_ref[...] = jnp.zeros_like(norm_ref)
    kn_ref[...] = jnp.zeros_like(kn_ref)

    def make_query(i, carry):
        q0 = pl.multiple_of(i * T, T)
        q = (dot(x_ref[pl.ds(q0, T), :], wq_ref[...]) + bq_ref[...]) * (SCALE * LOG2E)
        qt_ref[:, pl.ds(q0, T)] = q.astype(BF16).T
        qm_ref[i] = query_mask(bcol_ref, meta.own + q0)
        keep_norms(norm_ref, q)
        return carry

    lax.fori_loop(0, nq, make_query, 0)
    waits[2]()
    waits[3]()
    waits[4]()
    for rows, tile in ((x_ref, meta.own_tile), (xp_ref, meta.partner_tile)):
        project_keys(
            meta, brow_ref, meta.chip + tile * T, tile, rows, wk_ref, wv_ref, bv_ref,
            k_ref, v_ref, vt_ref, km_ref, kn_ref,
        )
    blank_tile(2 * nq, k_ref, vt_ref, km_ref)
    acc_ref[...] = jnp.zeros_like(acc_ref)
    total_ref[...] = jnp.zeros_like(total_ref)
    safe = bounded(norm_ref[0:1, :], kn_ref[0:1, :])
    norm_ref[1:2, :] = jnp.full((1, LANES), jnp.where(safe, 1.0, 0.0), F32)
    top_ref[...] = jnp.full(top_ref.shape, jnp.where(safe, 0.0, -BIG), F32)
    attend(
        meta, [(meta.chip, 0, 2 * nq)], qt_ref, k_ref, vt_ref, km_ref, qm_ref, acc_ref, top_ref, total_ref, safe,
        lambda q0: None,
    )


def attend_far(meta, brow_ref, blocks, waits, wk_ref, wv_ref, bv_ref, qt_ref, norm_ref, qm_ref,
               k_ref, v_ref, att_ref, attt_ref, lse_ref, vt_ref, km_ref, kn_ref, top_ref, total_ref):
    nq = meta.nq
    kn_ref[...] = jnp.zeros_like(kn_ref)
    for wait, rows, start, tile in blocks:
        wait()
        project_keys(
            meta, brow_ref, start, tile, rows, wk_ref, wv_ref, bv_ref, k_ref, v_ref, vt_ref, km_ref, kn_ref
        )
    blank_tile(2 * nq, k_ref, vt_ref, km_ref)
    blank_tile(3 * nq + 1, k_ref, vt_ref, km_ref)
    for wait in waits:
        wait()

    def finish(q0):
        qs = pl.ds(q0, T)
        for h in range(H):
            total = total_ref[h : h + 1, qs]
            lse_ref[h : h + 1, qs] = top_ref[h : h + 1, qs] + jnp.log2(total)
            att = attt_ref[head(h), qs] / total
            attt_ref[head(h), qs] = att
            att_ref[qs, head(h)] = att.T.astype(BF16)

    safe = jnp.logical_and(bounded(norm_ref[0:1, :], kn_ref[0:1, :]), jnp.max(norm_ref[1:2, :]) > 0.5)
    attend(
        meta, [(meta.side, 0, 2 * nq), (meta.forward, 2 * nq + 1, nq)], qt_ref, k_ref, vt_ref, km_ref, qm_ref,
        attt_ref, top_ref, total_ref, safe, finish,
    )


def column_sum(rows):
    return jnp.sum(rows, axis=0, keepdims=True)


def mean(rows):
    return jnp.mean(rows, axis=-1, keepdims=True)


def norm(rows):
    centre = rows - mean(rows)
    inverse = lax.rsqrt(mean(centre * centre) + EPS)
    return centre * inverse, inverse


def norm_back(grad, n, inverse):
    return inverse * (grad - mean(grad) - n * mean(grad * n))


def middle(
    nq, x_ref, cot_ref, att_ref, attt_ref, wo_ref, wu_ref, wd_ref, vec_ref, bup_ref,
    layer_ref, dfirst_ref, da_ref, delta_ref, small_ref, gd_ref, gu_ref, go_ref,
):
    width = x_ref.shape[1]
    hidden = wu_ref.shape[1]
    b_out, gain_one, shift_one = vec_ref[0:1, :], vec_ref[1:2, :], vec_ref[2:3, :]
    b_down, gain_two, shift_two = vec_ref[3:4, :], vec_ref[4:5, :], vec_ref[5:6, :]
    for ref in (gd_ref, gu_ref, go_ref, small_ref):
        ref[...] = jnp.zeros_like(ref)

    def row_tile(i, carry):
        rs = pl.ds(pl.multiple_of(i * T, T), T)
        att = att_ref[rs, :]
        first_sum = x_ref[rs, :].astype(F32) + dot(att, wo_ref[...]) + b_out
        n_one, inv_one = norm(first_sum)
        normed = n_one * gain_one + shift_one
        normed_low = normed.astype(BF16)
        pre = dot(normed_low, wu_ref[...]) + bup_ref[...]
        cdf = 0.5 * (1.0 + lax.erf(pre * math.sqrt(0.5)))
        act_low = (pre * cdf).astype(BF16)
        slope = cdf + pre * (jnp.exp(-0.5 * pre * pre) * (1.0 / math.sqrt(2.0 * math.pi)))
        second_sum = normed + dot(act_low, wd_ref[...]) + b_down
        n_two, inv_two = norm(second_sum)
        layer_ref[rs, :] = (n_two * gain_two + shift_two).astype(BF16)
        cot = cot_ref[rs, :].astype(F32)
        d_sum = norm_back(cot * gain_two, n_two, inv_two)
        d_ffn = d_sum.astype(BF16)
        gd_ref[...] += dot(act_low, d_ffn, TN)
        d_pre = (dot(d_ffn, wd_ref[...], NT) * slope).astype(BF16)
        gu_ref[...] += dot(normed_low, d_pre, TN)
        d_normed = d_sum + dot(d_pre, wu_ref[...], NT)
        d_first = norm_back(d_normed * gain_one, n_one, inv_one)
        dfirst_ref[rs, :] = d_first
        d_branch = d_first.astype(BF16)
        go_ref[...] += dot(att, d_branch, TN)
        d_att = dot(wo_ref[...], d_branch, NT).astype(BF16)
        da_ref[:, rs] = d_att
        for h in range(H):
            delta_ref[h : h + 1, rs] = column_sum(d_att[head(h), :].astype(F32) * attt_ref[head(h), rs])
        up = column_sum(d_pre.astype(F32))
        sums = [
            column_sum(d_branch.astype(F32)),
            column_sum(d_normed * n_one),
            column_sum(d_normed),
            column_sum(d_ffn.astype(F32)),
            column_sum(cot * n_two),
            column_sum(cot),
        ]
        for at in range(0, hidden, width):
            sums.append(up[:, at : at + width])
        small_ref[...] += jnp.concatenate(sums, axis=0)
        return carry

    lax.fori_loop(0, nq, row_tile, 0)


def attend_back(
    meta, brow_ref, start, tile, tiles, heads, k_ref, v_ref, qt_ref, da_ref, lse_ref, delta_ref, qm_ref,
    kt_ref, km_ref, dk_ref, dv_ref, dq_ref, done,
):
    nq = meta.nq
    columns = slice(heads[0] * HD, (heads[-1] + 1) * HD)
    first, last = tile_range(*meta.all_keys, start, tiles)

    def key_tile(t, carry):
        ks = pl.ds(pl.multiple_of((tile + t) * T, T), T)
        row = start + t * T
        q_first = sum((meta.hi(i) <= row).astype(jnp.int32) for i in range(nq))
        q_last = sum((meta.lo(i) < row + T).astype(jnp.int32) for i in range(nq))
        km_ref[...] = key_mask(brow_ref, row)
        kt_ref[...] = k_ref[ks, columns].T
        dk_ref[...] = jnp.zeros_like(dk_ref)
        dv_ref[...] = jnp.zeros_like(dv_ref)

        def query_tile(i, inner):
            qs = pl.ds(pl.multiple_of(i * T, T), T)
            ps, ds = [], []
            for h in heads:
                kx = jnp.concatenate([k_ref[ks, head(h)], km_ref[...]], axis=1)
                qx = jnp.concatenate([qt_ref[head(h), qs], qm_ref[i]], axis=0)
                p = jnp.exp2(dot(kx, qx) - lse_ref[h : h + 1, qs])
                ps.append(p.astype(BF16))
                dp = dot(v_ref[ks, head(h)], da_ref[head(h), qs])
                ds.append((p * (dp - delta_ref[h : h + 1, qs])).astype(BF16))
            dv_ref[...] += jnp.concatenate([dot(da_ref[head(h), qs], p, NT) for h, p in zip(heads, ps)], axis=0)
            dk_ref[...] += jnp.concatenate([dot(qt_ref[head(h), qs], d, NT) for h, d in zip(heads, ds)], axis=0)
            dq_ref[:, qs] += jnp.concatenate([dot(kt_ref[head(n), :], d) for n, d in enumerate(ds)], axis=0)
            return inner

        lax.fori_loop(q_first, q_last, query_tile, 0)
        done(t, (dk_ref[...] * LN2).astype(BF16), dv_ref[...].astype(BF16))
        return carry

    lax.fori_loop(first, last, key_tile, 0)


def layer_kernel(
    nq,
    meta_ref, brow_ref, bv_ref, vec_ref, bup_ref, norm_ref, qm_ref, *refs,
):
    sources, refs = refs[:18], refs[18:]
    (layer_ref, ig_ref, pn_ref, pf_ref, pw_ref, pp_ref, grads_ref), refs = refs[:7], refs[7:]
    staged, refs = refs[:18], refs[18:]
    sems, k_ref, v_ref, vt_ref, km_ref, kn_ref, lse_ref, delta_ref, small_ref = refs[:9]
    att_ref, da_ref, gd_ref, gu_ref, go_ref, dq_ref, dwk_ref, dwv_ref, sum_ref = refs[9:18]
    kt_ref, mask_ref, dk_ref, dv_ref = refs[18:]
    waits = load(sources, staged, sems)
    wk_ref, wv_ref, xn_ref, xf_ref, xw_ref, qt_ref, top_ref, total_ref, attt_ref = staged[:9]
    wo_ref, x_ref, wu_ref, wd_ref, cot_ref, kc_ref, vc_ref, xp_ref, wq_ref = staged[9:]
    meta = Meta(meta_ref, nq)
    near_start = meta.side + meta.near_tile * T
    far_start = meta.side + meta.far_tile * T
    waits[0]()
    waits[1]()
    attend_far(
        meta, brow_ref,
        (
            (waits[2], xn_ref, near_start, meta.near_tile),
            (waits[3], xf_ref, far_start, meta.far_tile),
            (waits[4], xw_ref, meta.forward, 2 * nq + 1),
        ),
        waits[5:9],
        wk_ref, wv_ref, bv_ref, qt_ref, norm_ref, qm_ref,
        k_ref, v_ref, att_ref, attt_ref, lse_ref, vt_ref, km_ref, kn_ref, top_ref, total_ref,
    )
    for wait in waits[9:14]:
        wait()
    middle(
        nq, x_ref, cot_ref, att_ref, attt_ref, wo_ref, wu_ref, wd_ref, vec_ref, bup_ref,
        layer_ref, ig_ref, da_ref, delta_ref, small_ref, gd_ref, gu_ref, go_ref,
    )
    hidden, width = wd_ref.shape
    grads_ref[0:hidden, :] = gd_ref[...].astype(BF16)
    for part in range(hidden // width):
        at = hidden + part * width
        grads_ref[at : at + width, :] = gu_ref[:, part * width : (part + 1) * width].astype(BF16)
    grads_ref[2 * hidden : 2 * hidden + width, :] = go_ref[...].astype(BF16)

    for wait in waits[14:]:
        wait()
    for ref in (dq_ref, dwk_ref, dwv_ref, sum_ref, pn_ref, pf_ref, pw_ref, pp_ref):
        ref[...] = jnp.zeros_like(ref)
    for rows, out, start, tile, keys_ref, values_ref in (
        (xn_ref, pn_ref, near_start, meta.near_tile, k_ref, v_ref),
        (xf_ref, pf_ref, far_start, meta.far_tile, k_ref, v_ref),
        (xw_ref, pw_ref, meta.forward, 2 * nq + 1, k_ref, v_ref),
        (xp_ref, pp_ref, meta.chip + meta.partner_tile * T, meta.partner_tile, kc_ref, vc_ref),
        (x_ref, ig_ref, meta.own, meta.own_tile, kc_ref, vc_ref),
    ):

        def done(t, dk, dv, rows=rows, out=out):
            rs = pl.ds(pl.multiple_of(t * T, T), T)
            x = rows[rs, :]
            dwk_ref[...] += dot(dk, x)
            dwv_ref[...] += dot(dv, x)
            sum_ref[:, 0:1] += jnp.sum(dv.astype(F32), axis=1, keepdims=True)
            grad = (dot(wk_ref[...], dk) + dot(wv_ref[...], dv)).T
            if out is ig_ref:
                ig_ref[rs, :] += grad
            else:
                out[rs, :] = grad.astype(BF16)

        attend_back(
            meta, brow_ref, start, tile, nq, range(H), keys_ref, values_ref, qt_ref, da_ref, lse_ref, delta_ref, qm_ref,
            kt_ref, mask_ref, dk_ref, dv_ref, dq_ref, done,
        )
    base = 2 * hidden + width
    grads_ref[base + width : base + 2 * width, :] = dwk_ref[...].T.astype(BF16)
    grads_ref[base + 2 * width : base + 3 * width, :] = dwv_ref[...].T.astype(BF16)
    dwk_ref[...] = jnp.zeros_like(dwk_ref)

    def query_tile(i, carry):
        qs = pl.ds(pl.multiple_of(i * T, T), T)
        dq = (dq_ref[:, qs] * SCALE).astype(BF16)
        dwk_ref[...] += dot(dq, x_ref[qs, :])
        sum_ref[:, 1:2] += jnp.sum(dq.astype(F32), axis=1, keepdims=True)
        ig_ref[qs, :] += dot(wq_ref[...], dq).T
        return carry

    lax.fori_loop(0, nq, query_tile, 0)
    grads_ref[base : base + width, :] = dwk_ref[...].T.astype(BF16)
    end = base + 3 * width
    rows = jnp.concatenate([sum_ref[...].T[0:8, :], small_ref[...]], axis=0)
    grads_ref[end : end + 16, :] = rows.astype(BF16)
    grads_ref[end + 16 :, :] = jnp.zeros((grads_ref.shape[0] - end - 16, width), BF16)


def vmem(count):
    return [pl.BlockSpec(memory_space=pltpu.VMEM)] * count


VMEM_LIMIT = 60 << 20


def call(kernel, inputs, staged, outputs, scratch, flops):
    size = lambda arrays: sum(math.prod(a.shape) * jnp.dtype(a.dtype).itemsize for a in arrays)
    everything = tuple(inputs) + tuple(staged)
    return pl.pallas_call(
        kernel,
        out_shape=outputs,
        in_specs=[pl.BlockSpec(memory_space=pltpu.SMEM)]
        + vmem(len(inputs) - 1)
        + [pl.BlockSpec(memory_space=pltpu.HBM)] * len(staged),
        out_specs=vmem(len(outputs)),
        scratch_shapes=scratch,
        compiler_params=pltpu.CompilerParams(vmem_limit_bytes=VMEM_LIMIT),
        cost_estimate=pl.CostEstimate(
            flops=flops, bytes_accessed=size(everything) + size(outputs), transcendentals=0
        ),
    )(*everything)


def struct(shape, dtype):
    return jax.ShapeDtypeStruct(shape, dtype)


def after(value, other):
    return lax.optimization_barrier((value, other))[0]


class Summing:
    def __init__(self, rows, dp, seq):
        dp_masks = [seq * (1 << j) for j in range(dp.bit_length() - 1)]
        seq_masks = [1 << j for j in range(seq.bit_length() - 1)]
        order = [(seq_masks[0], seq_masks[0])]
        for j in range(len(dp_masks)):
            order.append((dp_masks[j], dp_masks[(j + 1) % len(dp_masks)]))
        order += [(mask, mask) for mask in seq_masks[1:]]
        core = lax.axis_index("seq") % 2
        index = lax.axis_index("dp") * seq + lax.axis_index("seq")
        split = []
        for even, odd in order:
            pairs = [(i, i ^ (even if i % 2 == 0 else odd)) for i in range(dp * seq)]
            split.append((pairs, jnp.where(core == 0, index // even, index // odd) % 2))
        self.todo = [("halve", *step) for step in split[:-1]] + [("whole", *split[-1])]
        self.todo += [("double", *step) for step in split[:-1][::-1]]
        self.rows = rows

    def start(self):
        kind, pairs, bit = self.todo.pop(0)
        send = lambda rows: lax.ppermute(rows, ("dp", "seq"), pairs)
        rows = self.rows
        half = rows.shape[0] // 2
        if kind == "halve":
            self.mine = lax.dynamic_slice_in_dim(rows, bit * half, half, 0)
            self.sent = lax.dynamic_slice_in_dim(rows, (1 - bit) * half, half, 0)
        else:
            self.mine = self.sent = rows
        self.kind, self.bit = kind, bit
        self.got = send(self.sent)

    def finish(self, late=None):
        mine = self.mine if late is None else after(self.mine, late)
        if self.kind == "double":
            half = mine.shape[0]
            whole = jnp.zeros((2 * half, mine.shape[1]), mine.dtype)
            whole = lax.dynamic_update_slice_in_dim(whole, mine, self.bit * half, 0)
            self.rows = lax.dynamic_update_slice_in_dim(whole, self.got, (1 - self.bit) * half, 0)
        else:
            self.rows = mine + self.got

    def run(self, others):
        for number in range(len(self.todo)):
            self.start()
            self.finish(others.get(number))
        return self.rows


GROUPS = 1


def shards(
    tokens, counts, w_query, b_query, w_key, w_value, b_value, w_out, b_out, gain_one, shift_one,
    w_up, b_up, w_down, b_down, gain_two, shift_two, cotangent,
):
    shard, width = tokens.shape
    hidden = w_up.shape[1]
    nq = shard // T
    seq = lax.axis_size("seq")
    dp = lax.axis_size("dp")
    position = lax.axis_index("seq")

    def swap(rows):
        return lax.ppermute(rows, "seq", [(i, i ^ 1) for i in range(seq)])

    def near(rows):
        pairs = [(i, i + 1) for i in range(1, seq - 1, 2)]
        return lax.ppermute(rows, "seq", pairs + [(b, a) for a, b in pairs])

    def far(rows, back=False):
        pairs = [(i, i + 2) for i in range(0, seq - 2, 2)] + [(i, i - 2) for i in range(3, seq, 2)]
        return lax.ppermute(rows, "seq", [(b, a) for a, b in pairs] if back else pairs)

    x_partner = swap(tokens)
    x_near = near(tokens)
    x_far = far(tokens)

    core = position % 2
    side = position + jnp.where(core == 0, -2, 1)
    forward = position + jnp.where(core == 0, 2, -2)
    place = lambda at, inside: jnp.where(inside, at * shard, 1 << 28)
    ends = jnp.cumsum(counts[0])
    starts = ends - counts[0]
    firsts = position * shard + T * jnp.arange(nq, dtype=jnp.int32)
    lasts = firsts + (T - 1)
    lo = jnp.max(jnp.where(starts[None, :] <= firsts[:, None], starts[None, :], 0), axis=1)
    hi = jnp.min(jnp.where(ends[None, :] > lasts[:, None], ends[None, :], seq * shard), axis=1)
    more = jnp.stack([
        (position - core) * shard,
        place(side, jnp.logical_and(side >= 0, side + 1 < seq)),
        place(forward, jnp.logical_and(forward >= 0, forward < seq)),
        core * nq,
        (1 - core) * nq,
    ])
    meta = jnp.concatenate([lo, hi, more]).astype(jnp.int32)
    bounds = jnp.zeros((8, LANES), jnp.int32)
    bounds = bounds.at[0, : starts.shape[0]].set(starts).at[1, : starts.shape[0]].set(ends)
    bounds_t = bounds.T

    row = lambda v: v.reshape(1, -1)
    tile_mask = struct((nq, LANES, T), BF16)
    stats = struct((8, shard), F32)

    def keys_scratch(tiles):
        return [
            pltpu.VMEM((width, tiles * T), BF16), pltpu.VMEM((tiles * T, LANES), BF16), pltpu.VMEM((8, LANES), F32)
        ]

    unit = 2 * shard * width * width
    chip_tiles, far_tiles = 2 * nq + 1, 3 * nq + 2
    keys = lambda tiles: struct((tiles * T, width), BF16)
    block = pltpu.VMEM((shard, width), BF16)
    weight = pltpu.VMEM((width, width), BF16)
    wide = pltpu.VMEM((width, shard), F32)
    square = pltpu.VMEM((width, width), F32)
    stat = pltpu.VMEM((8, shard), F32)
    qt, k_chip, v_chip, top, total, acc, norms, qm = call(
        functools.partial(attend_chip_kernel, nq),
        (meta, bounds, bounds_t, row(b_query), row(b_value)),
        (tokens, w_query, w_key, w_value, x_partner),
        (
            struct((width, shard), BF16), keys(chip_tiles), keys(chip_tiles), stats, stats,
            struct((width, shard), F32), struct((8, LANES), F32), tile_mask,
        ),
        keys_scratch(chip_tiles) + [block, weight, weight, weight, block, pltpu.SemaphoreType.DMA((5,))],
        13 * unit,
    )
    x_forward = swap(after(x_near, norms))

    granule = 8 * dp * seq // 2
    grad_rows = (2 * hidden + 4 * width + 16 + granule - 1) // granule * granule
    vectors = jnp.stack([b_out, gain_one, shift_one, b_down, gain_two, shift_two, b_out, b_out])
    part = struct((shard, width), BF16)
    layer, input_grad, p_near, p_far, p_forward, p_partner, grads = call(
        functools.partial(layer_kernel, nq),
        (meta, bounds, row(b_value), vectors, row(b_up), norms, qm),
        (
            w_key, w_value, x_near, x_far, x_forward, qt, top, total, acc,
            w_out, tokens, w_up, w_down, cotangent, k_chip, v_chip, x_partner, w_query,
        ),
        (
            part, struct((shard, width), F32), part, part, part, part, struct((grad_rows, width), BF16),
        ),
        [
            weight, weight, block, block, block, pltpu.VMEM((width, shard), BF16), stat, stat, wide,
            weight, block, pltpu.VMEM((width, hidden), BF16), pltpu.VMEM((hidden, width), BF16), block,
            pltpu.VMEM((chip_tiles * T, width), BF16), pltpu.VMEM((chip_tiles * T, width), BF16), block, weight,
            pltpu.SemaphoreType.DMA((18,)),
            pltpu.VMEM((far_tiles * T, width), BF16), pltpu.VMEM((far_tiles * T, width), BF16),
        ]
        + keys_scratch(far_tiles)
        + [stat, stat, pltpu.VMEM((8, width), F32)]
        + [block, pltpu.VMEM((width, shard), BF16)]
        + [pltpu.VMEM((hidden, width), F32), pltpu.VMEM((width, hidden), F32), square]
        + [wide, square, square, pltpu.VMEM((width, LANES), F32)]
        + [
            pltpu.VMEM((width, T), BF16), pltpu.VMEM((T, LANES), BF16),
            pltpu.VMEM((width, T), F32), pltpu.VMEM((width, T), F32),
        ],
        60 * unit,
    )
    p_far = far(p_far, back=True)
    p_sum = p_near + swap(p_forward)
    p_near = near(p_sum)
    p_partner = swap(p_partner)
    summing = Summing(after(grads, p_sum), dp, seq)
    grads = summing.run({2: p_near, 3: p_far, 4: p_partner}).astype(F32)
    input_grad = input_grad + p_partner.astype(F32) + p_near.astype(F32) + p_far.astype(F32)
    early, late = grads[: 2 * hidden + width], grads[2 * hidden + width :]

    g_w_down = early[:hidden]
    g_w_up = jnp.concatenate([early[at : at + width] for at in range(hidden, 2 * hidden, width)], axis=1)
    g_w_out = early[2 * hidden :]
    biases = late[3 * width :]
    g_b_up = biases[14 : 14 + hidden // width].reshape(hidden)
    return (
        layer, input_grad,
        late[:width], biases[1], late[width : 2 * width], late[2 * width : 3 * width], biases[0],
        g_w_out, biases[8], biases[9], biases[10], g_w_up, g_b_up, g_w_down, biases[11], biases[12], biases[13],
    )


def solution(mesh):
    rows = P(("dp", "seq"), None)
    return jax.shard_map(
        shards,
        mesh=mesh,
        in_specs=(rows, P("dp", None)) + (P(),) * 15 + (rows,),
        out_specs=(rows, rows) + (P(),) * 15,
        check_vma=False,
    )
```

```python
import functools
import math

import jax
import jax.numpy as jnp
from jax import lax
from jax.experimental import pallas as pl
from jax.experimental.pallas import tpu as pltpu
from jax.sharding import PartitionSpec as P

H = 4
HD = 128
EPS = 1e-05
BIG = 1e30
T = 256
LANES = 128
SCALE = 1.0 / math.sqrt(HD)
LOG2E = 1.0 / math.log(2.0)
LN2 = math.log(2.0)
F32 = jnp.float32
BF16 = jnp.bfloat16

NN = (((1,), (0,)), ((), ()))
NT = (((1,), (1,)), ((), ()))
TN = (((0,), (0,)), ((), ()))


def dot(left, right, dims=NN):
    return lax.dot_general(left, right, dims, preferred_element_type=F32)


def head(h):
    return slice(h * HD, (h + 1) * HD)


def query_mask(bcol_ref, start):
    place = start + lax.broadcasted_iota(jnp.int32, (LANES, T), 1)
    inside = jnp.logical_and(place >= bcol_ref[:, 0:1], place < bcol_ref[:, 1:2])
    return jnp.where(inside, 1.0, 0.0).astype(BF16)


def key_mask(brow_ref, start):
    place = start + lax.broadcasted_iota(jnp.int32, (T, LANES), 0)
    inside = jnp.logical_and(place >= brow_ref[0:1, :], place < brow_ref[1:2, :])
    return jnp.where(inside, 0.0, -BIG).astype(BF16)


def tile_range(lo, hi, start, tiles):
    first = jnp.clip((lo - start) // T, 0, tiles)
    last = jnp.clip((hi - start + T - 1) // T, 0, tiles)
    return first, last


class Meta:
    def __init__(self, ref, nq):
        self.ref, self.nq = ref, nq
        self.chip, self.side, self.forward, self.own_tile, self.near_tile = (ref[2 * nq + j] for j in range(5))
        self.partner_tile = nq - self.own_tile
        self.far_tile = nq - self.near_tile
        self.own = self.chip + self.own_tile * T

    def lo(self, i):
        return self.ref[i]

    def hi(self, i):
        return self.ref[self.nq + i]

    @property
    def all_keys(self):
        return self.ref[0], self.ref[2 * self.nq - 1]


LIMIT_SQUARED = 9000.0


def head_pick(width):
    shape = (width, LANES)
    same = lax.broadcasted_iota(jnp.int32, shape, 0) // HD == lax.broadcasted_iota(jnp.int32, shape, 1)
    return jnp.where(same, 1.0, 0.0).astype(BF16)


def keep_norms(norm_ref, rows):
    squares = dot((rows * rows).astype(BF16), head_pick(rows.shape[1]))
    norm_ref[0:1, :] = jnp.maximum(norm_ref[0:1, :], jnp.max(squares, axis=0, keepdims=True))


def attend(meta, segments, qt_ref, k_ref, vt_ref, km_ref, qm_ref, acc_ref, top_ref, total_ref, safe, finish):
    nq = meta.nq

    def query_tile(i, carry):
        q0 = pl.multiple_of(i * T, T)
        qs = pl.ds(q0, T)

        def scores(h, k0):
            ks = pl.ds(k0, 2 * T)
            kx = jnp.concatenate([k_ref[ks, head(h)], km_ref[ks, :]], axis=1)
            qx = jnp.concatenate([qt_ref[head(h), qs], qm_ref[i]], axis=0)
            return dot(kx, qx)

        def weigh(h, k0, p):
            values = jnp.concatenate([vt_ref[head(h), pl.ds(k0, 2 * T)], jnp.ones((16, 2 * T), BF16)], axis=0)
            return dot(values, p)

        def plain(k0):
            ps = [jnp.exp2(scores(h, k0)).astype(BF16) for h in range(H)]
            sums = [weigh(h, k0, ps[h]) for h in range(H)]
            acc_ref[:, qs] += jnp.concatenate([out[0:HD] for out in sums], axis=0)
            for h in range(H):
                total_ref[h : h + 1, qs] += sums[h][HD : HD + 1]

        def guarded(k0):
            for h in range(H):
                s = scores(h, k0)
                old = top_ref[h : h + 1, qs]
                top = jnp.maximum(old, jnp.max(s, axis=0, keepdims=True))
                decay = jnp.exp2(old - top)
                out = weigh(h, k0, jnp.exp2(s - top).astype(BF16))
                acc_ref[head(h), qs] = acc_ref[head(h), qs] * decay + out[0:HD]
                total_ref[h : h + 1, qs] = total_ref[h : h + 1, qs] * decay + out[HD : HD + 1]
                top_ref[h : h + 1, qs] = top

        def walk(body):
            for start, tile, tiles in segments:
                first, last = tile_range(meta.lo(i), meta.hi(i), start, tiles)

                def step(j, inner):
                    body(pl.multiple_of((tile + first + 2 * j) * T, T))
                    return inner

                lax.fori_loop(0, (last - first + 1) // 2, step, 0)

        @pl.when(safe)
        def _():
            walk(plain)

        @pl.when(jnp.logical_not(safe))
        def _():
            walk(guarded)

        finish(q0)
        return carry

    lax.fori_loop(0, nq, query_tile, 0)


def project_keys(meta, brow_ref, start, tile, x_ref, wk_ref, wv_ref, bv_ref, k_ref, v_ref, vt_ref, km_ref, norm_ref):
    lo, hi = meta.all_keys
    first, last = tile_range(lo, hi + T, start, meta.nq)

    def step(t, carry):
        r0 = pl.multiple_of(t * T, T)
        ks = pl.ds(pl.multiple_of((tile + t) * T, T), T)
        x = x_ref[pl.ds(r0, T), :]
        k = dot(x, wk_ref[...])
        v = (dot(x, wv_ref[...]) + bv_ref[...]).astype(BF16)
        k_ref[ks, :] = k.astype(BF16)
        v_ref[ks, :] = v
        vt_ref[:, ks] = v.T
        km_ref[ks, :] = key_mask(brow_ref, start + r0)
        keep_norms(norm_ref, k)
        return carry

    lax.fori_loop(first, last, step, 0)


def blank_tile(tile, k_ref, vt_ref, km_ref):
    ks = slice(tile * T, (tile + 1) * T)
    k_ref[ks, :] = jnp.zeros((T, k_ref.shape[1]), BF16)
    vt_ref[:, ks] = jnp.zeros((vt_ref.shape[0], T), BF16)
    km_ref[ks, :] = jnp.full((T, LANES), -BIG, BF16)


def bounded(query_norms, key_norms):
    return jnp.max(query_norms * key_norms) <= LIMIT_SQUARED


def load(sources, targets, sems):
    copies = [pltpu.make_async_copy(src, dst, sems.at[n]) for n, (src, dst) in enumerate(zip(sources, targets))]
    for copy in copies:
        copy.start()
    return [copy.wait for copy in copies]


def attend_chip_kernel(
    nq,
    meta_ref, brow_ref, bcol_ref, bq_ref, bv_ref, *refs,
):
    sources, refs = refs[:5], refs[5:]
    (q_ref, qt_ref, k_ref, v_ref, top_ref, total_ref, acc_ref, norm_ref, qm_ref), refs = refs[:9], refs[9:]
    vt_ref, km_ref, kn_ref, x_ref, wq_ref, wk_ref, wv_ref, xp_ref, sems = refs
    waits = load(sources, (x_ref, wq_ref, wk_ref, wv_ref, xp_ref), sems)
    meta = Meta(meta_ref, nq)
    waits[0]()
    waits[1]()
    norm_ref[...] = jnp.zeros_like(norm_ref)
    kn_ref[...] = jnp.zeros_like(kn_ref)

    def make_query(i, carry):
        q0 = pl.multiple_of(i * T, T)
        q = (dot(x_ref[pl.ds(q0, T), :], wq_ref[...]) + bq_ref[...]) * (SCALE * LOG2E)
        low = q.astype(BF16)
        q_ref[pl.ds(q0, T), :] = low
        qt_ref[:, pl.ds(q0, T)] = low.T
        qm_ref[i] = query_mask(bcol_ref, meta.own + q0)
        keep_norms(norm_ref, q)
        return carry

    lax.fori_loop(0, nq, make_query, 0)
    waits[2]()
    waits[3]()
    waits[4]()
    for rows, tile in ((x_ref, meta.own_tile), (xp_ref, meta.partner_tile)):
        project_keys(
            meta, brow_ref, meta.chip + tile * T, tile, rows, wk_ref, wv_ref, bv_ref,
            k_ref, v_ref, vt_ref, km_ref, kn_ref,
        )
    blank_tile(2 * nq, k_ref, vt_ref, km_ref)
    acc_ref[...] = jnp.zeros_like(acc_ref)
    total_ref[...] = jnp.zeros_like(total_ref)
    safe = bounded(norm_ref[0:1, :], kn_ref[0:1, :])
    norm_ref[1:2, :] = jnp.full((1, LANES), jnp.where(safe, 1.0, 0.0), F32)
    top_ref[...] = jnp.full(top_ref.shape, jnp.where(safe, 0.0, -BIG), F32)
    attend(
        meta, [(meta.chip, 0, 2 * nq)], qt_ref, k_ref, vt_ref, km_ref, qm_ref, acc_ref, top_ref, total_ref, safe,
        lambda q0: None,
    )


def attend_far(meta, brow_ref, blocks, waits, wk_ref, wv_ref, bv_ref, qt_ref, norm_ref, qm_ref,
               k_ref, v_ref, att_ref, attt_ref, lse_ref, vt_ref, km_ref, kn_ref, top_ref, total_ref):
    nq = meta.nq
    kn_ref[...] = jnp.zeros_like(kn_ref)
    for wait, rows, start, tile in blocks:
        wait()
        project_keys(
            meta, brow_ref, start, tile, rows, wk_ref, wv_ref, bv_ref, k_ref, v_ref, vt_ref, km_ref, kn_ref
        )
    blank_tile(2 * nq, k_ref, vt_ref, km_ref)
    blank_tile(3 * nq + 1, k_ref, vt_ref, km_ref)
    for wait in waits:
        wait()

    def finish(q0):
        qs = pl.ds(q0, T)
        for h in range(H):
            total = total_ref[h : h + 1, qs]
            lse_ref[h : h + 1, qs] = top_ref[h : h + 1, qs] + jnp.log2(total)
            att = attt_ref[head(h), qs] / total
            attt_ref[head(h), qs] = att
            att_ref[qs, head(h)] = att.T.astype(BF16)

    safe = jnp.logical_and(bounded(norm_ref[0:1, :], kn_ref[0:1, :]), jnp.max(norm_ref[1:2, :]) > 0.5)
    attend(
        meta, [(meta.side, 0, 2 * nq), (meta.forward, 2 * nq + 1, nq)], qt_ref, k_ref, vt_ref, km_ref, qm_ref,
        attt_ref, top_ref, total_ref, safe, finish,
    )


def column_sum(rows):
    return jnp.sum(rows, axis=0, keepdims=True)


def mean(rows):
    return jnp.mean(rows, axis=-1, keepdims=True)


def norm(rows):
    centre = rows - mean(rows)
    inverse = lax.rsqrt(mean(centre * centre) + EPS)
    return centre * inverse, inverse


def norm_back(grad, n, inverse):
    return inverse * (grad - mean(grad) - n * mean(grad * n))


def middle(
    nq, x_ref, cot_ref, att_ref, attt_ref, wo_ref, wu_ref, wd_ref, vec_ref, bup_ref,
    dfirst_ref, da_ref, dat_ref, delta_ref, small_ref, gd_ref, gu_ref, go_ref,
):
    width = x_ref.shape[1]
    hidden = wu_ref.shape[1]
    b_out, gain_one, shift_one = vec_ref[0:1, :], vec_ref[1:2, :], vec_ref[2:3, :]
    b_down, gain_two, shift_two = vec_ref[3:4, :], vec_ref[4:5, :], vec_ref[5:6, :]
    for ref in (gd_ref, gu_ref, go_ref, small_ref):
        ref[...] = jnp.zeros_like(ref)
    rows_of = lambda tiles: jnp.concatenate(tiles, axis=0)

    def row_tiles(i, carry):
        both = [pl.ds(pl.multiple_of((2 * i + n) * T, T), T) for n in range(2)]
        att = [att_ref[rs, :] for rs in both]
        branch = [dot(a, wo_ref[...]) for a in att]
        one = [norm(x_ref[rs, :].astype(F32) + b + b_out) for rs, b in zip(both, branch)]
        normed = [n * gain_one + shift_one for n, _ in one]
        normed_low = [n.astype(BF16) for n in normed]
        pre, act_low, slope = [], [], []
        for n in range(2):
            pre.append(dot(normed_low[n], wu_ref[...]) + bup_ref[...])
        for n in range(2):
            cdf = 0.5 * (1.0 + lax.erf(pre[n] * math.sqrt(0.5)))
            act_low.append((pre[n] * cdf).astype(BF16))
            slope.append(cdf + pre[n] * (jnp.exp(-0.5 * pre[n] * pre[n]) * (1.0 / math.sqrt(2.0 * math.pi))))
        down = [dot(act, wd_ref[...]) for act in act_low]
        two = [norm(n + d + b_down) for n, d in zip(normed, down)]
        cot = [cot_ref[rs, :].astype(F32) for rs in both]
        for rs, (n, _) in zip(both, two):
            cot_ref[rs, :] = (n * gain_two + shift_two).astype(BF16)
        d_sum = [norm_back(c * gain_two, n, inverse) for c, (n, inverse) in zip(cot, two)]
        d_ffn = [d.astype(BF16) for d in d_sum]
        d_act = [dot(d, wd_ref[...], NT) for d in d_ffn]
        gd_ref[...] += dot(rows_of(act_low), rows_of(d_ffn), TN)
        d_pre = [(d * s).astype(BF16) for d, s in zip(d_act, slope)]
        d_normed = [a + dot(d, wu_ref[...], NT) for a, d in zip(d_sum, d_pre)]
        gu_ref[...] += dot(rows_of(normed_low), rows_of(d_pre), TN)
        d_first = [norm_back(d * gain_one, n, inverse) for d, (n, inverse) in zip(d_normed, one)]
        d_branch = [d.astype(BF16) for d in d_first]
        d_att = [dot(d, wo_ref[...], NT).astype(BF16) for d in d_branch]
        go_ref[...] += dot(rows_of(att), rows_of(d_branch), TN)
        for rs, d, a in zip(both, d_first, d_att):
            dfirst_ref[rs, :] = d
            da_ref[rs, :] = a
            turned = a.T
            dat_ref[:, rs] = turned
            for h in range(H):
                delta_ref[h : h + 1, rs] = column_sum(turned[head(h), :].astype(F32) * attt_ref[head(h), rs])
        pair_sum = lambda rows: column_sum(rows[0].astype(F32) + rows[1].astype(F32))
        up = pair_sum(d_pre)
        sums = [
            pair_sum(d_branch),
            pair_sum([d * n for d, (n, _) in zip(d_normed, one)]),
            pair_sum(d_normed),
            pair_sum(d_ffn),
            pair_sum([c * n for c, (n, _) in zip(cot, two)]),
            pair_sum(cot),
        ]
        for at in range(0, hidden, width):
            sums.append(up[:, at : at + width])
        small_ref[...] += jnp.concatenate(sums, axis=0)
        return carry

    lax.fori_loop(0, nq // 2, row_tiles, 0)


def attend_back(
    meta, brow_ref, start, tile, k_ref, v_ref, q_ref, qt_ref, da_ref, dat_ref, lse_ref, delta_ref, qm_ref,
    kt_ref, km_ref, dk_ref, dv_ref, dq_ref,
):
    nq = meta.nq
    first, last = tile_range(*meta.all_keys, start, nq)

    def rows_at(t):
        return pl.ds(pl.multiple_of((tile + t) * T, T), T)

    def blank(t, carry):
        for ref in (k_ref, v_ref):
            ref[rows_at(t), :] = jnp.zeros((T, ref.shape[1]), BF16)
        return carry

    def key_tile(t, carry):
        ks = rows_at(t)
        row = start + t * T
        q_first = sum((meta.hi(i) <= row).astype(jnp.int32) for i in range(nq))
        q_last = sum((meta.lo(i) < row + T).astype(jnp.int32) for i in range(nq))
        km_ref[...] = key_mask(brow_ref, row)
        kt_ref[...] = k_ref[ks, :].T
        dk_ref[...] = jnp.zeros_like(dk_ref)
        dv_ref[...] = jnp.zeros_like(dv_ref)

        def query_tile(i, inner):
            qs = pl.ds(pl.multiple_of(i * T, T), T)
            ps, ds, sums = [], [], []

            def products(h):
                sums.append((dot(ps[h], da_ref[qs, head(h)]), dot(ds[h], q_ref[qs, head(h)]), dot(kt_ref[head(h), :], ds[h])))

            for h in range(H):
                kx = jnp.concatenate([k_ref[ks, head(h)], km_ref[...]], axis=1)
                qx = jnp.concatenate([qt_ref[head(h), qs], qm_ref[i]], axis=0)
                p = jnp.exp2(dot(kx, qx) - lse_ref[h : h + 1, qs])
                ps.append(p.astype(BF16))
                dp = dot(v_ref[ks, head(h)], dat_ref[head(h), qs])
                ds.append((p * (dp - delta_ref[h : h + 1, qs])).astype(BF16))
                if h >= 2:
                    products(h - 2)
            products(H - 2)
            products(H - 1)
            dv_ref[...] += jnp.concatenate([out[0] for out in sums], axis=1)
            dk_ref[...] += jnp.concatenate([out[1] for out in sums], axis=1)
            dq_ref[:, qs] += jnp.concatenate([out[2] for out in sums], axis=0)
            return inner

        lax.fori_loop(q_first, q_last, query_tile, 0)
        k_ref[ks, :] = (dk_ref[...] * LN2).astype(BF16)
        v_ref[ks, :] = dv_ref[...].astype(BF16)
        return carry

    lax.fori_loop(0, first, blank, 0)
    lax.fori_loop(first, last, key_tile, 0)
    lax.fori_loop(last, nq, blank, 0)


def layer_kernel(
    nq,
    meta_ref, brow_ref, bv_ref, vec_ref, bup_ref, norm_ref, qm_ref, *refs,
):
    loads = 19
    sources, refs = refs[:loads], refs[loads:]
    layer_out, ig_out, pn_out, pf_out, pw_out, pp_out, keep_out, send_out = refs[:8]
    refs = refs[8:]
    staged, refs = refs[:loads], refs[loads:]
    sems, out_sems, grads_ref, ig_ref, k_ref, v_ref, vt_ref, km_ref, kn_ref, lse_ref, delta_ref, small_ref = refs[:12]
    att_ref, da_ref, dat_ref, gd_ref, gu_ref, go_ref, sum_ref = refs[12:19]
    kt_ref, mask_ref, dk_ref, dv_ref = refs[19:]
    waits = load(sources, staged, sems)
    wk_ref, wv_ref, xn_ref, xf_ref, xw_ref, qt_ref, top_ref, total_ref, attt_ref = staged[:9]
    wo_ref, x_ref, wu_ref, wd_ref, cot_ref, q_ref, kc_ref, vc_ref, xp_ref, wq_ref = staged[9:]
    stores = []

    def store(source, target):
        copy = pltpu.make_async_copy(source, target, out_sems.at[len(stores)])
        copy.start()
        stores.append(copy)

    meta = Meta(meta_ref, nq)
    near_start = meta.side + meta.near_tile * T
    far_start = meta.side + meta.far_tile * T
    waits[0]()
    waits[1]()
    attend_far(
        meta, brow_ref,
        (
            (waits[2], xn_ref, near_start, meta.near_tile),
            (waits[3], xf_ref, far_start, meta.far_tile),
            (waits[4], xw_ref, meta.forward, 2 * nq + 1),
        ),
        waits[5:9],
        wk_ref, wv_ref, bv_ref, qt_ref, norm_ref, qm_ref,
        k_ref, v_ref, att_ref, attt_ref, lse_ref, vt_ref, km_ref, kn_ref, top_ref, total_ref,
    )
    for wait in waits[9:14]:
        wait()
    middle(
        nq, x_ref, cot_ref, att_ref, attt_ref, wo_ref, wu_ref, wd_ref, vec_ref, bup_ref,
        ig_ref, da_ref, dat_ref, delta_ref, small_ref, gd_ref, gu_ref, go_ref,
    )
    store(cot_ref, layer_out)
    hidden, width = wd_ref.shape
    shard = x_ref.shape[0]
    grads_ref[0:hidden, :] = gd_ref[...].astype(BF16)
    for part in range(hidden // width):
        at = hidden + part * width
        grads_ref[at : at + width, :] = gu_ref[:, part * width : (part + 1) * width].astype(BF16)
    base = 2 * hidden + width
    grads_ref[base - width : base, :] = go_ref[...].astype(BF16)
    half = grads_ref.shape[0] // 2
    assert half <= base
    first_core = meta.own_tile == 0

    def store_half(source, stays):
        copies = [pltpu.make_async_copy(source, target, out_sems.at[len(stores)]) for target in (keep_out, send_out)]
        pl.when(stays)(copies[0].start)
        pl.when(jnp.logical_not(stays))(copies[1].start)
        stores.append(copies[0])

    store_half(grads_ref.at[0:half, :], first_core)

    for wait in waits[14:]:
        wait()
    xt_ref = vt_ref.at[:, 0:shard]
    dq_ref = attt_ref
    dwk_ref = gd_ref.at[0:width, :]
    dwv_ref = gd_ref.at[width : 2 * width, :]
    wkv_ref = wd_ref
    wkv_ref[0:width, :] = wk_ref[...].T
    wkv_ref[width : 2 * width, :] = wv_ref[...].T
    wo_ref[...] = wq_ref[...].T
    for ref in (dq_ref, dwk_ref, dwv_ref, sum_ref):
        ref[...] = jnp.zeros_like(ref)
    for rows, out, start, tile, keys_ref, values_ref in (
        (xn_ref, pn_out, near_start, meta.near_tile, k_ref, v_ref),
        (xf_ref, pf_out, far_start, meta.far_tile, k_ref, v_ref),
        (xw_ref, pw_out, meta.forward, 2 * nq + 1, k_ref, v_ref),
        (xp_ref, pp_out, meta.chip + meta.partner_tile * T, meta.partner_tile, kc_ref, vc_ref),
        (x_ref, None, meta.own, meta.own_tile, kc_ref, vc_ref),
    ):
        first, last = tile_range(*meta.all_keys, start, nq)

        def work(rows=rows, out=out, start=start, tile=tile, keys_ref=keys_ref, values_ref=values_ref):
            attend_back(
                meta, brow_ref, start, tile, keys_ref, values_ref, q_ref, qt_ref, da_ref, dat_ref,
                lse_ref, delta_ref, qm_ref, kt_ref, mask_ref, dk_ref, dv_ref, dq_ref,
            )
            block = pl.ds(pl.multiple_of(tile * T, T), shard)
            xt_ref[...] = rows[...].T
            dwk_ref[...] += dot(xt_ref[...], keys_ref[block, :])
            dwv_ref[...] += dot(xt_ref[...], values_ref[block, :])
            sum_ref[0:1, :] += column_sum(values_ref[block, :].astype(F32))

            def input_tile(t, carry):
                rs = pl.ds(pl.multiple_of(2 * t * T, 2 * T), 2 * T)
                ks = pl.ds(pl.multiple_of((tile + 2 * t) * T, T), 2 * T)
                grad = dot(jnp.concatenate([keys_ref[ks, :], values_ref[ks, :]], axis=1), wkv_ref[...])
                if out is None:
                    ig_ref[rs, :] += grad
                else:
                    rows[rs, :] = grad.astype(BF16)
                return carry

            lax.fori_loop(0, nq // 2, input_tile, 0)

        if out is None:
            work()
        else:
            pl.when(first < last)(work)

            @pl.when(first >= last)
            def _(rows=rows):
                rows[...] = jnp.zeros_like(rows)

            store(rows, out)

    dwk_low = dwk_ref[...].astype(BF16)
    dwv_low = dwv_ref[...].astype(BF16)

    def query_tile(i, carry):
        qs = pl.ds(pl.multiple_of(i * T, T), T)
        dq = (dq_ref[:, qs] * SCALE).astype(BF16).T
        q_ref[qs, :] = dq
        sum_ref[1:2, :] += column_sum(dq.astype(F32))
        ig_ref[qs, :] += dot(dq, wo_ref[...])
        return carry

    lax.fori_loop(0, nq, query_tile, 0)
    store(ig_ref, ig_out)
    grads_ref[base : base + width, :] = dot(xt_ref[...], q_ref[...]).astype(BF16)
    grads_ref[base + width : base + 2 * width, :] = dwk_low
    grads_ref[base + 2 * width : base + 3 * width, :] = dwv_low
    end = base + 3 * width
    rows = jnp.concatenate([sum_ref[...], small_ref[...]], axis=0)
    grads_ref[end : end + 16, :] = rows.astype(BF16)
    grads_ref[end + 16 :, :] = jnp.zeros((grads_ref.shape[0] - end - 16, width), BF16)
    store_half(grads_ref.at[half:, :], jnp.logical_not(first_core))
    for copy in stores:
        copy.wait()


def vmem(count):
    return [pl.BlockSpec(memory_space=pltpu.VMEM)] * count


VMEM_LIMIT = 60 << 20


def call(kernel, inputs, staged, outputs, scratch, flops, out_space=pltpu.VMEM, limit=VMEM_LIMIT):
    size = lambda arrays: sum(math.prod(a.shape) * jnp.dtype(a.dtype).itemsize for a in arrays)
    everything = tuple(inputs) + tuple(staged)
    return pl.pallas_call(
        kernel,
        out_shape=outputs,
        in_specs=[pl.BlockSpec(memory_space=pltpu.SMEM)]
        + vmem(len(inputs) - 1)
        + [pl.BlockSpec(memory_space=pltpu.HBM)] * len(staged),
        out_specs=[pl.BlockSpec(memory_space=out_space)] * len(outputs),
        scratch_shapes=scratch,
        compiler_params=pltpu.CompilerParams(vmem_limit_bytes=limit),
        cost_estimate=pl.CostEstimate(
            flops=flops, bytes_accessed=size(everything) + size(outputs), transcendentals=0
        ),
    )(*everything)


def struct(shape, dtype):
    return jax.ShapeDtypeStruct(shape, dtype)


def after(value, other):
    return lax.optimization_barrier((value, other))[0]


class Summing:
    def __init__(self, dp, seq):
        dp_masks = [seq * (1 << j) for j in range(dp.bit_length() - 1)]
        seq_masks = [1 << j for j in range(seq.bit_length() - 1)]
        self.order = [(dp_masks[j], dp_masks[(j + 1) % len(dp_masks)]) for j in range(len(dp_masks))]
        self.dp_steps = len(self.order)
        self.order += [(mask, mask) for mask in seq_masks[1:]]
        self.devices = dp * seq
        core = lax.axis_index("seq") % 2
        index = lax.axis_index("dp") * seq + lax.axis_index("seq")
        self.bits = [jnp.where(core == 0, index // even, index // odd) % 2 for even, odd in self.order]

    def exchange(self, rows, even=1, odd=1):
        pairs = [(i, i ^ (even if i % 2 == 0 else odd)) for i in range(self.devices)]
        return lax.ppermute(rows, ("dp", "seq"), pairs)

    def halve(self, rows, waits):
        for number, (even, odd) in enumerate(self.order[:-1]):
            half = rows.shape[0] // 2
            bit = self.bits[number]
            mine = lax.dynamic_slice_in_dim(rows, bit * half, half, 0)
            got = self.exchange(lax.dynamic_slice_in_dim(rows, (1 - bit) * half, half, 0), even, odd)
            rows = (after(mine, waits[number]) if number in waits else mine) + got
        return rows + self.exchange(rows, *self.order[-1])

    def double(self, rows, numbers, waits):
        for number in numbers:
            got = self.exchange(rows, *self.order[number])
            half = rows.shape[0]
            if number in waits:
                rows = after(rows, waits[number])
            whole = jnp.zeros((2 * half, rows.shape[1]), rows.dtype)
            whole = lax.dynamic_update_slice_in_dim(whole, rows, self.bits[number] * half, 0)
            rows = lax.dynamic_update_slice_in_dim(whole, got, (1 - self.bits[number]) * half, 0)
        return rows


def widen_kernel(core_ref, mine_ref, other_ref, *refs):
    outs, refs = refs[:7], refs[7:]
    wide, sems = refs[:7], refs[7]
    half, width = mine_ref.shape
    hidden = wide[0].shape[0]
    spans = [(0, hidden, 0, 0)]
    spans += [(hidden + at, width, 1, at) for at in range(0, hidden, width)]
    spans += [(2 * hidden + n * width, width, 2 + n, 0) for n in range(4)]
    spans += [(2 * hidden + 4 * width, 16, 6, 0)]
    copies = [pltpu.make_async_copy(src, dst, sems.at[n]) for n, (src, dst) in enumerate(zip(wide, outs))]

    def write(low_ref, high_ref):
        for start, rows, number, column in spans:
            for source, base in ((low_ref, 0), (high_ref, half)):
                first, last = max(start, base), min(start + rows, base + half)
                if first < last:
                    wide[number][first - start : last - start, column : column + width] = source[
                        first - base : last - base, :
                    ].astype(F32)
            if column + width == wide[number].shape[1]:
                copies[number].start()

    @pl.when(core_ref[0] == 0)
    def _():
        write(mine_ref, other_ref)

    @pl.when(core_ref[0] != 0)
    def _():
        write(other_ref, mine_ref)

    for copy in copies:
        copy.wait()


def shards(
    tokens, counts, w_query, b_query, w_key, w_value, b_value, w_out, b_out, gain_one, shift_one,
    w_up, b_up, w_down, b_down, gain_two, shift_two, cotangent,
):
    shard, width = tokens.shape
    hidden = w_up.shape[1]
    nq = shard // T
    seq = lax.axis_size("seq")
    dp = lax.axis_size("dp")
    position = lax.axis_index("seq")

    def swap(rows):
        return lax.ppermute(rows, "seq", [(i, i ^ 1) for i in range(seq)])

    def near(rows):
        pairs = [(i, i + 1) for i in range(1, seq - 1, 2)]
        return lax.ppermute(rows, "seq", pairs + [(b, a) for a, b in pairs])

    def far(rows, back=False):
        pairs = [(i, i + 2) for i in range(0, seq - 2, 2)] + [(i, i - 2) for i in range(3, seq, 2)]
        return lax.ppermute(rows, "seq", [(b, a) for a, b in pairs] if back else pairs)

    x_partner = swap(tokens)
    x_near = near(tokens)
    x_far = far(tokens)

    core = position % 2
    side = position + jnp.where(core == 0, -2, 1)
    forward = position + jnp.where(core == 0, 2, -2)
    place = lambda at, inside: jnp.where(inside, at * shard, 1 << 28)
    ends = jnp.cumsum(counts[0])
    starts = ends - counts[0]
    firsts = position * shard + T * jnp.arange(nq, dtype=jnp.int32)
    lasts = firsts + (T - 1)
    lo = jnp.max(jnp.where(starts[None, :] <= firsts[:, None], starts[None, :], 0), axis=1)
    hi = jnp.min(jnp.where(ends[None, :] > lasts[:, None], ends[None, :], seq * shard), axis=1)
    more = jnp.stack([
        (position - core) * shard,
        place(side, jnp.logical_and(side >= 0, side + 1 < seq)),
        place(forward, jnp.logical_and(forward >= 0, forward < seq)),
        core * nq,
        (1 - core) * nq,
    ])
    meta = jnp.concatenate([lo, hi, more]).astype(jnp.int32)
    bounds = jnp.zeros((8, LANES), jnp.int32)
    bounds = bounds.at[0, : starts.shape[0]].set(starts).at[1, : starts.shape[0]].set(ends)
    bounds_t = bounds.T

    row = lambda v: v.reshape(1, -1)
    tile_mask = struct((nq, LANES, T), BF16)
    stats = struct((8, shard), F32)

    def keys_scratch(tiles):
        return [
            pltpu.VMEM((width, tiles * T), BF16), pltpu.VMEM((tiles * T, LANES), BF16), pltpu.VMEM((8, LANES), F32)
        ]

    unit = 2 * shard * width * width
    chip_tiles, far_tiles = 2 * nq + 1, 3 * nq + 2
    keys = lambda tiles: struct((tiles * T, width), BF16)
    block = pltpu.VMEM((shard, width), BF16)
    weight = pltpu.VMEM((width, width), BF16)
    wide = pltpu.VMEM((width, shard), F32)
    square = pltpu.VMEM((width, width), F32)
    stat = pltpu.VMEM((8, shard), F32)
    part = struct((shard, width), BF16)
    q, qt, k_chip, v_chip, top, total, acc, norms, qm = call(
        functools.partial(attend_chip_kernel, nq),
        (meta, bounds, bounds_t, row(b_query), row(b_value)),
        (tokens, w_query, w_key, w_value, x_partner),
        (
            part, struct((width, shard), BF16), keys(chip_tiles), keys(chip_tiles), stats, stats,
            struct((width, shard), F32), struct((8, LANES), F32), tile_mask,
        ),
        keys_scratch(chip_tiles) + [block, weight, weight, weight, block, pltpu.SemaphoreType.DMA((5,))],
        13 * unit,
    )
    x_forward = swap(after(x_near, norms))

    granule = 8 * dp * seq // 2
    grad_rows = (2 * hidden + 4 * width + 16 + granule - 1) // granule * granule
    vectors = jnp.stack([b_out, gain_one, shift_one, b_down, gain_two, shift_two, b_out, b_out])
    layer, input_grad, p_near, p_far, p_forward, p_partner, keep, send = call(
        functools.partial(layer_kernel, nq),
        (meta, bounds, row(b_value), vectors, row(b_up), norms, qm),
        (
            w_key, w_value, x_near, x_far, x_forward, qt, top, total, acc,
            w_out, tokens, w_up, w_down, cotangent, q, k_chip, v_chip, x_partner, w_query,
        ),
        (
            part, struct((shard, width), F32), part, part, part, part,
            struct((grad_rows // 2, width), BF16), struct((grad_rows // 2, width), BF16),
        ),
        [
            weight, weight, block, block, block, pltpu.VMEM((width, shard), BF16), stat, stat, wide,
            weight, block, pltpu.VMEM((width, hidden), BF16), pltpu.VMEM((hidden, width), BF16), block, block,
            pltpu.VMEM((chip_tiles * T, width), BF16), pltpu.VMEM((chip_tiles * T, width), BF16), block, weight,
            pltpu.SemaphoreType.DMA((19,)), pltpu.SemaphoreType.DMA((8,)),
            pltpu.VMEM((grad_rows, width), BF16), pltpu.VMEM((shard, width), F32),
            pltpu.VMEM((far_tiles * T, width), BF16), pltpu.VMEM((far_tiles * T, width), BF16),
        ]
        + keys_scratch(far_tiles)
        + [stat, stat, pltpu.VMEM((8, width), F32)]
        + [block, block, pltpu.VMEM((width, shard), BF16)]
        + [pltpu.VMEM((hidden, width), F32), pltpu.VMEM((width, hidden), F32), square]
        + [pltpu.VMEM((8, width), F32)]
        + [
            pltpu.VMEM((width, T), BF16), pltpu.VMEM((T, LANES), BF16),
            pltpu.VMEM((T, width), F32), pltpu.VMEM((T, width), F32),
        ],
        60 * unit,
        out_space=pltpu.HBM,
    )
    summing = Summing(dp, seq)
    p_forward = swap(p_forward)
    grads = keep + summing.exchange(send)
    p_far = far(after(p_far, grads), back=True)
    p_partner = swap(after(p_partner, grads))
    p_near = p_near + p_forward
    grads = summing.halve(grads, {0: p_near, 1: p_partner, summing.dp_steps: p_far})
    steps = list(range(len(summing.order) - 1))[::-1]
    z_steps = len(steps) - summing.dp_steps
    grads = summing.double(grads, steps[:z_steps], {})
    p_near = near(after(p_near, grads))
    mine = summing.double(grads, steps[z_steps:], {0: p_near})
    other = summing.exchange(mine)
    input_grad = input_grad + p_partner.astype(F32) + p_far.astype(F32) + p_near.astype(F32)
    shapes = [(hidden, width), (width, hidden)] + [(width, width)] * 4 + [(16, width)]
    g_w_down, g_w_up, g_w_out, g_w_query, g_w_key, g_w_value, biases = call(
        widen_kernel,
        (core.reshape(1).astype(jnp.int32), mine, other),
        (),
        [struct(shape, F32) for shape in shapes],
        [pltpu.VMEM(shape, F32) for shape in shapes] + [pltpu.SemaphoreType.DMA((7,))],
        0,
        out_space=pltpu.HBM,
        limit=20 << 20,
    )
    g_b_up = biases[14 : 14 + hidden // width].reshape(hidden)
    return (
        layer, input_grad,
        g_w_query, biases[1], g_w_key, g_w_value, biases[0],
        g_w_out, biases[8], biases[9], biases[10], g_w_up, g_b_up, g_w_down, biases[11], biases[12], biases[13],
    )


def solution(mesh):
    rows = P(("dp", "seq"), None)
    return jax.shard_map(
        shards,
        mesh=mesh,
        in_specs=(rows, P("dp", None)) + (P(),) * 15 + (rows,),
        out_specs=(rows, rows) + (P(),) * 15,
        check_vma=False,
    )
```

```python
import functools
import math

import jax
import jax.numpy as jnp
from jax import lax
from jax.experimental import pallas as pl
from jax.experimental.pallas import tpu as pltpu
from jax.sharding import PartitionSpec as P

H = 4
HD = 128
EPS = 1e-05
BIG = 1e30
T = 256
LANES = 128
SCALE = 1.0 / math.sqrt(HD)
LOG2E = 1.0 / math.log(2.0)
LN2 = math.log(2.0)
F32 = jnp.float32
BF16 = jnp.bfloat16

NN = (((1,), (0,)), ((), ()))
NT = (((1,), (1,)), ((), ()))
TN = (((0,), (0,)), ((), ()))


def dot(left, right, dims=NN):
    return lax.dot_general(left, right, dims, preferred_element_type=F32)


def head(h):
    return slice(h * HD, (h + 1) * HD)


def query_mask(starts, ends, start):
    place = start + lax.broadcasted_iota(jnp.int32, (LANES, T), 1)
    inside = jnp.logical_and(place >= starts, place < ends)
    return jnp.where(inside, 1.0, 0.0).astype(BF16)


def key_mask(brow_ref, start):
    place = start + lax.broadcasted_iota(jnp.int32, (T, LANES), 0)
    inside = jnp.logical_and(place >= brow_ref[0:1, :], place < brow_ref[1:2, :])
    return jnp.where(inside, 0.0, -BIG).astype(BF16)


def tile_range(lo, hi, start, tiles):
    first = jnp.clip((lo - start) // T, 0, tiles)
    last = jnp.clip((hi - start + T - 1) // T, 0, tiles)
    return first, last


class Meta:
    def __init__(self, ref, nq):
        self.ref, self.nq = ref, nq
        self.chip, self.side, self.forward, self.own_tile, self.near_tile = (ref[2 * nq + j] for j in range(5))
        self.partner_tile = nq - self.own_tile
        self.far_tile = nq - self.near_tile
        self.own = self.chip + self.own_tile * T

    def lo(self, i):
        return self.ref[i]

    def hi(self, i):
        return self.ref[self.nq + i]

    @property
    def all_keys(self):
        return self.ref[0], self.ref[2 * self.nq - 1]


def survey(nq, seq, counts_ref, position_ref, meta_ref, brow_ref):
    position = position_ref[0]
    shard = nq * T
    sizes = [counts_ref[0, j] for j in range(counts_ref.shape[1])]
    starts, ends, end = [], [], 0
    for size in sizes:
        starts.append(end + 0 * size)
        end = end + size
        ends.append(end)
    for i in range(nq):
        first = position * shard + i * T
        lo, hi = 0, seq * shard
        for a, b in zip(starts[::-1], ends[::-1]):
            lo = jnp.maximum(lo, jnp.where(a <= first, a, 0))
            hi = jnp.minimum(hi, jnp.where(b > first + (T - 1), b, seq * shard))
        meta_ref[i] = lo
        meta_ref[nq + i] = hi
    core = position % 2
    side = position + jnp.where(core == 0, -2, 1)
    forward = position + jnp.where(core == 0, 2, -2)
    meta_ref[2 * nq] = (position - core) * shard
    meta_ref[2 * nq + 1] = jnp.where(jnp.logical_and(side >= 0, side + 1 < seq), side * shard, 1 << 28)
    meta_ref[2 * nq + 2] = jnp.where(jnp.logical_and(forward >= 0, forward < seq), forward * shard, 1 << 28)
    meta_ref[2 * nq + 3] = core * nq
    meta_ref[2 * nq + 4] = (1 - core) * nq

    def spread(values, shape, dimension):
        at = lax.broadcasted_iota(jnp.int32, shape, dimension)
        out = jnp.zeros(shape, jnp.int32)
        for j, value in enumerate(values):
            out = jnp.where(at == j, value, out)
        return out

    brow_ref[0:1, :] = spread(starts, (1, LANES), 1)
    brow_ref[1:2, :] = spread(ends, (1, LANES), 1)
    brow_ref[2:8, :] = jnp.zeros((6, LANES), jnp.int32)
    return spread(starts, (LANES, 1), 0), spread(ends, (LANES, 1), 0)


LIMIT_SQUARED = 9000.0


def head_pick(width):
    shape = (width, LANES)
    same = lax.broadcasted_iota(jnp.int32, shape, 0) // HD == lax.broadcasted_iota(jnp.int32, shape, 1)
    return jnp.where(same, 1.0, 0.0).astype(BF16)


def keep_norms(norm_ref, rows):
    squares = dot((rows * rows).astype(BF16), head_pick(rows.shape[1]))
    norm_ref[0:1, :] = jnp.maximum(norm_ref[0:1, :], jnp.max(squares, axis=0, keepdims=True))


def attend(meta, segments, qt_ref, k_ref, vt_ref, km_ref, qm_ref, acc_ref, top_ref, total_ref, safe, finish):
    nq = meta.nq

    def query_tile(i, carry):
        q0 = pl.multiple_of(i * T, T)
        qs = pl.ds(q0, T)

        def scores(h, k0):
            ks = pl.ds(k0, 2 * T)
            kx = jnp.concatenate([k_ref[ks, head(h)], km_ref[ks, :]], axis=1)
            qx = jnp.concatenate([qt_ref[head(h), qs], qm_ref[i]], axis=0)
            return dot(kx, qx)

        def weigh(h, k0, p):
            values = jnp.concatenate([vt_ref[head(h), pl.ds(k0, 2 * T)], jnp.ones((16, 2 * T), BF16)], axis=0)
            return dot(values, p)

        def plain(k0):
            ps = [jnp.exp2(scores(h, k0)).astype(BF16) for h in range(H)]
            sums = [weigh(h, k0, ps[h]) for h in range(H)]
            acc_ref[:, qs] += jnp.concatenate([out[0:HD] for out in sums], axis=0)
            for h in range(H):
                total_ref[h : h + 1, qs] += sums[h][HD : HD + 1]

        def guarded(k0):
            for h in range(H):
                s = scores(h, k0)
                old = top_ref[h : h + 1, qs]
                top = jnp.maximum(old, jnp.max(s, axis=0, keepdims=True))
                decay = jnp.exp2(old - top)
                out = weigh(h, k0, jnp.exp2(s - top).astype(BF16))
                acc_ref[head(h), qs] = acc_ref[head(h), qs] * decay + out[0:HD]
                total_ref[h : h + 1, qs] = total_ref[h : h + 1, qs] * decay + out[HD : HD + 1]
                top_ref[h : h + 1, qs] = top

        def walk(body):
            for start, tile, tiles in segments:
                first, last = tile_range(meta.lo(i), meta.hi(i), start, tiles)

                def step(j, inner):
                    body(pl.multiple_of((tile + first + 2 * j) * T, T))
                    return inner

                lax.fori_loop(0, (last - first + 1) // 2, step, 0)

        @pl.when(safe)
        def _():
            walk(plain)

        @pl.when(jnp.logical_not(safe))
        def _():
            walk(guarded)

        finish(q0)
        return carry

    lax.fori_loop(0, nq, query_tile, 0)


def project_keys(meta, brow_ref, start, tile, x_ref, wk_ref, wv_ref, bv_ref, k_ref, v_ref, vt_ref, km_ref, norm_ref):
    lo, hi = meta.all_keys
    first, last = tile_range(lo, hi + T, start, meta.nq)

    def step(t, carry):
        r0 = pl.multiple_of(t * T, T)
        ks = pl.ds(pl.multiple_of((tile + t) * T, T), T)
        x = x_ref[pl.ds(r0, T), :]
        k = dot(x, wk_ref[...])
        v = (dot(x, wv_ref[...]) + bv_ref[...]).astype(BF16)
        k_ref[ks, :] = k.astype(BF16)
        v_ref[ks, :] = v
        vt_ref[:, ks] = v.T
        km_ref[ks, :] = key_mask(brow_ref, start + r0)
        keep_norms(norm_ref, k)
        return carry

    lax.fori_loop(first, last, step, 0)


def blank_tile(tile, k_ref, vt_ref, km_ref):
    ks = slice(tile * T, (tile + 1) * T)
    k_ref[ks, :] = jnp.zeros((T, k_ref.shape[1]), BF16)
    vt_ref[:, ks] = jnp.zeros((vt_ref.shape[0], T), BF16)
    km_ref[ks, :] = jnp.full((T, LANES), -BIG, BF16)


def bounded(query_norms, key_norms):
    return jnp.max(query_norms * key_norms) <= LIMIT_SQUARED


def copies_of(sources, targets, sems):
    return [pltpu.make_async_copy(src, dst, sems.at[n]) for n, (src, dst) in enumerate(zip(sources, targets))]


def start(copies):
    for copy in copies:
        copy.start()


def wait(copies):
    for copy in copies:
        copy.wait()


def attend_chip_kernel(
    nq, seq,
    counts_ref, position_ref, bq_ref, bv_ref, xp_ref, *refs,
):
    sources, meta_ref, outs, held, refs = refs[:4], refs[4], refs[5:15], refs[15:25], refs[25:]
    q_ref, qt_ref, k_ref, v_ref, top_ref, total_ref, acc_ref, norm_ref, qm_ref, brow_ref = held
    vt_ref, km_ref, kn_ref, x_ref, wq_ref, wk_ref, wv_ref, sems, out_sems = refs
    loads = copies_of(sources, (x_ref, wq_ref, wk_ref, wv_ref), sems)
    stores = copies_of(held, outs, out_sems)
    start(loads[:2])
    starts, ends = survey(nq, seq, counts_ref, position_ref, meta_ref, brow_ref)
    meta = Meta(meta_ref, nq)
    wait(loads[:2])
    start(loads[2:])
    norm_ref[...] = jnp.zeros_like(norm_ref)
    kn_ref[...] = jnp.zeros_like(kn_ref)

    def make_query(i, carry):
        q0 = pl.multiple_of(i * T, T)
        q = (dot(x_ref[pl.ds(q0, T), :], wq_ref[...]) + bq_ref[...]) * (SCALE * LOG2E)
        low = q.astype(BF16)
        q_ref[pl.ds(q0, T), :] = low
        qt_ref[:, pl.ds(q0, T)] = low.T
        qm_ref[i] = query_mask(starts, ends, meta.own + q0)
        keep_norms(norm_ref, q)
        return carry

    lax.fori_loop(0, nq, make_query, 0)
    start(stores[:2] + stores[8:])
    wait(loads[2:])
    for rows, tile in ((x_ref, meta.own_tile), (xp_ref, meta.partner_tile)):
        project_keys(
            meta, brow_ref, meta.chip + tile * T, tile, rows, wk_ref, wv_ref, bv_ref,
            k_ref, v_ref, vt_ref, km_ref, kn_ref,
        )
    blank_tile(2 * nq, k_ref, vt_ref, km_ref)
    start(stores[2:4])
    acc_ref[...] = jnp.zeros_like(acc_ref)
    total_ref[...] = jnp.zeros_like(total_ref)
    safe = bounded(norm_ref[0:1, :], kn_ref[0:1, :])
    norm_ref[1:2, :] = jnp.full((1, LANES), jnp.where(safe, 1.0, 0.0), F32)
    top_ref[...] = jnp.full(top_ref.shape, jnp.where(safe, 0.0, -BIG), F32)
    attend(
        meta, [(meta.chip, 0, 2 * nq)], qt_ref, k_ref, vt_ref, km_ref, qm_ref, acc_ref, top_ref, total_ref, safe,
        lambda q0: None,
    )
    start(stores[4:8])
    wait(stores)


def attend_far(meta, brow_ref, blocks, queries, others, wk_ref, wv_ref, bv_ref, qt_ref, norm_ref, qm_ref,
               k_ref, v_ref, att_ref, attt_ref, lse_ref, vt_ref, km_ref, kn_ref, top_ref, total_ref):
    nq = meta.nq
    kn_ref[...] = jnp.zeros_like(kn_ref)
    for copies, rows, first_row, tile in blocks:
        wait(copies)
        project_keys(
            meta, brow_ref, first_row, tile, rows, wk_ref, wv_ref, bv_ref, k_ref, v_ref, vt_ref, km_ref, kn_ref
        )
    blank_tile(2 * nq, k_ref, vt_ref, km_ref)
    blank_tile(3 * nq + 1, k_ref, vt_ref, km_ref)
    wait(queries)
    start(others)

    def finish(q0):
        qs = pl.ds(q0, T)
        for h in range(H):
            total = total_ref[h : h + 1, qs]
            lse_ref[h : h + 1, qs] = top_ref[h : h + 1, qs] + jnp.log2(total)
            att = attt_ref[head(h), qs] / total
            attt_ref[head(h), qs] = att
            att_ref[qs, head(h)] = att.T.astype(BF16)

    safe = jnp.logical_and(bounded(norm_ref[0:1, :], kn_ref[0:1, :]), jnp.max(norm_ref[1:2, :]) > 0.5)
    attend(
        meta, [(meta.side, 0, 2 * nq), (meta.forward, 2 * nq + 1, nq)], qt_ref, k_ref, vt_ref, km_ref, qm_ref,
        attt_ref, top_ref, total_ref, safe, finish,
    )


def column_sum(rows):
    return jnp.sum(rows, axis=0, keepdims=True)


def mean(rows):
    return jnp.mean(rows, axis=-1, keepdims=True)


def norm(rows):
    centre = rows - mean(rows)
    inverse = lax.rsqrt(mean(centre * centre) + EPS)
    return centre * inverse, inverse


def norm_back(grad, n, inverse):
    return inverse * (grad - mean(grad) - n * mean(grad * n))


def middle(
    nq, x_ref, cot_ref, att_ref, attt_ref, wo_ref, wu_ref, wd_ref, vectors, bup_ref,
    dfirst_ref, da_ref, dat_ref, delta_ref, small_ref, gd_ref, gu_ref, go_ref,
):
    width = x_ref.shape[1]
    hidden = wu_ref.shape[1]
    b_out, gain_one, shift_one, b_down, gain_two, shift_two = (ref[...] for ref in vectors)
    for ref in (gd_ref, gu_ref, go_ref, small_ref):
        ref[...] = jnp.zeros_like(ref)
    rows_of = lambda tiles: jnp.concatenate(tiles, axis=0)

    def row_tiles(i, carry):
        both = [pl.ds(pl.multiple_of((2 * i + n) * T, T), T) for n in range(2)]
        att = [att_ref[rs, :] for rs in both]
        branch = [dot(a, wo_ref[...]) for a in att]
        one = [norm(x_ref[rs, :].astype(F32) + b + b_out) for rs, b in zip(both, branch)]
        normed = [n * gain_one + shift_one for n, _ in one]
        normed_low = [n.astype(BF16) for n in normed]
        pre, act_low, slope = [], [], []
        for n in range(2):
            pre.append(dot(normed_low[n], wu_ref[...]) + bup_ref[...])
        for n in range(2):
            cdf = 0.5 * (1.0 + lax.erf(pre[n] * math.sqrt(0.5)))
            act_low.append((pre[n] * cdf).astype(BF16))
            slope.append(cdf + pre[n] * (jnp.exp(-0.5 * pre[n] * pre[n]) * (1.0 / math.sqrt(2.0 * math.pi))))
        down = [dot(act, wd_ref[...]) for act in act_low]
        two = [norm(n + d + b_down) for n, d in zip(normed, down)]
        cot = [cot_ref[rs, :].astype(F32) for rs in both]
        for rs, (n, _) in zip(both, two):
            cot_ref[rs, :] = (n * gain_two + shift_two).astype(BF16)
        d_sum = [norm_back(c * gain_two, n, inverse) for c, (n, inverse) in zip(cot, two)]
        d_ffn = [d.astype(BF16) for d in d_sum]
        d_act = [dot(d, wd_ref[...], NT) for d in d_ffn]
        gd_ref[...] += dot(rows_of(act_low), rows_of(d_ffn), TN)
        d_pre = [(d * s).astype(BF16) for d, s in zip(d_act, slope)]
        d_normed = [a + dot(d, wu_ref[...], NT) for a, d in zip(d_sum, d_pre)]
        gu_ref[...] += dot(rows_of(normed_low), rows_of(d_pre), TN)
        d_first = [norm_back(d * gain_one, n, inverse) for d, (n, inverse) in zip(d_normed, one)]
        d_branch = [d.astype(BF16) for d in d_first]
        d_att = [dot(d, wo_ref[...], NT).astype(BF16) for d in d_branch]
        go_ref[...] += dot(rows_of(att), rows_of(d_branch), TN)
        for rs, d, a in zip(both, d_first, d_att):
            dfirst_ref[rs, :] = d
            da_ref[rs, :] = a
            turned = a.T
            dat_ref[:, rs] = turned
            for h in range(H):
                delta_ref[h : h + 1, rs] = column_sum(turned[head(h), :].astype(F32) * attt_ref[head(h), rs])
        pair_sum = lambda rows: column_sum(rows[0].astype(F32) + rows[1].astype(F32))
        up = pair_sum(d_pre)
        sums = [
            pair_sum(d_branch),
            pair_sum([d * n for d, (n, _) in zip(d_normed, one)]),
            pair_sum(d_normed),
            pair_sum(d_ffn),
            pair_sum([c * n for c, (n, _) in zip(cot, two)]),
            pair_sum(cot),
        ]
        for at in range(0, hidden, width):
            sums.append(up[:, at : at + width])
        small_ref[...] += jnp.concatenate(sums, axis=0)
        return carry

    lax.fori_loop(0, nq // 2, row_tiles, 0)


def attend_back(
    meta, brow_ref, start, tile, k_ref, v_ref, q_ref, qt_ref, da_ref, dat_ref, lse_ref, delta_ref, qm_ref,
    kt_ref, km_ref, dk_ref, dv_ref, dq_ref,
):
    nq = meta.nq
    first, last = tile_range(*meta.all_keys, start, nq)

    def rows_at(t):
        return pl.ds(pl.multiple_of((tile + t) * T, T), T)

    def blank(t, carry):
        for ref in (k_ref, v_ref):
            ref[rows_at(t), :] = jnp.zeros((T, ref.shape[1]), BF16)
        return carry

    def key_tile(t, carry):
        ks = rows_at(t)
        row = start + t * T
        q_first = sum((meta.hi(i) <= row).astype(jnp.int32) for i in range(nq))
        q_last = sum((meta.lo(i) < row + T).astype(jnp.int32) for i in range(nq))
        km_ref[...] = key_mask(brow_ref, row)
        kt_ref[...] = k_ref[ks, :].T
        dk_ref[...] = jnp.zeros_like(dk_ref)
        dv_ref[...] = jnp.zeros_like(dv_ref)

        def query_tile(i, inner):
            qs = pl.ds(pl.multiple_of(i * T, T), T)
            ps, ds, sums = [], [], []

            def products(h):
                sums.append((dot(ps[h], da_ref[qs, head(h)]), dot(ds[h], q_ref[qs, head(h)]), dot(kt_ref[head(h), :], ds[h])))

            for h in range(H):
                kx = jnp.concatenate([k_ref[ks, head(h)], km_ref[...]], axis=1)
                qx = jnp.concatenate([qt_ref[head(h), qs], qm_ref[i]], axis=0)
                p = jnp.exp2(dot(kx, qx) - lse_ref[h : h + 1, qs])
                ps.append(p.astype(BF16))
                dp = dot(v_ref[ks, head(h)], dat_ref[head(h), qs])
                ds.append((p * (dp - delta_ref[h : h + 1, qs])).astype(BF16))
                if h >= 2:
                    products(h - 2)
            products(H - 2)
            products(H - 1)
            dv_ref[...] += jnp.concatenate([out[0] for out in sums], axis=1)
            dk_ref[...] += jnp.concatenate([out[1] for out in sums], axis=1)
            dq_ref[:, qs] += jnp.concatenate([out[2] for out in sums], axis=0)
            return inner

        lax.fori_loop(q_first, q_last, query_tile, 0)
        k_ref[ks, :] = (dk_ref[...] * LN2).astype(BF16)
        v_ref[ks, :] = dv_ref[...].astype(BF16)
        return carry

    lax.fori_loop(0, first, blank, 0)
    lax.fori_loop(first, last, key_tile, 0)
    lax.fori_loop(last, nq, blank, 0)


def layer_kernel(
    nq,
    meta_ref, brow_ref, bv_ref, bup_ref, norm_ref, qm_ref, xw_ref, *refs,
):
    vectors, refs = refs[:6], refs[6:]
    count = 18
    sources, refs = refs[:count], refs[count:]
    layer_out, ig_out, pn_out, pf_out, pw_out, pp_out, keep_out, send_out = refs[:8]
    refs = refs[8:]
    staged, refs = refs[:count], refs[count:]
    sems, out_sems, grads_ref, ig_ref, k_ref, v_ref, vt_ref, km_ref, kn_ref, lse_ref, delta_ref, small_ref = refs[:12]
    att_ref, da_ref, dat_ref, gd_ref, gu_ref, go_ref, sum_ref = refs[12:19]
    kt_ref, mask_ref, dk_ref, dv_ref = refs[19:]
    loads = copies_of(sources, staged, sems)
    start(loads[:4])
    wk_ref, wv_ref, xn_ref, xf_ref, qt_ref, top_ref, total_ref, attt_ref = staged[:8]
    wo_ref, x_ref, wu_ref, wd_ref, cot_ref, q_ref, kc_ref, vc_ref, xp_ref, wq_ref = staged[8:]
    stores = []

    def store(source, target):
        copy = pltpu.make_async_copy(source, target, out_sems.at[len(stores)])
        copy.start()
        stores.append(copy)

    meta = Meta(meta_ref, nq)
    near_start = meta.side + meta.near_tile * T
    far_start = meta.side + meta.far_tile * T
    wait(loads[:2])
    start(loads[4:8])
    attend_far(
        meta, brow_ref,
        (
            ([], xw_ref, meta.forward, 2 * nq + 1),
            (loads[2:3], xn_ref, near_start, meta.near_tile),
            (loads[3:4], xf_ref, far_start, meta.far_tile),
        ),
        loads[4:8],
        loads[8:],
        wk_ref, wv_ref, bv_ref, qt_ref, norm_ref, qm_ref,
        k_ref, v_ref, att_ref, attt_ref, lse_ref, vt_ref, km_ref, kn_ref, top_ref, total_ref,
    )
    wait(loads[8:13])
    middle(
        nq, x_ref, cot_ref, att_ref, attt_ref, wo_ref, wu_ref, wd_ref, vectors, bup_ref,
        ig_ref, da_ref, dat_ref, delta_ref, small_ref, gd_ref, gu_ref, go_ref,
    )
    store(cot_ref, layer_out)
    hidden, width = wd_ref.shape
    shard = x_ref.shape[0]
    grads_ref[0:hidden, :] = gd_ref[...].astype(BF16)
    for part in range(hidden // width):
        at = hidden + part * width
        grads_ref[at : at + width, :] = gu_ref[:, part * width : (part + 1) * width].astype(BF16)
    base = 2 * hidden + width
    grads_ref[base - width : base, :] = go_ref[...].astype(BF16)
    half = grads_ref.shape[0] // 2
    assert half <= base
    first_core = meta.own_tile == 0

    def store_half(source, stays):
        copies = [pltpu.make_async_copy(source, target, out_sems.at[len(stores)]) for target in (keep_out, send_out)]
        pl.when(stays)(copies[0].start)
        pl.when(jnp.logical_not(stays))(copies[1].start)
        stores.append(copies[0])

    store_half(grads_ref.at[0:half, :], first_core)

    wait(loads[13:])
    xt_ref = vt_ref.at[:, 0:shard]
    dq_ref = attt_ref
    dwk_ref = gd_ref.at[0:width, :]
    dwv_ref = gd_ref.at[width : 2 * width, :]
    wkv_ref = wd_ref
    wkv_ref[0:width, :] = wk_ref[...].T
    wkv_ref[width : 2 * width, :] = wv_ref[...].T
    wo_ref[...] = wq_ref[...].T
    for ref in (dq_ref, dwk_ref, dwv_ref, sum_ref):
        ref[...] = jnp.zeros_like(ref)
    for rows, part_ref, out, first_row, tile, keys_ref, values_ref in (
        (xn_ref, xn_ref, pn_out, near_start, meta.near_tile, k_ref, v_ref),
        (xf_ref, xf_ref, pf_out, far_start, meta.far_tile, k_ref, v_ref),
        (xw_ref, att_ref, pw_out, meta.forward, 2 * nq + 1, k_ref, v_ref),
        (xp_ref, xp_ref, pp_out, meta.chip + meta.partner_tile * T, meta.partner_tile, kc_ref, vc_ref),
        (x_ref, None, None, meta.own, meta.own_tile, kc_ref, vc_ref),
    ):
        first, last = tile_range(*meta.all_keys, first_row, nq)

        def work(rows=rows, part_ref=part_ref, out=out, first_row=first_row, tile=tile, keys_ref=keys_ref, values_ref=values_ref):
            attend_back(
                meta, brow_ref, first_row, tile, keys_ref, values_ref, q_ref, qt_ref, da_ref, dat_ref,
                lse_ref, delta_ref, qm_ref, kt_ref, mask_ref, dk_ref, dv_ref, dq_ref,
            )
            block = pl.ds(pl.multiple_of(tile * T, T), shard)
            xt_ref[...] = rows[...].T
            dwk_ref[...] += dot(xt_ref[...], keys_ref[block, :])
            dwv_ref[...] += dot(xt_ref[...], values_ref[block, :])
            sum_ref[0:1, :] += column_sum(values_ref[block, :].astype(F32))

            def input_tile(t, carry):
                rs = pl.ds(pl.multiple_of(2 * t * T, 2 * T), 2 * T)
                ks = pl.ds(pl.multiple_of((tile + 2 * t) * T, T), 2 * T)
                grad = dot(jnp.concatenate([keys_ref[ks, :], values_ref[ks, :]], axis=1), wkv_ref[...])
                if out is None:
                    ig_ref[rs, :] += grad
                else:
                    part_ref[rs, :] = grad.astype(BF16)
                return carry

            lax.fori_loop(0, nq // 2, input_tile, 0)

        if out is None:
            work()
        else:
            pl.when(first < last)(work)

            @pl.when(first >= last)
            def _(part_ref=part_ref):
                part_ref[...] = jnp.zeros_like(part_ref)

            store(part_ref, out)

    dwk_low = dwk_ref[...].astype(BF16)
    dwv_low = dwv_ref[...].astype(BF16)

    def query_tile(i, carry):
        qs = pl.ds(pl.multiple_of(i * T, T), T)
        dq = (dq_ref[:, qs] * SCALE).astype(BF16).T
        q_ref[qs, :] = dq
        sum_ref[1:2, :] += column_sum(dq.astype(F32))
        ig_ref[qs, :] += dot(dq, wo_ref[...])
        return carry

    lax.fori_loop(0, nq, query_tile, 0)
    store(ig_ref, ig_out)
    grads_ref[base : base + width, :] = dot(xt_ref[...], q_ref[...]).astype(BF16)
    grads_ref[base + width : base + 2 * width, :] = dwk_low
    grads_ref[base + 2 * width : base + 3 * width, :] = dwv_low
    end = base + 3 * width
    rows = jnp.concatenate([sum_ref[...], small_ref[...]], axis=0)
    grads_ref[end : end + 16, :] = rows.astype(BF16)
    grads_ref[end + 16 :, :] = jnp.zeros((grads_ref.shape[0] - end - 16, width), BF16)
    store_half(grads_ref.at[half:, :], jnp.logical_not(first_core))
    wait(stores)


def vmem(count):
    return [pl.BlockSpec(memory_space=pltpu.VMEM)] * count


VMEM_LIMIT = 60 << 20


def call(kernel, inputs, staged, outputs, scratch, flops, scalars=1, out_scalars=0, limit=VMEM_LIMIT):
    size = lambda arrays: sum(math.prod(a.shape) * jnp.dtype(a.dtype).itemsize for a in arrays)
    everything = tuple(inputs) + tuple(staged)
    smem = [pl.BlockSpec(memory_space=pltpu.SMEM)]
    hbm = [pl.BlockSpec(memory_space=pltpu.HBM)]
    return pl.pallas_call(
        kernel,
        out_shape=outputs,
        in_specs=smem * scalars + vmem(len(inputs) - scalars) + hbm * len(staged),
        out_specs=smem * out_scalars + hbm * (len(outputs) - out_scalars),
        scratch_shapes=scratch,
        compiler_params=pltpu.CompilerParams(vmem_limit_bytes=limit),
        cost_estimate=pl.CostEstimate(
            flops=flops, bytes_accessed=size(everything) + size(outputs), transcendentals=0
        ),
    )(*everything)


def struct(shape, dtype):
    return jax.ShapeDtypeStruct(shape, dtype)


def after(value, other):
    return lax.optimization_barrier((value, other))[0]


class Summing:
    def __init__(self, dp, seq):
        dp_masks = [seq * (1 << j) for j in range(dp.bit_length() - 1)]
        seq_masks = [1 << j for j in range(seq.bit_length() - 1)]
        self.order = [(dp_masks[j], dp_masks[(j + 1) % len(dp_masks)]) for j in range(len(dp_masks))]
        self.dp_steps = len(self.order)
        self.order += [(mask, mask) for mask in seq_masks[1:]]
        self.devices = dp * seq
        core = lax.axis_index("seq") % 2
        index = lax.axis_index("dp") * seq + lax.axis_index("seq")
        self.bits = [jnp.where(core == 0, index // even, index // odd) % 2 for even, odd in self.order]

    def exchange(self, rows, even=1, odd=1):
        pairs = [(i, i ^ (even if i % 2 == 0 else odd)) for i in range(self.devices)]
        return lax.ppermute(rows, ("dp", "seq"), pairs)

    def halve(self, rows, waits):
        for number, (even, odd) in enumerate(self.order[:-1]):
            half = rows.shape[0] // 2
            bit = self.bits[number]
            mine = lax.dynamic_slice_in_dim(rows, bit * half, half, 0)
            got = self.exchange(lax.dynamic_slice_in_dim(rows, (1 - bit) * half, half, 0), even, odd)
            rows = (after(mine, waits[number]) if number in waits else mine) + got
        return rows + self.exchange(rows, *self.order[-1])

    def double(self, rows, numbers, waits):
        for number in numbers:
            got = self.exchange(rows, *self.order[number])
            half = rows.shape[0]
            if number in waits:
                rows = after(rows, waits[number])
            whole = jnp.zeros((2 * half, rows.shape[1]), rows.dtype)
            whole = lax.dynamic_update_slice_in_dim(whole, rows, self.bits[number] * half, 0)
            rows = lax.dynamic_update_slice_in_dim(whole, got, (1 - self.bits[number]) * half, 0)
        return rows


def widen_kernel(bias_rows, core_ref, mine_ref, other_ref, *refs):
    count = 6 + len(bias_rows)
    outs, wide, sems = refs[:count], refs[count : 2 * count], refs[2 * count]
    half, width = mine_ref.shape
    hidden = wide[0].shape[0]
    spans = [(0, hidden, 0, 0)]
    spans += [(hidden + at, width, 1, at) for at in range(0, hidden, width)]
    spans += [(2 * hidden + n * width, width, 2 + n, 0) for n in range(4)]
    copies = copies_of(wide, outs, sems)

    def write(low_ref, high_ref):
        for first_row, rows, number, column in spans:
            for source, base in ((low_ref, 0), (high_ref, half)):
                first, last = max(first_row, base), min(first_row + rows, base + half)
                if first < last:
                    wide[number][first - first_row : last - first_row, column : column + width] = source[
                        first - base : last - base, :
                    ].astype(F32)
            if column + width == wide[number].shape[1]:
                copies[number].start()
        at = 2 * hidden + 4 * width - half
        vectors = high_ref[at : at + 16, :].astype(F32)
        for number, rows in enumerate(bias_rows):
            for part, row in enumerate(rows):
                wide[6 + number][:, part * width : (part + 1) * width] = vectors[row : row + 1, :]
            copies[6 + number].start()

    @pl.when(core_ref[0] == 0)
    def _():
        write(mine_ref, other_ref)

    @pl.when(core_ref[0] != 0)
    def _():
        write(other_ref, mine_ref)

    wait(copies)


def shards(
    tokens, counts, w_query, b_query, w_key, w_value, b_value, w_out, b_out, gain_one, shift_one,
    w_up, b_up, w_down, b_down, gain_two, shift_two, cotangent,
):
    shard, width = tokens.shape
    hidden = w_up.shape[1]
    nq = shard // T
    seq = lax.axis_size("seq")
    dp = lax.axis_size("dp")
    position = lax.axis_index("seq")

    def swap(rows):
        return lax.ppermute(rows, "seq", [(i, i ^ 1) for i in range(seq)])

    def near(rows):
        pairs = [(i, i + 1) for i in range(1, seq - 1, 2)]
        return lax.ppermute(rows, "seq", pairs + [(b, a) for a, b in pairs])

    def far(rows, back=False):
        pairs = [(i, i + 2) for i in range(0, seq - 2, 2)] + [(i, i - 2) for i in range(3, seq, 2)]
        return lax.ppermute(rows, "seq", [(b, a) for a, b in pairs] if back else pairs)

    x_partner = swap(tokens)
    x_near = near(tokens)
    x_far = far(tokens)

    core = position % 2
    row = lambda v: v.reshape(1, -1)
    tile_mask = struct((nq, LANES, T), BF16)
    stats = struct((8, shard), F32)

    def keys_scratch(tiles):
        return [
            pltpu.VMEM((width, tiles * T), BF16), pltpu.VMEM((tiles * T, LANES), BF16), pltpu.VMEM((8, LANES), F32)
        ]

    unit = 2 * shard * width * width
    chip_tiles, far_tiles = 2 * nq + 1, 3 * nq + 2
    keys = lambda tiles: struct((tiles * T, width), BF16)
    block = pltpu.VMEM((shard, width), BF16)
    weight = pltpu.VMEM((width, width), BF16)
    wide = pltpu.VMEM((width, shard), F32)
    square = pltpu.VMEM((width, width), F32)
    stat = pltpu.VMEM((8, shard), F32)
    part = struct((shard, width), BF16)
    meta, q, qt, k_chip, v_chip, top, total, acc, norms, qm, bounds = call(
        functools.partial(attend_chip_kernel, nq, seq),
        (counts, position.reshape(1).astype(jnp.int32), row(b_query), row(b_value), x_partner),
        (tokens, w_query, w_key, w_value),
        (
            struct((2 * nq + 5,), jnp.int32),
            part, struct((width, shard), BF16), keys(chip_tiles), keys(chip_tiles), stats, stats,
            struct((width, shard), F32), struct((8, LANES), F32), tile_mask, struct((8, LANES), jnp.int32),
        ),
        [
            block, pltpu.VMEM((width, shard), BF16), pltpu.VMEM((chip_tiles * T, width), BF16),
            pltpu.VMEM((chip_tiles * T, width), BF16), stat, stat, wide, pltpu.VMEM((8, LANES), F32),
            pltpu.VMEM((nq, LANES, T), BF16), pltpu.VMEM((8, LANES), jnp.int32),
        ]
        + keys_scratch(chip_tiles)
        + [block, weight, weight, weight, pltpu.SemaphoreType.DMA((4,)), pltpu.SemaphoreType.DMA((10,))],
        13 * unit,
        scalars=2,
        out_scalars=1,
    )
    x_forward = swap(after(x_near, norms))

    granule = 8 * dp * seq // 2
    grad_rows = (2 * hidden + 4 * width + 16 + granule - 1) // granule * granule
    vectors = [row(v) for v in (b_out, gain_one, shift_one, b_down, gain_two, shift_two)]
    layer, input_grad, p_near, p_far, p_forward, p_partner, keep, send = call(
        functools.partial(layer_kernel, nq),
        (meta, bounds, row(b_value), row(b_up), norms, qm, x_forward, *vectors),
        (
            w_key, w_value, x_near, x_far, qt, top, total, acc,
            w_out, tokens, w_up, w_down, cotangent, q, k_chip, v_chip, x_partner, w_query,
        ),
        (
            part, struct((shard, width), F32), part, part, part, part,
            struct((grad_rows // 2, width), BF16), struct((grad_rows // 2, width), BF16),
        ),
        [
            weight, weight, block, block, pltpu.VMEM((width, shard), BF16), stat, stat, wide,
            weight, block, pltpu.VMEM((width, hidden), BF16), pltpu.VMEM((hidden, width), BF16), block, block,
            pltpu.VMEM((chip_tiles * T, width), BF16), pltpu.VMEM((chip_tiles * T, width), BF16), block, weight,
            pltpu.SemaphoreType.DMA((18,)), pltpu.SemaphoreType.DMA((8,)),
            pltpu.VMEM((grad_rows, width), BF16), pltpu.VMEM((shard, width), F32),
            pltpu.VMEM((far_tiles * T, width), BF16), pltpu.VMEM((far_tiles * T, width), BF16),
        ]
        + keys_scratch(far_tiles)
        + [stat, stat, pltpu.VMEM((8, width), F32)]
        + [block, block, pltpu.VMEM((width, shard), BF16)]
        + [pltpu.VMEM((hidden, width), F32), pltpu.VMEM((width, hidden), F32), square]
        + [pltpu.VMEM((8, width), F32)]
        + [
            pltpu.VMEM((width, T), BF16), pltpu.VMEM((T, LANES), BF16),
            pltpu.VMEM((T, width), F32), pltpu.VMEM((T, width), F32),
        ],
        60 * unit,
    )
    summing = Summing(dp, seq)
    p_forward = swap(p_forward)
    grads = keep + summing.exchange(send)
    p_far = far(after(p_far, grads), back=True)
    p_partner = swap(after(p_partner, grads))
    p_near = p_near + p_forward
    grads = summing.halve(grads, {0: p_near, 1: p_partner, summing.dp_steps: p_far})
    steps = list(range(len(summing.order) - 1))[::-1]
    z_steps = len(steps) - summing.dp_steps
    grads = summing.double(grads, steps[:z_steps], {})
    p_near = near(after(p_near, grads))
    mine = summing.double(grads, steps[z_steps:], {0: p_near})
    other = summing.exchange(mine)
    input_grad = input_grad + p_partner.astype(F32) + p_far.astype(F32) + p_near.astype(F32)
    bias_rows = [(0,), (1,)] + [(n,) for n in range(8, 14)] + [tuple(range(14, 14 + hidden // width))]
    shapes = [(hidden, width), (width, hidden)] + [(width, width)] * 4
    shapes += [(1, len(rows) * width) for rows in bias_rows]
    wide_grads = call(
        functools.partial(widen_kernel, bias_rows),
        (core.reshape(1).astype(jnp.int32), mine, other),
        (),
        [struct(shape, F32) for shape in shapes],
        [pltpu.VMEM(shape, F32) for shape in shapes] + [pltpu.SemaphoreType.DMA((len(shapes),))],
        0,
        limit=20 << 20,
    )
    g_w_down, g_w_up, g_w_out, g_w_query, g_w_key, g_w_value = wide_grads[:6]
    g_b_value, g_b_query, g_b_out, g_gain_one, g_shift_one, g_b_down, g_gain_two, g_shift_two, g_b_up = (
        v.reshape(-1) for v in wide_grads[6:]
    )
    return (
        layer, input_grad, g_w_query, g_b_query, g_w_key, g_w_value, g_b_value, g_w_out, g_b_out,
        g_gain_one, g_shift_one, g_w_up, g_b_up, g_w_down, g_b_down, g_gain_two, g_shift_two,
    )


def solution(mesh):
    rows = P(("dp", "seq"), None)
    return jax.shard_map(
        shards,
        mesh=mesh,
        in_specs=(rows, P("dp", None)) + (P(),) * 15 + (rows,),
        out_specs=(rows, rows) + (P(),) * 15,
        check_vma=False,
    )
```

```python
import functools
import math

import jax
import jax.numpy as jnp
from jax import lax
from jax.experimental import pallas as pl
from jax.experimental.pallas import tpu as pltpu
from jax.sharding import PartitionSpec as P

H = 4
HD = 128
EPS = 1e-05
BIG = 1e30
T = 256
LANES = 128
SCALE = 1.0 / math.sqrt(HD)
LOG2E = 1.0 / math.log(2.0)
LN2 = math.log(2.0)
F32 = jnp.float32
BF16 = jnp.bfloat16

NN = (((1,), (0,)), ((), ()))
NT = (((1,), (1,)), ((), ()))
TN = (((0,), (0,)), ((), ()))


def dot(left, right, dims=NN):
    return lax.dot_general(left, right, dims, preferred_element_type=F32)


def head(h):
    return slice(h * HD, (h + 1) * HD)


def query_mask(starts, ends, start):
    place = start + lax.broadcasted_iota(jnp.int32, (LANES, T), 1)
    inside = jnp.logical_and(place >= starts, place < ends)
    return jnp.where(inside, 1.0, 0.0).astype(BF16)


def key_mask(brow_ref, start):
    place = start + lax.broadcasted_iota(jnp.int32, (T, LANES), 0)
    inside = jnp.logical_and(place >= brow_ref[0:1, :], place < brow_ref[1:2, :])
    return jnp.where(inside, 0.0, -BIG).astype(BF16)


def tile_range(lo, hi, start, tiles):
    first = jnp.clip((lo - start) // T, 0, tiles)
    last = jnp.clip((hi - start + T - 1) // T, 0, tiles)
    return first, last


class Meta:
    def __init__(self, ref, nq):
        self.ref, self.nq = ref, nq
        self.chip, self.side, self.forward, self.own_tile, self.near_tile = (ref[2 * nq + j] for j in range(5))
        self.partner_tile = nq - self.own_tile
        self.far_tile = nq - self.near_tile
        self.own = self.chip + self.own_tile * T

    def lo(self, i):
        return self.ref[i]

    def hi(self, i):
        return self.ref[self.nq + i]

    @property
    def all_keys(self):
        return self.ref[0], self.ref[2 * self.nq - 1]


def survey(nq, seq, counts_ref, position_ref, meta_ref, brow_ref):
    position = position_ref[0]
    shard = nq * T
    sizes = [counts_ref[0, j] for j in range(counts_ref.shape[1])]
    starts, ends, end = [], [], 0
    for size in sizes:
        starts.append(end + 0 * size)
        end = end + size
        ends.append(end)
    for i in range(nq):
        first = position * shard + i * T
        lo, hi = 0, seq * shard
        for a, b in zip(starts[::-1], ends[::-1]):
            lo = jnp.maximum(lo, jnp.where(a <= first, a, 0))
            hi = jnp.minimum(hi, jnp.where(b > first + (T - 1), b, seq * shard))
        meta_ref[i] = lo
        meta_ref[nq + i] = hi
    core = position % 2
    side = position + jnp.where(core == 0, -2, 1)
    forward = position + jnp.where(core == 0, 2, -2)
    meta_ref[2 * nq] = (position - core) * shard
    meta_ref[2 * nq + 1] = jnp.where(jnp.logical_and(side >= 0, side + 1 < seq), side * shard, 1 << 28)
    meta_ref[2 * nq + 2] = jnp.where(jnp.logical_and(forward >= 0, forward < seq), forward * shard, 1 << 28)
    meta_ref[2 * nq + 3] = core * nq
    meta_ref[2 * nq + 4] = (1 - core) * nq

    def spread(values, shape, dimension):
        at = lax.broadcasted_iota(jnp.int32, shape, dimension)
        out = jnp.zeros(shape, jnp.int32)
        for j, value in enumerate(values):
            out = jnp.where(at == j, value, out)
        return out

    brow_ref[0:1, :] = spread(starts, (1, LANES), 1)
    brow_ref[1:2, :] = spread(ends, (1, LANES), 1)
    brow_ref[2:8, :] = jnp.zeros((6, LANES), jnp.int32)
    return spread(starts, (LANES, 1), 0), spread(ends, (LANES, 1), 0)


LIMIT_SQUARED = 9000.0


def head_pick(width):
    shape = (width, LANES)
    same = lax.broadcasted_iota(jnp.int32, shape, 0) // HD == lax.broadcasted_iota(jnp.int32, shape, 1)
    return jnp.where(same, 1.0, 0.0).astype(BF16)


def keep_norms(norm_ref, rows):
    squares = dot((rows * rows).astype(BF16), head_pick(rows.shape[1]))
    norm_ref[0:1, :] = jnp.maximum(norm_ref[0:1, :], jnp.max(squares, axis=0, keepdims=True))


def attend(meta, segments, qt_ref, k_ref, vt_ref, km_ref, qm_ref, acc_ref, top_ref, total_ref, safe, finish):
    nq = meta.nq

    def query_tile(i, carry):
        q0 = pl.multiple_of(i * T, T)
        qs = pl.ds(q0, T)

        def scores(h, k0):
            ks = pl.ds(k0, 2 * T)
            kx = jnp.concatenate([k_ref[ks, head(h)], km_ref[ks, :]], axis=1)
            qx = jnp.concatenate([qt_ref[head(h), qs], qm_ref[i]], axis=0)
            return dot(kx, qx)

        def weigh(h, k0, p):
            values = jnp.concatenate([vt_ref[head(h), pl.ds(k0, 2 * T)], jnp.ones((16, 2 * T), BF16)], axis=0)
            return dot(values, p)

        def plain(k0):
            ps = [jnp.exp2(scores(h, k0)).astype(BF16) for h in range(H)]
            sums = [weigh(h, k0, ps[h]) for h in range(H)]
            acc_ref[:, qs] += jnp.concatenate([out[0:HD] for out in sums], axis=0)
            for h in range(H):
                total_ref[h : h + 1, qs] += sums[h][HD : HD + 1]

        def guarded(k0):
            for h in range(H):
                s = scores(h, k0)
                old = top_ref[h : h + 1, qs]
                top = jnp.maximum(old, jnp.max(s, axis=0, keepdims=True))
                decay = jnp.exp2(old - top)
                out = weigh(h, k0, jnp.exp2(s - top).astype(BF16))
                acc_ref[head(h), qs] = acc_ref[head(h), qs] * decay + out[0:HD]
                total_ref[h : h + 1, qs] = total_ref[h : h + 1, qs] * decay + out[HD : HD + 1]
                top_ref[h : h + 1, qs] = top

        def walk(body):
            for start, tile, tiles in segments:
                first, last = tile_range(meta.lo(i), meta.hi(i), start, tiles)

                def step(j, inner):
                    body(pl.multiple_of((tile + first + 2 * j) * T, T))
                    return inner

                lax.fori_loop(0, (last - first + 1) // 2, step, 0)

        @pl.when(safe)
        def _():
            walk(plain)

        @pl.when(jnp.logical_not(safe))
        def _():
            walk(guarded)

        finish(q0)
        return carry

    lax.fori_loop(0, nq, query_tile, 0)


def project_keys(meta, brow_ref, start, tile, x_ref, wk_ref, wv_ref, bv_ref, k_ref, v_ref, vt_ref, km_ref, norm_ref):
    lo, hi = meta.all_keys
    first, last = tile_range(lo, hi + T, start, meta.nq)

    def step(t, carry):
        r0 = pl.multiple_of(t * T, T)
        ks = pl.ds(pl.multiple_of((tile + t) * T, T), T)
        x = x_ref[pl.ds(r0, T), :]
        k = dot(x, wk_ref[...])
        v = (dot(x, wv_ref[...]) + bv_ref[...]).astype(BF16)
        k_ref[ks, :] = k.astype(BF16)
        v_ref[ks, :] = v
        vt_ref[:, ks] = v.T
        km_ref[ks, :] = key_mask(brow_ref, start + r0)
        keep_norms(norm_ref, k)
        return carry

    lax.fori_loop(first, last, step, 0)


def blank_tile(tile, k_ref, vt_ref, km_ref):
    ks = slice(tile * T, (tile + 1) * T)
    k_ref[ks, :] = jnp.zeros((T, k_ref.shape[1]), BF16)
    vt_ref[:, ks] = jnp.zeros((vt_ref.shape[0], T), BF16)
    km_ref[ks, :] = jnp.full((T, LANES), -BIG, BF16)


def bounded(query_norms, key_norms):
    return jnp.max(query_norms * key_norms) <= LIMIT_SQUARED


def copies_of(sources, targets, sems):
    return [pltpu.make_async_copy(src, dst, sems.at[n]) for n, (src, dst) in enumerate(zip(sources, targets))]


def start(copies):
    for copy in copies:
        copy.start()


def wait(copies):
    for copy in copies:
        copy.wait()


def attend_chip_kernel(
    nq, seq,
    counts_ref, position_ref, bq_ref, bv_ref, xp_ref, *refs,
):
    sources, meta_ref, outs, held, refs = refs[:4], refs[4], refs[5:15], refs[15:25], refs[25:]
    q_ref, qt_ref, k_ref, v_ref, top_ref, total_ref, acc_ref, norm_ref, qm_ref, brow_ref = held
    vt_ref, km_ref, kn_ref, x_ref, wq_ref, wk_ref, wv_ref, sems, out_sems = refs
    loads = copies_of(sources, (x_ref, wq_ref, wk_ref, wv_ref), sems)
    stores = copies_of(held, outs, out_sems)
    start(loads[:2])
    starts, ends = survey(nq, seq, counts_ref, position_ref, meta_ref, brow_ref)
    meta = Meta(meta_ref, nq)
    wait(loads[:2])
    start(loads[2:])
    norm_ref[...] = jnp.zeros_like(norm_ref)
    kn_ref[...] = jnp.zeros_like(kn_ref)

    def make_query(i, carry):
        q0 = pl.multiple_of(i * T, T)
        q = (dot(x_ref[pl.ds(q0, T), :], wq_ref[...]) + bq_ref[...]) * (SCALE * LOG2E)
        low = q.astype(BF16)
        q_ref[pl.ds(q0, T), :] = low
        qt_ref[:, pl.ds(q0, T)] = low.T
        qm_ref[i] = query_mask(starts, ends, meta.own + q0)
        keep_norms(norm_ref, q)
        return carry

    lax.fori_loop(0, nq, make_query, 0)
    start(stores[:2] + stores[8:])
    wait(loads[2:])
    for rows, tile in ((x_ref, meta.own_tile), (xp_ref, meta.partner_tile)):
        project_keys(
            meta, brow_ref, meta.chip + tile * T, tile, rows, wk_ref, wv_ref, bv_ref,
            k_ref, v_ref, vt_ref, km_ref, kn_ref,
        )
    blank_tile(2 * nq, k_ref, vt_ref, km_ref)
    start(stores[2:4])
    acc_ref[...] = jnp.zeros_like(acc_ref)
    total_ref[...] = jnp.zeros_like(total_ref)
    safe = bounded(norm_ref[0:1, :], kn_ref[0:1, :])
    norm_ref[1:2, :] = jnp.full((1, LANES), jnp.where(safe, 1.0, 0.0), F32)
    top_ref[...] = jnp.full(top_ref.shape, jnp.where(safe, 0.0, -BIG), F32)
    attend(
        meta, [(meta.chip, 0, 2 * nq)], qt_ref, k_ref, vt_ref, km_ref, qm_ref, acc_ref, top_ref, total_ref, safe,
        lambda q0: None,
    )
    start(stores[4:8])
    wait(stores)


def attend_far(meta, brow_ref, blocks, queries, others, wk_ref, wv_ref, bv_ref, qt_ref, norm_ref, qm_ref,
               k_ref, v_ref, att_ref, attt_ref, lse_ref, vt_ref, km_ref, kn_ref, top_ref, total_ref):
    nq = meta.nq
    kn_ref[...] = jnp.zeros_like(kn_ref)
    for copies, rows, first_row, tile in blocks:
        wait(copies)
        project_keys(
            meta, brow_ref, first_row, tile, rows, wk_ref, wv_ref, bv_ref, k_ref, v_ref, vt_ref, km_ref, kn_ref
        )
    blank_tile(2 * nq, k_ref, vt_ref, km_ref)
    blank_tile(3 * nq + 1, k_ref, vt_ref, km_ref)
    wait(queries)
    start(others)

    def finish(q0):
        qs = pl.ds(q0, T)
        for h in range(H):
            total = total_ref[h : h + 1, qs]
            lse_ref[h : h + 1, qs] = top_ref[h : h + 1, qs] + jnp.log2(total)
            att = attt_ref[head(h), qs] / total
            attt_ref[head(h), qs] = att
            att_ref[qs, head(h)] = att.T.astype(BF16)

    safe = jnp.logical_and(bounded(norm_ref[0:1, :], kn_ref[0:1, :]), jnp.max(norm_ref[1:2, :]) > 0.5)
    attend(
        meta, [(meta.side, 0, 2 * nq), (meta.forward, 2 * nq + 1, nq)], qt_ref, k_ref, vt_ref, km_ref, qm_ref,
        attt_ref, top_ref, total_ref, safe, finish,
    )


def column_sum(rows):
    return jnp.sum(rows, axis=0, keepdims=True)


def mean(rows):
    return jnp.mean(rows, axis=-1, keepdims=True)


def norm(rows):
    centre = rows - mean(rows)
    inverse = lax.rsqrt(mean(centre * centre) + EPS)
    return centre * inverse, inverse


def norm_back(grad, n, inverse):
    return inverse * (grad - mean(grad) - n * mean(grad * n))


def middle(
    nq, x_ref, cot_ref, att_ref, attt_ref, wo_ref, wu_ref, wd_ref, vectors, bup_ref,
    dfirst_ref, da_ref, dat_ref, delta_ref, small_ref, gd_ref, gu_ref, go_ref,
):
    width = x_ref.shape[1]
    hidden = wu_ref.shape[1]
    b_out, gain_one, shift_one, b_down, gain_two, shift_two = (ref[...] for ref in vectors)
    for ref in (gd_ref, gu_ref, go_ref, small_ref):
        ref[...] = jnp.zeros_like(ref)
    rows_of = lambda tiles: jnp.concatenate(tiles, axis=0)

    def row_tiles(i, carry):
        both = [pl.ds(pl.multiple_of((2 * i + n) * T, T), T) for n in range(2)]
        att = [att_ref[rs, :] for rs in both]
        branch = [dot(a, wo_ref[...]) for a in att]
        one = [norm(x_ref[rs, :].astype(F32) + b + b_out) for rs, b in zip(both, branch)]
        normed = [n * gain_one + shift_one for n, _ in one]
        normed_low = [n.astype(BF16) for n in normed]
        pre, act_low, slope = [], [], []
        for n in range(2):
            pre.append(dot(normed_low[n], wu_ref[...]) + bup_ref[...])
        for n in range(2):
            cdf = 0.5 * (1.0 + lax.erf(pre[n] * math.sqrt(0.5)))
            act_low.append((pre[n] * cdf).astype(BF16))
            slope.append(cdf + pre[n] * (jnp.exp(-0.5 * pre[n] * pre[n]) * (1.0 / math.sqrt(2.0 * math.pi))))
        down = [dot(act, wd_ref[...]) for act in act_low]
        two = [norm(n + d + b_down) for n, d in zip(normed, down)]
        cot = [cot_ref[rs, :].astype(F32) for rs in both]
        for rs, (n, _) in zip(both, two):
            cot_ref[rs, :] = (n * gain_two + shift_two).astype(BF16)
        d_sum = [norm_back(c * gain_two, n, inverse) for c, (n, inverse) in zip(cot, two)]
        d_ffn = [d.astype(BF16) for d in d_sum]
        d_act = [dot(d, wd_ref[...], NT) for d in d_ffn]
        gd_ref[...] += dot(rows_of(act_low), rows_of(d_ffn), TN)
        d_pre = [(d * s).astype(BF16) for d, s in zip(d_act, slope)]
        d_normed = [a + dot(d, wu_ref[...], NT) for a, d in zip(d_sum, d_pre)]
        gu_ref[...] += dot(rows_of(normed_low), rows_of(d_pre), TN)
        d_first = [norm_back(d * gain_one, n, inverse) for d, (n, inverse) in zip(d_normed, one)]
        d_branch = [d.astype(BF16) for d in d_first]
        d_att = [dot(d, wo_ref[...], NT).astype(BF16) for d in d_branch]
        go_ref[...] += dot(rows_of(att), rows_of(d_branch), TN)
        for rs, d, a in zip(both, d_first, d_att):
            dfirst_ref[rs, :] = d
            da_ref[rs, :] = a
            turned = a.T
            dat_ref[:, rs] = turned
            for h in range(H):
                delta_ref[h : h + 1, rs] = column_sum(turned[head(h), :].astype(F32) * attt_ref[head(h), rs])
        pair_sum = lambda rows: column_sum(rows[0].astype(F32) + rows[1].astype(F32))
        up = pair_sum(d_pre)
        sums = [
            pair_sum(d_branch),
            pair_sum([d * n for d, (n, _) in zip(d_normed, one)]),
            pair_sum(d_normed),
            pair_sum(d_ffn),
            pair_sum([c * n for c, (n, _) in zip(cot, two)]),
            pair_sum(cot),
        ]
        for at in range(0, hidden, width):
            sums.append(up[:, at : at + width])
        small_ref[...] += jnp.concatenate(sums, axis=0)
        return carry

    lax.fori_loop(0, nq // 2, row_tiles, 0)


def attend_back(
    meta, brow_ref, start, tile, k_ref, v_ref, q_ref, qt_ref, da_ref, dat_ref, lse_ref, delta_ref, qm_ref,
    kt_ref, km_ref, dk_ref, dv_ref, dq_ref,
):
    nq = meta.nq
    first, last = tile_range(*meta.all_keys, start, nq)

    def rows_at(t):
        return pl.ds(pl.multiple_of((tile + t) * T, T), T)

    def blank(t, carry):
        for ref in (k_ref, v_ref):
            ref[rows_at(t), :] = jnp.zeros((T, ref.shape[1]), BF16)
        return carry

    def key_tile(t, carry):
        ks = rows_at(t)
        row = start + t * T
        q_first = sum((meta.hi(i) <= row).astype(jnp.int32) for i in range(nq))
        q_last = sum((meta.lo(i) < row + T).astype(jnp.int32) for i in range(nq))
        km_ref[...] = key_mask(brow_ref, row)
        kt_ref[...] = k_ref[ks, :].T
        dk_ref[...] = jnp.zeros_like(dk_ref)
        dv_ref[...] = jnp.zeros_like(dv_ref)

        def query_tile(i, inner):
            qs = pl.ds(pl.multiple_of(i * T, T), T)
            ps, ds, sums = [], [], []

            def products(h):
                sums.append((dot(ps[h], da_ref[qs, head(h)]), dot(ds[h], q_ref[qs, head(h)]), dot(kt_ref[head(h), :], ds[h])))

            for h in range(H):
                kx = jnp.concatenate([k_ref[ks, head(h)], km_ref[...]], axis=1)
                qx = jnp.concatenate([qt_ref[head(h), qs], qm_ref[i]], axis=0)
                p = jnp.exp2(dot(kx, qx) - lse_ref[h : h + 1, qs])
                ps.append(p.astype(BF16))
                dp = dot(v_ref[ks, head(h)], dat_ref[head(h), qs])
                ds.append((p * (dp - delta_ref[h : h + 1, qs])).astype(BF16))
                if h >= 2:
                    products(h - 2)
            products(H - 2)
            products(H - 1)
            dv_ref[...] += jnp.concatenate([out[0] for out in sums], axis=1)
            dk_ref[...] += jnp.concatenate([out[1] for out in sums], axis=1)
            dq_ref[:, qs] += jnp.concatenate([out[2] for out in sums], axis=0)
            return inner

        lax.fori_loop(q_first, q_last, query_tile, 0)
        k_ref[ks, :] = (dk_ref[...] * LN2).astype(BF16)
        v_ref[ks, :] = dv_ref[...].astype(BF16)
        return carry

    lax.fori_loop(0, first, blank, 0)
    lax.fori_loop(first, last, key_tile, 0)
    lax.fori_loop(last, nq, blank, 0)


def layer_kernel(
    nq,
    meta_ref, brow_ref, bv_ref, bup_ref, norm_ref, qm_ref, xw_ref, *refs,
):
    vectors, refs = refs[:6], refs[6:]
    count = 18
    sources, refs = refs[:count], refs[count:]
    layer_out, ig_out, pn_out, pf_out, pw_out, pp_out, keep_out, send_out = refs[:8]
    refs = refs[8:]
    staged, refs = refs[:count], refs[count:]
    sems, out_sems, grads_ref, ig_ref, k_ref, v_ref, vt_ref, km_ref, kn_ref, lse_ref, delta_ref, small_ref = refs[:12]
    att_ref, da_ref, dat_ref, gd_ref, gu_ref, go_ref, sum_ref = refs[12:19]
    kt_ref, mask_ref, dk_ref, dv_ref = refs[19:]
    loads = copies_of(sources, staged, sems)
    start(loads[:4])
    wk_ref, wv_ref, xn_ref, xf_ref, qt_ref, top_ref, total_ref, attt_ref = staged[:8]
    wo_ref, x_ref, wu_ref, wd_ref, cot_ref, q_ref, kc_ref, vc_ref, xp_ref, wq_ref = staged[8:]
    stores = []

    def store(source, target):
        copy = pltpu.make_async_copy(source, target, out_sems.at[len(stores)])
        copy.start()
        stores.append(copy)

    meta = Meta(meta_ref, nq)
    near_start = meta.side + meta.near_tile * T
    far_start = meta.side + meta.far_tile * T
    wait(loads[:2])
    start(loads[4:8])
    attend_far(
        meta, brow_ref,
        (
            ([], xw_ref, meta.forward, 2 * nq + 1),
            (loads[2:3], xn_ref, near_start, meta.near_tile),
            (loads[3:4], xf_ref, far_start, meta.far_tile),
        ),
        loads[4:8],
        loads[8:],
        wk_ref, wv_ref, bv_ref, qt_ref, norm_ref, qm_ref,
        k_ref, v_ref, att_ref, attt_ref, lse_ref, vt_ref, km_ref, kn_ref, top_ref, total_ref,
    )
    wait(loads[8:13])
    middle(
        nq, x_ref, cot_ref, att_ref, attt_ref, wo_ref, wu_ref, wd_ref, vectors, bup_ref,
        ig_ref, da_ref, dat_ref, delta_ref, small_ref, gd_ref, gu_ref, go_ref,
    )
    store(cot_ref, layer_out)
    hidden, width = wd_ref.shape
    shard = x_ref.shape[0]
    grads_ref[0:hidden, :] = gd_ref[...].astype(BF16)
    for part in range(hidden // width):
        at = hidden + part * width
        grads_ref[at : at + width, :] = gu_ref[:, part * width : (part + 1) * width].astype(BF16)
    base = 2 * hidden + width
    grads_ref[base - width : base, :] = go_ref[...].astype(BF16)
    half = grads_ref.shape[0] // 2
    assert half <= base
    first_core = meta.own_tile == 0

    def store_half(source, stays):
        copies = [pltpu.make_async_copy(source, target, out_sems.at[len(stores)]) for target in (keep_out, send_out)]
        pl.when(stays)(copies[0].start)
        pl.when(jnp.logical_not(stays))(copies[1].start)
        stores.append(copies[0])

    store_half(grads_ref.at[0:half, :], first_core)

    wait(loads[13:])
    xt_ref = vt_ref.at[:, 0:shard]
    dq_ref = attt_ref
    dwk_ref = gd_ref.at[0:width, :]
    dwv_ref = gd_ref.at[width : 2 * width, :]
    wkv_ref = wd_ref
    wkv_ref[0:width, :] = wk_ref[...].T
    wkv_ref[width : 2 * width, :] = wv_ref[...].T
    wo_ref[...] = wq_ref[...].T
    for ref in (dq_ref, dwk_ref, dwv_ref, sum_ref):
        ref[...] = jnp.zeros_like(ref)
    for rows, part_ref, out, first_row, tile, keys_ref, values_ref in (
        (xn_ref, xn_ref, pn_out, near_start, meta.near_tile, k_ref, v_ref),
        (xf_ref, xf_ref, pf_out, far_start, meta.far_tile, k_ref, v_ref),
        (xw_ref, att_ref, pw_out, meta.forward, 2 * nq + 1, k_ref, v_ref),
        (xp_ref, xp_ref, pp_out, meta.chip + meta.partner_tile * T, meta.partner_tile, kc_ref, vc_ref),
        (x_ref, None, None, meta.own, meta.own_tile, kc_ref, vc_ref),
    ):
        first, last = tile_range(*meta.all_keys, first_row, nq)

        def work(rows=rows, part_ref=part_ref, out=out, first_row=first_row, tile=tile, keys_ref=keys_ref, values_ref=values_ref):
            attend_back(
                meta, brow_ref, first_row, tile, keys_ref, values_ref, q_ref, qt_ref, da_ref, dat_ref,
                lse_ref, delta_ref, qm_ref, kt_ref, mask_ref, dk_ref, dv_ref, dq_ref,
            )
            block = pl.ds(pl.multiple_of(tile * T, T), shard)
            xt_ref[...] = rows[...].T
            dwk_ref[...] += dot(xt_ref[...], keys_ref[block, :])
            dwv_ref[...] += dot(xt_ref[...], values_ref[block, :])
            sum_ref[0:1, :] += column_sum(values_ref[block, :].astype(F32))

            def input_tile(t, carry):
                rs = pl.ds(pl.multiple_of(2 * t * T, 2 * T), 2 * T)
                ks = pl.ds(pl.multiple_of((tile + 2 * t) * T, T), 2 * T)
                grad = dot(jnp.concatenate([keys_ref[ks, :], values_ref[ks, :]], axis=1), wkv_ref[...])
                if out is None:
                    ig_ref[rs, :] += grad
                else:
                    part_ref[rs, :] = grad.astype(BF16)
                return carry

            lax.fori_loop(0, nq // 2, input_tile, 0)

        if out is None:
            work()
        else:
            pl.when(first < last)(work)

            @pl.when(first >= last)
            def _(part_ref=part_ref):
                part_ref[...] = jnp.zeros_like(part_ref)

            store(part_ref, out)

    dwk_low = dwk_ref[...].astype(BF16)
    dwv_low = dwv_ref[...].astype(BF16)

    def query_tile(i, carry):
        qs = pl.ds(pl.multiple_of(i * T, T), T)
        dq = (dq_ref[:, qs] * SCALE).astype(BF16).T
        q_ref[qs, :] = dq
        sum_ref[1:2, :] += column_sum(dq.astype(F32))
        ig_ref[qs, :] += dot(dq, wo_ref[...])
        return carry

    lax.fori_loop(0, nq, query_tile, 0)
    store(ig_ref, ig_out)
    grads_ref[base : base + width, :] = dot(xt_ref[...], q_ref[...]).astype(BF16)
    grads_ref[base + width : base + 2 * width, :] = dwk_low
    grads_ref[base + 2 * width : base + 3 * width, :] = dwv_low
    end = base + 3 * width
    rows = jnp.concatenate([sum_ref[...], small_ref[...]], axis=0)
    grads_ref[end : end + 16, :] = rows.astype(BF16)
    grads_ref[end + 16 :, :] = jnp.zeros((grads_ref.shape[0] - end - 16, width), BF16)
    store_half(grads_ref.at[half:, :], jnp.logical_not(first_core))
    wait(stores)


def vmem(count):
    return [pl.BlockSpec(memory_space=pltpu.VMEM)] * count


VMEM_LIMIT = 60 << 20


def call(kernel, inputs, staged, outputs, scratch, flops, scalars=1, out_scalars=0, limit=VMEM_LIMIT):
    size = lambda arrays: sum(math.prod(a.shape) * jnp.dtype(a.dtype).itemsize for a in arrays)
    everything = tuple(inputs) + tuple(staged)
    smem = [pl.BlockSpec(memory_space=pltpu.SMEM)]
    hbm = [pl.BlockSpec(memory_space=pltpu.HBM)]
    return pl.pallas_call(
        kernel,
        out_shape=outputs,
        in_specs=smem * scalars + vmem(len(inputs) - scalars) + hbm * len(staged),
        out_specs=smem * out_scalars + hbm * (len(outputs) - out_scalars),
        scratch_shapes=scratch,
        compiler_params=pltpu.CompilerParams(vmem_limit_bytes=limit),
        cost_estimate=pl.CostEstimate(
            flops=flops, bytes_accessed=size(everything) + size(outputs), transcendentals=0
        ),
    )(*everything)


def struct(shape, dtype):
    return jax.ShapeDtypeStruct(shape, dtype)


def after(value, other):
    return lax.optimization_barrier((value, other))[0]


class Summing:
    def __init__(self, dp, seq):
        dp_masks = [seq * (1 << j) for j in range(dp.bit_length() - 1)]
        seq_masks = [1 << j for j in range(seq.bit_length() - 1)]
        self.order = [(dp_masks[j], dp_masks[(j + 1) % len(dp_masks)]) for j in range(len(dp_masks))]
        self.dp_steps = len(self.order)
        self.order += [(mask, mask) for mask in seq_masks[1:]]
        self.devices = dp * seq
        core = lax.axis_index("seq") % 2
        index = lax.axis_index("dp") * seq + lax.axis_index("seq")
        self.bits = [jnp.where(core == 0, index // even, index // odd) % 2 for even, odd in self.order]

    def exchange(self, rows, even=1, odd=1):
        pairs = [(i, i ^ (even if i % 2 == 0 else odd)) for i in range(self.devices)]
        return lax.ppermute(rows, ("dp", "seq"), pairs)

    def halve(self, rows, number, other=None):
        half = rows.shape[0] // 2
        bit = self.bits[number]
        mine = lax.dynamic_slice_in_dim(rows, bit * half, half, 0)
        got = self.exchange(lax.dynamic_slice_in_dim(rows, (1 - bit) * half, half, 0), *self.order[number])
        return (mine if other is None else after(mine, other)) + got

    def whole(self, rows):
        return rows + self.exchange(rows, *self.order[-1])

    def double(self, rows, number, other=None):
        got = self.exchange(rows, *self.order[number])
        half = rows.shape[0]
        if other is not None:
            rows = after(rows, other)
        both = jnp.zeros((2 * half, rows.shape[1]), rows.dtype)
        both = lax.dynamic_update_slice_in_dim(both, rows, self.bits[number] * half, 0)
        return lax.dynamic_update_slice_in_dim(both, got, (1 - self.bits[number]) * half, 0)


def widen_kernel(bias_rows, core_ref, mine_one, mine_two, other_one, other_two, *refs):
    count = 6 + len(bias_rows)
    outs, wide, sems = refs[:count], refs[count : 2 * count], refs[2 * count]
    width = mine_one.shape[1]
    hidden = wide[0].shape[0]
    spans = [(0, hidden, 0, 0)]
    spans += [(hidden + at, width, 1, at) for at in range(0, hidden, width)]
    spans += [(2 * hidden + n * width, width, 2 + n, 0) for n in range(4)]
    copies = copies_of(wide, outs, sems)

    def write(*sources):
        bases = [sum(ref.shape[0] for ref in sources[:n]) for n in range(4)]
        for first_row, rows, number, column in spans:
            for source, base in zip(sources, bases):
                first, last = max(first_row, base), min(first_row + rows, base + source.shape[0])
                if first < last:
                    wide[number][first - first_row : last - first_row, column : column + width] = source[
                        first - base : last - base, :
                    ].astype(F32)
            if column + width == wide[number].shape[1]:
                copies[number].start()
        at = 2 * hidden + 4 * width - bases[3]
        vectors = sources[3][at : at + 16, :].astype(F32)
        for number, rows in enumerate(bias_rows):
            for part, row in enumerate(rows):
                wide[6 + number][:, part * width : (part + 1) * width] = vectors[row : row + 1, :]
            copies[6 + number].start()

    @pl.when(core_ref[0] == 0)
    def _():
        write(mine_one, mine_two, other_one, other_two)

    @pl.when(core_ref[0] != 0)
    def _():
        write(other_one, other_two, mine_one, mine_two)

    wait(copies)


def shards(
    tokens, counts, w_query, b_query, w_key, w_value, b_value, w_out, b_out, gain_one, shift_one,
    w_up, b_up, w_down, b_down, gain_two, shift_two, cotangent,
):
    shard, width = tokens.shape
    hidden = w_up.shape[1]
    nq = shard // T
    seq = lax.axis_size("seq")
    dp = lax.axis_size("dp")
    position = lax.axis_index("seq")

    def swap(rows):
        return lax.ppermute(rows, "seq", [(i, i ^ 1) for i in range(seq)])

    def near(rows):
        pairs = [(i, i + 1) for i in range(1, seq - 1, 2)]
        return lax.ppermute(rows, "seq", pairs + [(b, a) for a, b in pairs])

    def far(rows, back=False):
        pairs = [(i, i + 2) for i in range(0, seq - 2, 2)] + [(i, i - 2) for i in range(3, seq, 2)]
        return lax.ppermute(rows, "seq", [(b, a) for a, b in pairs] if back else pairs)

    x_partner = swap(tokens)
    x_near = near(tokens)
    x_far = far(tokens)

    core = position % 2
    row = lambda v: v.reshape(1, -1)
    tile_mask = struct((nq, LANES, T), BF16)
    stats = struct((8, shard), F32)

    def keys_scratch(tiles):
        return [
            pltpu.VMEM((width, tiles * T), BF16), pltpu.VMEM((tiles * T, LANES), BF16), pltpu.VMEM((8, LANES), F32)
        ]

    unit = 2 * shard * width * width
    chip_tiles, far_tiles = 2 * nq + 1, 3 * nq + 2
    keys = lambda tiles: struct((tiles * T, width), BF16)
    block = pltpu.VMEM((shard, width), BF16)
    weight = pltpu.VMEM((width, width), BF16)
    wide = pltpu.VMEM((width, shard), F32)
    square = pltpu.VMEM((width, width), F32)
    stat = pltpu.VMEM((8, shard), F32)
    part = struct((shard, width), BF16)
    meta, q, qt, k_chip, v_chip, top, total, acc, norms, qm, bounds = call(
        functools.partial(attend_chip_kernel, nq, seq),
        (counts, position.reshape(1).astype(jnp.int32), row(b_query), row(b_value), x_partner),
        (tokens, w_query, w_key, w_value),
        (
            struct((2 * nq + 5,), jnp.int32),
            part, struct((width, shard), BF16), keys(chip_tiles), keys(chip_tiles), stats, stats,
            struct((width, shard), F32), struct((8, LANES), F32), tile_mask, struct((8, LANES), jnp.int32),
        ),
        [
            block, pltpu.VMEM((width, shard), BF16), pltpu.VMEM((chip_tiles * T, width), BF16),
            pltpu.VMEM((chip_tiles * T, width), BF16), stat, stat, wide, pltpu.VMEM((8, LANES), F32),
            pltpu.VMEM((nq, LANES, T), BF16), pltpu.VMEM((8, LANES), jnp.int32),
        ]
        + keys_scratch(chip_tiles)
        + [block, weight, weight, weight, pltpu.SemaphoreType.DMA((4,)), pltpu.SemaphoreType.DMA((10,))],
        13 * unit,
        scalars=2,
        out_scalars=1,
    )
    x_forward = swap(after(x_near, norms))

    granule = 8 * dp * seq // 2
    grad_rows = (2 * hidden + 4 * width + 16 + granule - 1) // granule * granule
    vectors = [row(v) for v in (b_out, gain_one, shift_one, b_down, gain_two, shift_two)]
    layer, input_grad, p_near, p_far, p_forward, p_partner, keep, send = call(
        functools.partial(layer_kernel, nq),
        (meta, bounds, row(b_value), row(b_up), norms, qm, x_forward, *vectors),
        (
            w_key, w_value, x_near, x_far, qt, top, total, acc,
            w_out, tokens, w_up, w_down, cotangent, q, k_chip, v_chip, x_partner, w_query,
        ),
        (
            part, struct((shard, width), F32), part, part, part, part,
            struct((grad_rows // 2, width), BF16), struct((grad_rows // 2, width), BF16),
        ),
        [
            weight, weight, block, block, pltpu.VMEM((width, shard), BF16), stat, stat, wide,
            weight, block, pltpu.VMEM((width, hidden), BF16), pltpu.VMEM((hidden, width), BF16), block, block,
            pltpu.VMEM((chip_tiles * T, width), BF16), pltpu.VMEM((chip_tiles * T, width), BF16), block, weight,
            pltpu.SemaphoreType.DMA((18,)), pltpu.SemaphoreType.DMA((8,)),
            pltpu.VMEM((grad_rows, width), BF16), pltpu.VMEM((shard, width), F32),
            pltpu.VMEM((far_tiles * T, width), BF16), pltpu.VMEM((far_tiles * T, width), BF16),
        ]
        + keys_scratch(far_tiles)
        + [stat, stat, pltpu.VMEM((8, width), F32)]
        + [block, block, pltpu.VMEM((width, shard), BF16)]
        + [pltpu.VMEM((hidden, width), F32), pltpu.VMEM((width, hidden), F32), square]
        + [pltpu.VMEM((8, width), F32)]
        + [
            pltpu.VMEM((width, T), BF16), pltpu.VMEM((T, LANES), BF16),
            pltpu.VMEM((T, width), F32), pltpu.VMEM((T, width), F32),
        ],
        60 * unit,
    )
    summing = Summing(dp, seq)
    p_forward = swap(p_forward)
    grads = keep + summing.exchange(send)
    p_far = far(after(p_far, grads), back=True)
    p_partner = swap(after(p_partner, grads))
    p_near = p_near + p_forward
    unit = 8 << (len(summing.order) - 1)
    lead = (grad_rows // 2 // unit + 1) // 2 * unit
    one, two = grads[:lead], grads[lead:]
    dp_steps = summing.dp_steps
    steps = list(range(len(summing.order) - 1))
    others = {0: p_near, 1: p_partner, dp_steps: p_far}
    for number in steps:
        one = summing.halve(one, number, others.get(number))
        if number == 0:
            two = after(two, one)
    for number in steps:
        two = summing.halve(two, number)
    one, two = summing.whole(one), summing.whole(two)
    for number in steps[dp_steps:][::-1]:
        one, two = summing.double(one, number), summing.double(two, number)
    p_near = near(after(p_near, two))
    for number in steps[:dp_steps][::-1]:
        one = summing.double(one, number)
        two = summing.double(two, number, p_near if number == 0 else None)
    mine = (one, two)
    other = tuple(summing.exchange(rows) for rows in mine)
    input_grad = input_grad + p_partner.astype(F32) + p_far.astype(F32) + p_near.astype(F32)
    bias_rows = [(0,), (1,)] + [(n,) for n in range(8, 14)] + [tuple(range(14, 14 + hidden // width))]
    shapes = [(hidden, width), (width, hidden)] + [(width, width)] * 4
    shapes += [(1, len(rows) * width) for rows in bias_rows]
    wide_grads = call(
        functools.partial(widen_kernel, bias_rows),
        (core.reshape(1).astype(jnp.int32), *mine, *other),
        (),
        [struct(shape, F32) for shape in shapes],
        [pltpu.VMEM(shape, F32) for shape in shapes] + [pltpu.SemaphoreType.DMA((len(shapes),))],
        0,
        limit=20 << 20,
    )
    g_w_down, g_w_up, g_w_out, g_w_query, g_w_key, g_w_value = wide_grads[:6]
    g_b_value, g_b_query, g_b_out, g_gain_one, g_shift_one, g_b_down, g_gain_two, g_shift_two, g_b_up = (
        v.reshape(-1) for v in wide_grads[6:]
    )
    return (
        layer, input_grad, g_w_query, g_b_query, g_w_key, g_w_value, g_b_value, g_w_out, g_b_out,
        g_gain_one, g_shift_one, g_w_up, g_b_up, g_w_down, g_b_down, g_gain_two, g_shift_two,
    )


def solution(mesh):
    rows = P(("dp", "seq"), None)
    return jax.shard_map(
        shards,
        mesh=mesh,
        in_specs=(rows, P("dp", None)) + (P(),) * 15 + (rows,),
        out_specs=(rows, rows) + (P(),) * 15,
        check_vma=False,
    )
```

```python
import functools
import math

import jax
import jax.numpy as jnp
from jax import lax
from jax.experimental import pallas as pl
from jax.experimental.pallas import tpu as pltpu
from jax.sharding import PartitionSpec as P

H = 4
HD = 128
EPS = 1e-05
BIG = 1e30
T = 256
LANES = 128
SCALE = 1.0 / math.sqrt(HD)
LOG2E = 1.0 / math.log(2.0)
LN2 = math.log(2.0)
F32 = jnp.float32
BF16 = jnp.bfloat16

NN = (((1,), (0,)), ((), ()))
NT = (((1,), (1,)), ((), ()))
TN = (((0,), (0,)), ((), ()))


def dot(left, right, dims=NN):
    return lax.dot_general(left, right, dims, preferred_element_type=F32)


def head(h):
    return slice(h * HD, (h + 1) * HD)


def query_mask(starts, ends, start):
    place = start + lax.broadcasted_iota(jnp.int32, (LANES, T), 1)
    inside = jnp.logical_and(place >= starts, place < ends)
    return jnp.where(inside, 1.0, 0.0).astype(BF16)


def key_mask(brow_ref, start):
    place = start + lax.broadcasted_iota(jnp.int32, (T, LANES), 0)
    inside = jnp.logical_and(place >= brow_ref[0:1, :], place < brow_ref[1:2, :])
    return jnp.where(inside, 0.0, -BIG).astype(BF16)


def tile_range(lo, hi, start, tiles):
    first = jnp.clip((lo - start) // T, 0, tiles)
    last = jnp.clip((hi - start + T - 1) // T, 0, tiles)
    return first, last


class Meta:
    def __init__(self, ref, nq):
        self.ref, self.nq = ref, nq
        self.chip, self.side, self.forward, self.own_tile, self.near_tile = (ref[2 * nq + j] for j in range(5))
        self.partner_tile = nq - self.own_tile
        self.far_tile = nq - self.near_tile
        self.own = self.chip + self.own_tile * T

    def lo(self, i):
        return self.ref[i]

    def hi(self, i):
        return self.ref[self.nq + i]

    @property
    def all_keys(self):
        return self.ref[0], self.ref[2 * self.nq - 1]


def survey(nq, seq, counts_ref, position_ref, meta_ref, brow_ref):
    position = position_ref[0]
    shard = nq * T
    sizes = [counts_ref[0, j] for j in range(counts_ref.shape[1])]
    starts, ends, end = [], [], 0
    for size in sizes:
        starts.append(end + 0 * size)
        end = end + size
        ends.append(end)
    for i in range(nq):
        first = position * shard + i * T
        lo, hi = 0, seq * shard
        for a, b in zip(starts[::-1], ends[::-1]):
            lo = jnp.maximum(lo, jnp.where(a <= first, a, 0))
            hi = jnp.minimum(hi, jnp.where(b > first + (T - 1), b, seq * shard))
        meta_ref[i] = lo
        meta_ref[nq + i] = hi
    core = position % 2
    side = position + jnp.where(core == 0, -2, 1)
    forward = position + jnp.where(core == 0, 2, -2)
    meta_ref[2 * nq] = (position - core) * shard
    meta_ref[2 * nq + 1] = jnp.where(jnp.logical_and(side >= 0, side + 1 < seq), side * shard, 1 << 28)
    meta_ref[2 * nq + 2] = jnp.where(jnp.logical_and(forward >= 0, forward < seq), forward * shard, 1 << 28)
    meta_ref[2 * nq + 3] = core * nq
    meta_ref[2 * nq + 4] = (1 - core) * nq

    def spread(values, shape, dimension):
        at = lax.broadcasted_iota(jnp.int32, shape, dimension)
        out = jnp.zeros(shape, jnp.int32)
        for j, value in enumerate(values):
            out = jnp.where(at == j, value, out)
        return out

    brow_ref[0:1, :] = spread(starts, (1, LANES), 1)
    brow_ref[1:2, :] = spread(ends, (1, LANES), 1)
    brow_ref[2:8, :] = jnp.zeros((6, LANES), jnp.int32)
    return spread(starts, (LANES, 1), 0), spread(ends, (LANES, 1), 0)


LIMIT_SQUARED = 9000.0


def head_pick(width):
    shape = (width, LANES)
    same = lax.broadcasted_iota(jnp.int32, shape, 0) // HD == lax.broadcasted_iota(jnp.int32, shape, 1)
    return jnp.where(same, 1.0, 0.0).astype(BF16)


def keep_norms(norm_ref, rows):
    squares = dot((rows * rows).astype(BF16), head_pick(rows.shape[1]))
    norm_ref[0:1, :] = jnp.maximum(norm_ref[0:1, :], jnp.max(squares, axis=0, keepdims=True))


def attend(meta, segments, qt_ref, k_ref, vt_ref, km_ref, qm_ref, acc_ref, top_ref, total_ref, safe, finish):
    nq = meta.nq

    def query_tile(i, carry):
        q0 = pl.multiple_of(i * T, T)
        qs = pl.ds(q0, T)

        def scores(h, k0):
            ks = pl.ds(k0, 2 * T)
            kx = jnp.concatenate([k_ref[ks, head(h)], km_ref[ks, :]], axis=1)
            qx = jnp.concatenate([qt_ref[head(h), qs], qm_ref[i]], axis=0)
            return dot(kx, qx)

        def weigh(h, k0, p):
            values = jnp.concatenate([vt_ref[head(h), pl.ds(k0, 2 * T)], jnp.ones((16, 2 * T), BF16)], axis=0)
            return dot(values, p)

        def plain(k0):
            ps = [jnp.exp2(scores(h, k0)).astype(BF16) for h in range(H)]
            sums = [weigh(h, k0, ps[h]) for h in range(H)]
            acc_ref[:, qs] += jnp.concatenate([out[0:HD] for out in sums], axis=0)
            for h in range(H):
                total_ref[h : h + 1, qs] += sums[h][HD : HD + 1]

        def guarded(k0):
            for h in range(H):
                s = scores(h, k0)
                old = top_ref[h : h + 1, qs]
                top = jnp.maximum(old, jnp.max(s, axis=0, keepdims=True))
                decay = jnp.exp2(old - top)
                out = weigh(h, k0, jnp.exp2(s - top).astype(BF16))
                acc_ref[head(h), qs] = acc_ref[head(h), qs] * decay + out[0:HD]
                total_ref[h : h + 1, qs] = total_ref[h : h + 1, qs] * decay + out[HD : HD + 1]
                top_ref[h : h + 1, qs] = top

        def walk(body):
            for start, tile, tiles in segments:
                first, last = tile_range(meta.lo(i), meta.hi(i), start, tiles)

                def step(j, inner):
                    body(pl.multiple_of((tile + first + 2 * j) * T, T))
                    return inner

                lax.fori_loop(0, (last - first + 1) // 2, step, 0)

        @pl.when(safe)
        def _():
            walk(plain)

        @pl.when(jnp.logical_not(safe))
        def _():
            walk(guarded)

        finish(q0)
        return carry

    lax.fori_loop(0, nq, query_tile, 0)


def project_keys(meta, brow_ref, start, tile, x_ref, wk_ref, wv_ref, bv_ref, k_ref, v_ref, vt_ref, km_ref, norm_ref):
    lo, hi = meta.all_keys
    first, last = tile_range(lo, hi + T, start, meta.nq)

    def step(t, carry):
        r0 = pl.multiple_of(t * T, T)
        ks = pl.ds(pl.multiple_of((tile + t) * T, T), T)
        x = x_ref[pl.ds(r0, T), :]
        k = dot(x, wk_ref[...])
        v = (dot(x, wv_ref[...]) + bv_ref[...]).astype(BF16)
        k_ref[ks, :] = k.astype(BF16)
        v_ref[ks, :] = v
        vt_ref[:, ks] = v.T
        km_ref[ks, :] = key_mask(brow_ref, start + r0)
        keep_norms(norm_ref, k)
        return carry

    lax.fori_loop(first, last, step, 0)


def blank_tile(tile, k_ref, vt_ref, km_ref):
    ks = slice(tile * T, (tile + 1) * T)
    k_ref[ks, :] = jnp.zeros((T, k_ref.shape[1]), BF16)
    vt_ref[:, ks] = jnp.zeros((vt_ref.shape[0], T), BF16)
    km_ref[ks, :] = jnp.full((T, LANES), -BIG, BF16)


def bounded(query_norms, key_norms):
    return jnp.max(query_norms * key_norms) <= LIMIT_SQUARED


def copies_of(sources, targets, sems):
    return [pltpu.make_async_copy(src, dst, sems.at[n]) for n, (src, dst) in enumerate(zip(sources, targets))]


def start(copies):
    for copy in copies:
        copy.start()


def wait(copies):
    for copy in copies:
        copy.wait()


def attend_chip_kernel(
    nq, seq,
    counts_ref, position_ref, bq_ref, bv_ref, xp_ref, *refs,
):
    sources, meta_ref, outs, held, refs = refs[:4], refs[4], refs[5:15], refs[15:25], refs[25:]
    q_ref, qt_ref, k_ref, v_ref, top_ref, total_ref, acc_ref, norm_ref, qm_ref, brow_ref = held
    vt_ref, km_ref, kn_ref, x_ref, wq_ref, wk_ref, wv_ref, sems, out_sems = refs
    loads = copies_of(sources, (x_ref, wq_ref, wk_ref, wv_ref), sems)
    stores = copies_of(held, outs, out_sems)
    start(loads[:2])
    starts, ends = survey(nq, seq, counts_ref, position_ref, meta_ref, brow_ref)
    meta = Meta(meta_ref, nq)
    wait(loads[:2])
    start(loads[2:])
    norm_ref[...] = jnp.zeros_like(norm_ref)
    kn_ref[...] = jnp.zeros_like(kn_ref)

    def make_query(i, carry):
        q0 = pl.multiple_of(i * T, T)
        q = (dot(x_ref[pl.ds(q0, T), :], wq_ref[...]) + bq_ref[...]) * (SCALE * LOG2E)
        low = q.astype(BF16)
        q_ref[pl.ds(q0, T), :] = low
        qt_ref[:, pl.ds(q0, T)] = low.T
        qm_ref[i] = query_mask(starts, ends, meta.own + q0)
        keep_norms(norm_ref, q)
        return carry

    lax.fori_loop(0, nq, make_query, 0)
    start(stores[:2] + stores[8:])
    wait(loads[2:])
    for rows, tile in ((x_ref, meta.own_tile), (xp_ref, meta.partner_tile)):
        project_keys(
            meta, brow_ref, meta.chip + tile * T, tile, rows, wk_ref, wv_ref, bv_ref,
            k_ref, v_ref, vt_ref, km_ref, kn_ref,
        )
    blank_tile(2 * nq, k_ref, vt_ref, km_ref)
    start(stores[2:4])
    acc_ref[...] = jnp.zeros_like(acc_ref)
    total_ref[...] = jnp.zeros_like(total_ref)
    safe = bounded(norm_ref[0:1, :], kn_ref[0:1, :])
    norm_ref[1:2, :] = jnp.full((1, LANES), jnp.where(safe, 1.0, 0.0), F32)
    top_ref[...] = jnp.full(top_ref.shape, jnp.where(safe, 0.0, -BIG), F32)
    attend(
        meta, [(meta.chip, 0, 2 * nq)], qt_ref, k_ref, vt_ref, km_ref, qm_ref, acc_ref, top_ref, total_ref, safe,
        lambda q0: None,
    )
    start(stores[4:8])
    wait(stores)


def attend_far(meta, brow_ref, blocks, queries, others, wk_ref, wv_ref, bv_ref, qt_ref, norm_ref, qm_ref,
               k_ref, v_ref, att_ref, attt_ref, lse_ref, vt_ref, km_ref, kn_ref, top_ref, total_ref):
    nq = meta.nq
    kn_ref[...] = jnp.zeros_like(kn_ref)
    for copies, rows, first_row, tile in blocks:
        wait(copies)
        project_keys(
            meta, brow_ref, first_row, tile, rows, wk_ref, wv_ref, bv_ref, k_ref, v_ref, vt_ref, km_ref, kn_ref
        )
    blank_tile(2 * nq, k_ref, vt_ref, km_ref)
    blank_tile(3 * nq + 1, k_ref, vt_ref, km_ref)
    wait(queries)
    start(others)

    def finish(q0):
        qs = pl.ds(q0, T)
        for h in range(H):
            total = total_ref[h : h + 1, qs]
            lse_ref[h : h + 1, qs] = top_ref[h : h + 1, qs] + jnp.log2(total)
            att = attt_ref[head(h), qs] / total
            attt_ref[head(h), qs] = att
            att_ref[qs, head(h)] = att.T.astype(BF16)

    safe = jnp.logical_and(bounded(norm_ref[0:1, :], kn_ref[0:1, :]), jnp.max(norm_ref[1:2, :]) > 0.5)
    attend(
        meta, [(meta.side, 0, 2 * nq), (meta.forward, 2 * nq + 1, nq)], qt_ref, k_ref, vt_ref, km_ref, qm_ref,
        attt_ref, top_ref, total_ref, safe, finish,
    )


def column_sum(rows):
    return jnp.sum(rows, axis=0, keepdims=True)


def mean(rows):
    return jnp.mean(rows, axis=-1, keepdims=True)


def norm(rows):
    centre = rows - mean(rows)
    inverse = lax.rsqrt(mean(centre * centre) + EPS)
    return centre * inverse, inverse


def norm_back(grad, n, inverse):
    return inverse * (grad - mean(grad) - n * mean(grad * n))


def middle(
    nq, x_ref, cot_ref, att_ref, attt_ref, wo_ref, wu_ref, wd_ref, vectors, bup_ref,
    dfirst_ref, da_ref, dat_ref, delta_ref, small_ref, gd_ref, gu_ref, go_ref,
):
    width = x_ref.shape[1]
    hidden = wu_ref.shape[1]
    b_out, gain_one, shift_one, b_down, gain_two, shift_two = (ref[...] for ref in vectors)
    for ref in (gd_ref, gu_ref, go_ref, small_ref):
        ref[...] = jnp.zeros_like(ref)
    rows_of = lambda tiles: jnp.concatenate(tiles, axis=0)

    def row_tiles(i, carry):
        both = [pl.ds(pl.multiple_of((2 * i + n) * T, T), T) for n in range(2)]
        att = [att_ref[rs, :] for rs in both]
        branch = [dot(a, wo_ref[...]) for a in att]
        one = [norm(x_ref[rs, :].astype(F32) + b + b_out) for rs, b in zip(both, branch)]
        normed = [n * gain_one + shift_one for n, _ in one]
        normed_low = [n.astype(BF16) for n in normed]
        pre, act_low, slope = [], [], []
        for n in range(2):
            pre.append(dot(normed_low[n], wu_ref[...]) + bup_ref[...])
        for n in range(2):
            cdf = 0.5 * (1.0 + lax.erf(pre[n] * math.sqrt(0.5)))
            act_low.append((pre[n] * cdf).astype(BF16))
            slope.append(cdf + pre[n] * (jnp.exp(-0.5 * pre[n] * pre[n]) * (1.0 / math.sqrt(2.0 * math.pi))))
        down = [dot(act, wd_ref[...]) for act in act_low]
        two = [norm(n + d + b_down) for n, d in zip(normed, down)]
        cot = [cot_ref[rs, :].astype(F32) for rs in both]
        for rs, (n, _) in zip(both, two):
            cot_ref[rs, :] = (n * gain_two + shift_two).astype(BF16)
        d_sum = [norm_back(c * gain_two, n, inverse) for c, (n, inverse) in zip(cot, two)]
        d_ffn = [d.astype(BF16) for d in d_sum]
        d_act = [dot(d, wd_ref[...], NT) for d in d_ffn]
        gd_ref[...] += dot(rows_of(act_low), rows_of(d_ffn), TN)
        d_pre = [(d * s).astype(BF16) for d, s in zip(d_act, slope)]
        d_normed = [a + dot(d, wu_ref[...], NT) for a, d in zip(d_sum, d_pre)]
        gu_ref[...] += dot(rows_of(normed_low), rows_of(d_pre), TN)
        d_first = [norm_back(d * gain_one, n, inverse) for d, (n, inverse) in zip(d_normed, one)]
        d_branch = [d.astype(BF16) for d in d_first]
        d_att = [dot(d, wo_ref[...], NT).astype(BF16) for d in d_branch]
        go_ref[...] += dot(rows_of(att), rows_of(d_branch), TN)
        for rs, d, a in zip(both, d_first, d_att):
            dfirst_ref[rs, :] = d
            da_ref[rs, :] = a
            turned = a.T
            dat_ref[:, rs] = turned
            for h in range(H):
                delta_ref[h : h + 1, rs] = column_sum(turned[head(h), :].astype(F32) * attt_ref[head(h), rs])
        pair_sum = lambda rows: column_sum(rows[0].astype(F32) + rows[1].astype(F32))
        up = pair_sum(d_pre)
        sums = [
            pair_sum(d_branch),
            pair_sum([d * n for d, (n, _) in zip(d_normed, one)]),
            pair_sum(d_normed),
            pair_sum(d_ffn),
            pair_sum([c * n for c, (n, _) in zip(cot, two)]),
            pair_sum(cot),
        ]
        for at in range(0, hidden, width):
            sums.append(up[:, at : at + width])
        small_ref[...] += jnp.concatenate(sums, axis=0)
        return carry

    lax.fori_loop(0, nq // 2, row_tiles, 0)


def attend_back(
    meta, brow_ref, start, tile, k_ref, v_ref, q_ref, qt_ref, da_ref, dat_ref, lse_ref, delta_ref, qm_ref,
    kt_ref, km_ref, dk_ref, dv_ref, dq_ref,
):
    nq = meta.nq
    first, last = tile_range(*meta.all_keys, start, nq)

    def rows_at(t):
        return pl.ds(pl.multiple_of((tile + t) * T, T), T)

    def blank(t, carry):
        for ref in (k_ref, v_ref):
            ref[rows_at(t), :] = jnp.zeros((T, ref.shape[1]), BF16)
        return carry

    def key_tile(t, carry):
        ks = rows_at(t)
        row = start + t * T
        q_first = sum((meta.hi(i) <= row).astype(jnp.int32) for i in range(nq))
        q_last = sum((meta.lo(i) < row + T).astype(jnp.int32) for i in range(nq))
        km_ref[...] = key_mask(brow_ref, row)
        kt_ref[...] = k_ref[ks, :].T
        dk_ref[...] = jnp.zeros_like(dk_ref)
        dv_ref[...] = jnp.zeros_like(dv_ref)

        def query_tile(i, inner):
            qs = pl.ds(pl.multiple_of(i * T, T), T)
            ps, ds, sums = [], [], []

            def products(h):
                sums.append((dot(ps[h], da_ref[qs, head(h)]), dot(ds[h], q_ref[qs, head(h)]), dot(kt_ref[head(h), :], ds[h])))

            for h in range(H):
                kx = jnp.concatenate([k_ref[ks, head(h)], km_ref[...]], axis=1)
                qx = jnp.concatenate([qt_ref[head(h), qs], qm_ref[i]], axis=0)
                p = jnp.exp2(dot(kx, qx) - lse_ref[h : h + 1, qs])
                ps.append(p.astype(BF16))
                dp = dot(v_ref[ks, head(h)], dat_ref[head(h), qs])
                ds.append((p * (dp - delta_ref[h : h + 1, qs])).astype(BF16))
                if h >= 2:
                    products(h - 2)
            products(H - 2)
            products(H - 1)
            dv_ref[...] += jnp.concatenate([out[0] for out in sums], axis=1)
            dk_ref[...] += jnp.concatenate([out[1] for out in sums], axis=1)
            dq_ref[:, qs] += jnp.concatenate([out[2] for out in sums], axis=0)
            return inner

        lax.fori_loop(q_first, q_last, query_tile, 0)
        k_ref[ks, :] = (dk_ref[...] * LN2).astype(BF16)
        v_ref[ks, :] = dv_ref[...].astype(BF16)
        return carry

    lax.fori_loop(0, first, blank, 0)
    lax.fori_loop(first, last, key_tile, 0)
    lax.fori_loop(last, nq, blank, 0)


def layer_kernel(
    nq,
    meta_ref, brow_ref, bv_ref, bup_ref, norm_ref, qm_ref, xw_ref, *refs,
):
    vectors, refs = refs[:6], refs[6:]
    count = 18
    sources, refs = refs[:count], refs[count:]
    layer_out, ig_out, pn_out, pf_out, pw_out, pp_out, keep_out, send_out = refs[:8]
    refs = refs[8:]
    staged, refs = refs[:count], refs[count:]
    sems, out_sems, grads_ref, ig_ref, k_ref, v_ref, vt_ref, km_ref, kn_ref, lse_ref, delta_ref, small_ref = refs[:12]
    att_ref, da_ref, dat_ref, gd_ref, gu_ref, go_ref, sum_ref = refs[12:19]
    kt_ref, mask_ref, dk_ref, dv_ref = refs[19:]
    loads = copies_of(sources, staged, sems)
    start(loads[:4])
    wk_ref, wv_ref, xn_ref, xf_ref, qt_ref, top_ref, total_ref, attt_ref = staged[:8]
    wo_ref, x_ref, wu_ref, wd_ref, cot_ref, q_ref, kc_ref, vc_ref, xp_ref, wq_ref = staged[8:]
    stores = []

    def store(source, target):
        copy = pltpu.make_async_copy(source, target, out_sems.at[len(stores)])
        copy.start()
        stores.append(copy)

    meta = Meta(meta_ref, nq)
    near_start = meta.side + meta.near_tile * T
    far_start = meta.side + meta.far_tile * T
    wait(loads[:2])
    start(loads[4:8])
    attend_far(
        meta, brow_ref,
        (
            ([], xw_ref, meta.forward, 2 * nq + 1),
            (loads[2:3], xn_ref, near_start, meta.near_tile),
            (loads[3:4], xf_ref, far_start, meta.far_tile),
        ),
        loads[4:8],
        loads[8:],
        wk_ref, wv_ref, bv_ref, qt_ref, norm_ref, qm_ref,
        k_ref, v_ref, att_ref, attt_ref, lse_ref, vt_ref, km_ref, kn_ref, top_ref, total_ref,
    )
    wait(loads[8:13])
    middle(
        nq, x_ref, cot_ref, att_ref, attt_ref, wo_ref, wu_ref, wd_ref, vectors, bup_ref,
        ig_ref, da_ref, dat_ref, delta_ref, small_ref, gd_ref, gu_ref, go_ref,
    )
    store(cot_ref, layer_out)
    hidden, width = wd_ref.shape
    shard = x_ref.shape[0]
    grads_ref[0:hidden, :] = gd_ref[...].astype(BF16)
    for part in range(hidden // width):
        at = hidden + part * width
        grads_ref[at : at + width, :] = gu_ref[:, part * width : (part + 1) * width].astype(BF16)
    base = 2 * hidden + width
    grads_ref[base - width : base, :] = go_ref[...].astype(BF16)
    half = grads_ref.shape[0] // 2
    assert half <= base
    first_core = meta.own_tile == 0

    def store_half(source, stays):
        copies = [pltpu.make_async_copy(source, target, out_sems.at[len(stores)]) for target in (keep_out, send_out)]
        pl.when(stays)(copies[0].start)
        pl.when(jnp.logical_not(stays))(copies[1].start)
        stores.append(copies[0])

    store_half(grads_ref.at[0:half, :], first_core)

    wait(loads[13:])
    xt_ref = vt_ref.at[:, 0:shard]
    dq_ref = attt_ref
    dwk_ref = gd_ref.at[0:width, :]
    dwv_ref = gd_ref.at[width : 2 * width, :]
    wkv_ref = wd_ref
    wkv_ref[0:width, :] = wk_ref[...].T
    wkv_ref[width : 2 * width, :] = wv_ref[...].T
    wo_ref[...] = wq_ref[...].T
    for ref in (dq_ref, dwk_ref, dwv_ref, sum_ref):
        ref[...] = jnp.zeros_like(ref)
    for rows, part_ref, out, first_row, tile, keys_ref, values_ref in (
        (xn_ref, xn_ref, pn_out, near_start, meta.near_tile, k_ref, v_ref),
        (xf_ref, xf_ref, pf_out, far_start, meta.far_tile, k_ref, v_ref),
        (xw_ref, att_ref, pw_out, meta.forward, 2 * nq + 1, k_ref, v_ref),
        (xp_ref, xp_ref, pp_out, meta.chip + meta.partner_tile * T, meta.partner_tile, kc_ref, vc_ref),
        (x_ref, None, None, meta.own, meta.own_tile, kc_ref, vc_ref),
    ):
        first, last = tile_range(*meta.all_keys, first_row, nq)

        def work(rows=rows, part_ref=part_ref, out=out, first_row=first_row, tile=tile, keys_ref=keys_ref, values_ref=values_ref):
            attend_back(
                meta, brow_ref, first_row, tile, keys_ref, values_ref, q_ref, qt_ref, da_ref, dat_ref,
                lse_ref, delta_ref, qm_ref, kt_ref, mask_ref, dk_ref, dv_ref, dq_ref,
            )
            block = pl.ds(pl.multiple_of(tile * T, T), shard)
            xt_ref[...] = rows[...].T
            dwk_ref[...] += dot(xt_ref[...], keys_ref[block, :])
            dwv_ref[...] += dot(xt_ref[...], values_ref[block, :])
            sum_ref[0:1, :] += column_sum(values_ref[block, :].astype(F32))

            def input_tile(t, carry):
                rs = pl.ds(pl.multiple_of(2 * t * T, 2 * T), 2 * T)
                ks = pl.ds(pl.multiple_of((tile + 2 * t) * T, T), 2 * T)
                grad = dot(jnp.concatenate([keys_ref[ks, :], values_ref[ks, :]], axis=1), wkv_ref[...])
                if out is None:
                    ig_ref[rs, :] += grad
                else:
                    part_ref[rs, :] = grad.astype(BF16)
                return carry

            lax.fori_loop(0, nq // 2, input_tile, 0)

        if out is None:
            work()
        else:
            pl.when(first < last)(work)

            @pl.when(first >= last)
            def _(part_ref=part_ref):
                part_ref[...] = jnp.zeros_like(part_ref)

            store(part_ref, out)

    dwk_low = dwk_ref[...].astype(BF16)
    dwv_low = dwv_ref[...].astype(BF16)

    def query_tile(i, carry):
        qs = pl.ds(pl.multiple_of(i * T, T), T)
        dq = (dq_ref[:, qs] * SCALE).astype(BF16).T
        q_ref[qs, :] = dq
        sum_ref[1:2, :] += column_sum(dq.astype(F32))
        ig_ref[qs, :] += dot(dq, wo_ref[...])
        return carry

    lax.fori_loop(0, nq, query_tile, 0)
    store(ig_ref, ig_out)
    grads_ref[base : base + width, :] = dot(xt_ref[...], q_ref[...]).astype(BF16)
    grads_ref[base + width : base + 2 * width, :] = dwk_low
    grads_ref[base + 2 * width : base + 3 * width, :] = dwv_low
    end = base + 3 * width
    rows = jnp.concatenate([sum_ref[...], small_ref[...]], axis=0)
    grads_ref[end : end + 16, :] = rows.astype(BF16)
    grads_ref[end + 16 :, :] = jnp.zeros((grads_ref.shape[0] - end - 16, width), BF16)
    store_half(grads_ref.at[half:, :], jnp.logical_not(first_core))
    wait(stores)


def vmem(count):
    return [pl.BlockSpec(memory_space=pltpu.VMEM)] * count


VMEM_LIMIT = 60 << 20


def call(kernel, inputs, staged, outputs, scratch, flops, scalars=1, out_scalars=0, limit=VMEM_LIMIT):
    size = lambda arrays: sum(math.prod(a.shape) * jnp.dtype(a.dtype).itemsize for a in arrays)
    everything = tuple(inputs) + tuple(staged)
    smem = [pl.BlockSpec(memory_space=pltpu.SMEM)]
    hbm = [pl.BlockSpec(memory_space=pltpu.HBM)]
    return pl.pallas_call(
        kernel,
        out_shape=outputs,
        in_specs=smem * scalars + vmem(len(inputs) - scalars) + hbm * len(staged),
        out_specs=smem * out_scalars + hbm * (len(outputs) - out_scalars),
        scratch_shapes=scratch,
        compiler_params=pltpu.CompilerParams(vmem_limit_bytes=limit),
        cost_estimate=pl.CostEstimate(
            flops=flops, bytes_accessed=size(everything) + size(outputs), transcendentals=0
        ),
    )(*everything)


def struct(shape, dtype):
    return jax.ShapeDtypeStruct(shape, dtype)


def after(value, other):
    return lax.optimization_barrier((value, other))[0]


class Summing:
    def __init__(self, dp, seq):
        dp_masks = [seq * (1 << j) for j in range(dp.bit_length() - 1)]
        seq_masks = [1 << j for j in range(seq.bit_length() - 1)]
        self.order = [(dp_masks[j], dp_masks[(j + 1) % len(dp_masks)]) for j in range(len(dp_masks))]
        self.dp_steps = len(self.order)
        self.order += [(mask, mask) for mask in seq_masks[1:]]
        self.devices = dp * seq
        core = lax.axis_index("seq") % 2
        index = lax.axis_index("dp") * seq + lax.axis_index("seq")
        self.bits = [jnp.where(core == 0, index // even, index // odd) % 2 for even, odd in self.order]

    def exchange(self, rows, even=1, odd=1):
        pairs = [(i, i ^ (even if i % 2 == 0 else odd)) for i in range(self.devices)]
        return lax.ppermute(rows, ("dp", "seq"), pairs)

    def halve(self, rows, number, other=None):
        half = rows.shape[0] // 2
        bit = self.bits[number]
        mine = lax.dynamic_slice_in_dim(rows, bit * half, half, 0)
        got = self.exchange(lax.dynamic_slice_in_dim(rows, (1 - bit) * half, half, 0), *self.order[number])
        return (mine if other is None else after(mine, other)) + got

    def whole(self, rows):
        return rows + self.exchange(rows, *self.order[-1])

    def double(self, rows, number, other=None):
        got = self.exchange(rows, *self.order[number])
        half = rows.shape[0]
        if other is not None:
            rows = after(rows, other)
        both = jnp.zeros((2 * half, rows.shape[1]), rows.dtype)
        both = lax.dynamic_update_slice_in_dim(both, rows, self.bits[number] * half, 0)
        return lax.dynamic_update_slice_in_dim(both, got, (1 - self.bits[number]) * half, 0)


def widen_kernel(bias_rows, core_ref, mine_one, mine_two, other_one, other_two, *refs):
    count = 6 + len(bias_rows)
    outs, wide, sems = refs[:count], refs[count : 2 * count], refs[2 * count]
    width = mine_one.shape[1]
    hidden = wide[0].shape[0]
    spans = [(0, hidden, 0, 0)]
    spans += [(hidden + at, width, 1, at) for at in range(0, hidden, width)]
    spans += [(2 * hidden + n * width, width, 2 + n, 0) for n in range(4)]
    copies = copies_of(wide, outs, sems)

    def write(*sources):
        bases = [sum(ref.shape[0] for ref in sources[:n]) for n in range(4)]
        for first_row, rows, number, column in spans:
            for source, base in zip(sources, bases):
                first, last = max(first_row, base), min(first_row + rows, base + source.shape[0])
                if first < last:
                    wide[number][first - first_row : last - first_row, column : column + width] = source[
                        first - base : last - base, :
                    ].astype(F32)
            if column + width == wide[number].shape[1]:
                copies[number].start()
        at = 2 * hidden + 4 * width - bases[3]
        vectors = sources[3][at : at + 16, :].astype(F32)
        for number, rows in enumerate(bias_rows):
            for part, row in enumerate(rows):
                wide[6 + number][:, part * width : (part + 1) * width] = vectors[row : row + 1, :]
            copies[6 + number].start()

    @pl.when(core_ref[0] == 0)
    def _():
        write(mine_one, mine_two, other_one, other_two)

    @pl.when(core_ref[0] != 0)
    def _():
        write(other_one, other_two, mine_one, mine_two)

    wait(copies)


def shards(
    tokens, counts, w_query, b_query, w_key, w_value, b_value, w_out, b_out, gain_one, shift_one,
    w_up, b_up, w_down, b_down, gain_two, shift_two, cotangent,
):
    shard, width = tokens.shape
    hidden = w_up.shape[1]
    nq = shard // T
    seq = lax.axis_size("seq")
    dp = lax.axis_size("dp")
    position = lax.axis_index("seq")

    def swap(rows):
        return lax.ppermute(rows, "seq", [(i, i ^ 1) for i in range(seq)])

    def near(rows):
        pairs = [(i, i + 1) for i in range(1, seq - 1, 2)]
        return lax.ppermute(rows, "seq", pairs + [(b, a) for a, b in pairs])

    def far(rows, back=False):
        pairs = [(i, i + 2) for i in range(0, seq - 2, 2)] + [(i, i - 2) for i in range(3, seq, 2)]
        return lax.ppermute(rows, "seq", [(b, a) for a, b in pairs] if back else pairs)

    x_partner = swap(tokens)
    x_near = near(tokens)
    x_far = far(tokens)

    core = position % 2
    row = lambda v: v.reshape(1, -1)
    tile_mask = struct((nq, LANES, T), BF16)
    stats = struct((8, shard), F32)

    def keys_scratch(tiles):
        return [
            pltpu.VMEM((width, tiles * T), BF16), pltpu.VMEM((tiles * T, LANES), BF16), pltpu.VMEM((8, LANES), F32)
        ]

    unit = 2 * shard * width * width
    chip_tiles, far_tiles = 2 * nq + 1, 3 * nq + 2
    keys = lambda tiles: struct((tiles * T, width), BF16)
    block = pltpu.VMEM((shard, width), BF16)
    weight = pltpu.VMEM((width, width), BF16)
    wide = pltpu.VMEM((width, shard), F32)
    square = pltpu.VMEM((width, width), F32)
    stat = pltpu.VMEM((8, shard), F32)
    part = struct((shard, width), BF16)
    meta, q, qt, k_chip, v_chip, top, total, acc, norms, qm, bounds = call(
        functools.partial(attend_chip_kernel, nq, seq),
        (counts, position.reshape(1).astype(jnp.int32), row(b_query), row(b_value), x_partner),
        (tokens, w_query, w_key, w_value),
        (
            struct((2 * nq + 5,), jnp.int32),
            part, struct((width, shard), BF16), keys(chip_tiles), keys(chip_tiles), stats, stats,
            struct((width, shard), F32), struct((8, LANES), F32), tile_mask, struct((8, LANES), jnp.int32),
        ),
        [
            block, pltpu.VMEM((width, shard), BF16), pltpu.VMEM((chip_tiles * T, width), BF16),
            pltpu.VMEM((chip_tiles * T, width), BF16), stat, stat, wide, pltpu.VMEM((8, LANES), F32),
            pltpu.VMEM((nq, LANES, T), BF16), pltpu.VMEM((8, LANES), jnp.int32),
        ]
        + keys_scratch(chip_tiles)
        + [block, weight, weight, weight, pltpu.SemaphoreType.DMA((4,)), pltpu.SemaphoreType.DMA((10,))],
        13 * unit,
        scalars=2,
        out_scalars=1,
    )
    x_forward = swap(after(x_near, norms))

    granule = 8 * dp * seq // 2
    grad_rows = (2 * hidden + 4 * width + 16 + granule - 1) // granule * granule
    vectors = [row(v) for v in (b_out, gain_one, shift_one, b_down, gain_two, shift_two)]
    layer, input_grad, p_near, p_far, p_forward, p_partner, keep, send = call(
        functools.partial(layer_kernel, nq),
        (meta, bounds, row(b_value), row(b_up), norms, qm, x_forward, *vectors),
        (
            w_key, w_value, x_near, x_far, qt, top, total, acc,
            w_out, tokens, w_up, w_down, cotangent, q, k_chip, v_chip, x_partner, w_query,
        ),
        (
            part, struct((shard, width), F32), part, part, part, part,
            struct((grad_rows // 2, width), BF16), struct((grad_rows // 2, width), BF16),
        ),
        [
            weight, weight, block, block, pltpu.VMEM((width, shard), BF16), stat, stat, wide,
            weight, block, pltpu.VMEM((width, hidden), BF16), pltpu.VMEM((hidden, width), BF16), block, block,
            pltpu.VMEM((chip_tiles * T, width), BF16), pltpu.VMEM((chip_tiles * T, width), BF16), block, weight,
            pltpu.SemaphoreType.DMA((18,)), pltpu.SemaphoreType.DMA((8,)),
            pltpu.VMEM((grad_rows, width), BF16), pltpu.VMEM((shard, width), F32),
            pltpu.VMEM((far_tiles * T, width), BF16), pltpu.VMEM((far_tiles * T, width), BF16),
        ]
        + keys_scratch(far_tiles)
        + [stat, stat, pltpu.VMEM((8, width), F32)]
        + [block, block, pltpu.VMEM((width, shard), BF16)]
        + [pltpu.VMEM((hidden, width), F32), pltpu.VMEM((width, hidden), F32), square]
        + [pltpu.VMEM((8, width), F32)]
        + [
            pltpu.VMEM((width, T), BF16), pltpu.VMEM((T, LANES), BF16),
            pltpu.VMEM((T, width), F32), pltpu.VMEM((T, width), F32),
        ],
        60 * unit,
    )
    summing = Summing(dp, seq)
    p_forward = swap(p_forward)
    grads = keep + summing.exchange(send)
    p_far = far(after(p_far, grads), back=True)
    p_partner = swap(after(p_partner, grads))
    p_near = p_near + p_forward
    unit = 8 << (len(summing.order) - 1)
    lead = (grad_rows // 2 // unit + 1) // 2 * unit
    one, two = grads[:lead], grads[lead:]
    dp_steps = summing.dp_steps
    steps = list(range(len(summing.order) - 1))
    others = {0: p_near, dp_steps: p_far, dp_steps + 1: p_partner}
    for number in steps:
        one = summing.halve(one, number, others.get(number))
        if number == 0:
            two = after(two, one)
    for number in steps:
        two = summing.halve(two, number)
    one, two = summing.whole(one), summing.whole(two)
    for number in steps[dp_steps:][::-1]:
        one, two = summing.double(one, number), summing.double(two, number)
    p_near = near(after(p_near, two))
    for number in steps[:dp_steps][::-1]:
        one = summing.double(one, number)
        two = summing.double(two, number, p_near if number == 0 else None)
    mine = (one, two)
    other = tuple(summing.exchange(rows) for rows in mine)
    input_grad = input_grad + p_partner.astype(F32) + p_far.astype(F32) + p_near.astype(F32)
    bias_rows = [(0,), (1,)] + [(n,) for n in range(8, 14)] + [tuple(range(14, 14 + hidden // width))]
    shapes = [(hidden, width), (width, hidden)] + [(width, width)] * 4
    shapes += [(1, len(rows) * width) for rows in bias_rows]
    wide_grads = call(
        functools.partial(widen_kernel, bias_rows),
        (core.reshape(1).astype(jnp.int32), *mine, *other),
        (),
        [struct(shape, F32) for shape in shapes],
        [pltpu.VMEM(shape, F32) for shape in shapes] + [pltpu.SemaphoreType.DMA((len(shapes),))],
        0,
        limit=20 << 20,
    )
    g_w_down, g_w_up, g_w_out, g_w_query, g_w_key, g_w_value = wide_grads[:6]
    g_b_value, g_b_query, g_b_out, g_gain_one, g_shift_one, g_b_down, g_gain_two, g_shift_two, g_b_up = (
        v.reshape(-1) for v in wide_grads[6:]
    )
    return (
        layer, input_grad, g_w_query, g_b_query, g_w_key, g_w_value, g_b_value, g_w_out, g_b_out,
        g_gain_one, g_shift_one, g_w_up, g_b_up, g_w_down, g_b_down, g_gain_two, g_shift_two,
    )


def solution(mesh):
    rows = P(("dp", "seq"), None)
    return jax.shard_map(
        shards,
        mesh=mesh,
        in_specs=(rows, P("dp", None)) + (P(),) * 15 + (rows,),
        out_specs=(rows, rows) + (P(),) * 15,
        check_vma=False,
    )
```

```python
import functools
import math

import jax
import jax.numpy as jnp
from jax import lax
from jax.experimental import pallas as pl
from jax.experimental.pallas import tpu as pltpu
from jax.sharding import PartitionSpec as P

H = 4
HD = 128
EPS = 1e-05
BIG = 1e30
T = 256
LANES = 128
SCALE = 1.0 / math.sqrt(HD)
LOG2E = 1.0 / math.log(2.0)
LN2 = math.log(2.0)
F32 = jnp.float32
BF16 = jnp.bfloat16

NN = (((1,), (0,)), ((), ()))
NT = (((1,), (1,)), ((), ()))
TN = (((0,), (0,)), ((), ()))


def dot(left, right, dims=NN):
    return lax.dot_general(left, right, dims, preferred_element_type=F32)


def head(h):
    return slice(h * HD, (h + 1) * HD)


def query_mask(starts, ends, start):
    place = start + lax.broadcasted_iota(jnp.int32, (LANES, T), 1)
    inside = jnp.logical_and(place >= starts, place < ends)
    return jnp.where(inside, 1.0, 0.0).astype(BF16)


def key_mask(brow_ref, start):
    place = start + lax.broadcasted_iota(jnp.int32, (T, LANES), 0)
    inside = jnp.logical_and(place >= brow_ref[0:1, :], place < brow_ref[1:2, :])
    return jnp.where(inside, 0.0, -BIG).astype(BF16)


def tile_range(lo, hi, start, tiles):
    first = jnp.clip((lo - start) // T, 0, tiles)
    last = jnp.clip((hi - start + T - 1) // T, 0, tiles)
    return first, last


class Meta:
    def __init__(self, ref, nq):
        self.ref, self.nq = ref, nq
        self.chip, self.side, self.forward, self.own_tile, self.near_tile = (ref[2 * nq + j] for j in range(5))
        self.partner_tile = nq - self.own_tile
        self.far_tile = nq - self.near_tile
        self.own = self.chip + self.own_tile * T

    def lo(self, i):
        return self.ref[i]

    def hi(self, i):
        return self.ref[self.nq + i]

    @property
    def all_keys(self):
        return self.ref[0], self.ref[2 * self.nq - 1]


def survey(nq, seq, counts_ref, position_ref, meta_ref, brow_ref):
    position = position_ref[0]
    shard = nq * T
    sizes = [counts_ref[0, j] for j in range(counts_ref.shape[1])]
    starts, ends, end = [], [], 0
    for size in sizes:
        starts.append(end + 0 * size)
        end = end + size
        ends.append(end)
    for i in range(nq):
        first = position * shard + i * T
        lo, hi = 0, seq * shard
        for a, b in zip(starts[::-1], ends[::-1]):
            lo = jnp.maximum(lo, jnp.where(a <= first, a, 0))
            hi = jnp.minimum(hi, jnp.where(b > first + (T - 1), b, seq * shard))
        meta_ref[i] = lo
        meta_ref[nq + i] = hi
    core = position % 2
    side = position + jnp.where(core == 0, -2, 1)
    forward = position + jnp.where(core == 0, 2, -2)
    meta_ref[2 * nq] = (position - core) * shard
    meta_ref[2 * nq + 1] = jnp.where(jnp.logical_and(side >= 0, side + 1 < seq), side * shard, 1 << 28)
    meta_ref[2 * nq + 2] = jnp.where(jnp.logical_and(forward >= 0, forward < seq), forward * shard, 1 << 28)
    meta_ref[2 * nq + 3] = core * nq
    meta_ref[2 * nq + 4] = (1 - core) * nq

    def spread(values, shape, dimension):
        at = lax.broadcasted_iota(jnp.int32, shape, dimension)
        out = jnp.zeros(shape, jnp.int32)
        for j, value in enumerate(values):
            out = jnp.where(at == j, value, out)
        return out

    brow_ref[0:1, :] = spread(starts, (1, LANES), 1)
    brow_ref[1:2, :] = spread(ends, (1, LANES), 1)
    brow_ref[2:8, :] = jnp.zeros((6, LANES), jnp.int32)
    return spread(starts, (LANES, 1), 0), spread(ends, (LANES, 1), 0)


LIMIT_SQUARED = 9000.0


def head_pick(width):
    shape = (width, LANES)
    same = lax.broadcasted_iota(jnp.int32, shape, 0) // HD == lax.broadcasted_iota(jnp.int32, shape, 1)
    return jnp.where(same, 1.0, 0.0).astype(BF16)


def keep_norms(norm_ref, rows):
    squares = dot((rows * rows).astype(BF16), head_pick(rows.shape[1]))
    norm_ref[0:1, :] = jnp.maximum(norm_ref[0:1, :], jnp.max(squares, axis=0, keepdims=True))


def attend(meta, segments, qt_ref, k_ref, vt_ref, km_ref, qm_ref, acc_ref, top_ref, total_ref, safe, finish):
    nq = meta.nq

    def query_tile(i, carry):
        q0 = pl.multiple_of(i * T, T)
        qs = pl.ds(q0, T)

        def scores(h, k0):
            ks = pl.ds(k0, 2 * T)
            kx = jnp.concatenate([k_ref[ks, head(h)], km_ref[ks, :]], axis=1)
            qx = jnp.concatenate([qt_ref[head(h), qs], qm_ref[i]], axis=0)
            return dot(kx, qx)

        def weigh(h, k0, p):
            values = jnp.concatenate([vt_ref[head(h), pl.ds(k0, 2 * T)], jnp.ones((16, 2 * T), BF16)], axis=0)
            return dot(values, p)

        def plain(k0):
            ps = [jnp.exp2(scores(h, k0)).astype(BF16) for h in range(H)]
            sums = [weigh(h, k0, ps[h]) for h in range(H)]
            acc_ref[:, qs] += jnp.concatenate([out[0:HD] for out in sums], axis=0)
            for h in range(H):
                total_ref[h : h + 1, qs] += sums[h][HD : HD + 1]

        def guarded(k0):
            for h in range(H):
                s = scores(h, k0)
                old = top_ref[h : h + 1, qs]
                top = jnp.maximum(old, jnp.max(s, axis=0, keepdims=True))
                decay = jnp.exp2(old - top)
                out = weigh(h, k0, jnp.exp2(s - top).astype(BF16))
                acc_ref[head(h), qs] = acc_ref[head(h), qs] * decay + out[0:HD]
                total_ref[h : h + 1, qs] = total_ref[h : h + 1, qs] * decay + out[HD : HD + 1]
                top_ref[h : h + 1, qs] = top

        def walk(body):
            for start, tile, tiles in segments:
                first, last = tile_range(meta.lo(i), meta.hi(i), start, tiles)

                def step(j, inner):
                    body(pl.multiple_of((tile + first + 2 * j) * T, T))
                    return inner

                lax.fori_loop(0, (last - first + 1) // 2, step, 0)

        @pl.when(safe)
        def _():
            walk(plain)

        @pl.when(jnp.logical_not(safe))
        def _():
            walk(guarded)

        finish(q0)
        return carry

    lax.fori_loop(0, nq, query_tile, 0)


def project_keys(meta, brow_ref, start, tile, x_ref, wk_ref, wv_ref, bv_ref, k_ref, v_ref, vt_ref, km_ref, norm_ref):
    lo, hi = meta.all_keys
    first, last = tile_range(lo, hi + T, start, meta.nq)

    def step(t, carry):
        r0 = pl.multiple_of(t * T, T)
        ks = pl.ds(pl.multiple_of((tile + t) * T, T), T)
        x = x_ref[pl.ds(r0, T), :]
        k = dot(x, wk_ref[...])
        v = (dot(x, wv_ref[...]) + bv_ref[...]).astype(BF16)
        k_ref[ks, :] = k.astype(BF16)
        v_ref[ks, :] = v
        vt_ref[:, ks] = v.T
        km_ref[ks, :] = key_mask(brow_ref, start + r0)
        keep_norms(norm_ref, k)
        return carry

    lax.fori_loop(first, last, step, 0)


def blank_tile(tile, k_ref, vt_ref, km_ref):
    ks = slice(tile * T, (tile + 1) * T)
    k_ref[ks, :] = jnp.zeros((T, k_ref.shape[1]), BF16)
    vt_ref[:, ks] = jnp.zeros((vt_ref.shape[0], T), BF16)
    km_ref[ks, :] = jnp.full((T, LANES), -BIG, BF16)


def bounded(query_norms, key_norms):
    return jnp.max(query_norms * key_norms) <= LIMIT_SQUARED


def copies_of(sources, targets, sems):
    return [pltpu.make_async_copy(src, dst, sems.at[n]) for n, (src, dst) in enumerate(zip(sources, targets))]


def start(copies):
    for copy in copies:
        copy.start()


def wait(copies):
    for copy in copies:
        copy.wait()


def attend_chip_kernel(
    nq, seq,
    counts_ref, position_ref, bq_ref, bv_ref, xp_ref, *refs,
):
    sources, meta_ref, outs, held, refs = refs[:4], refs[4], refs[5:15], refs[15:25], refs[25:]
    q_ref, qt_ref, k_ref, v_ref, top_ref, total_ref, acc_ref, norm_ref, qm_ref, brow_ref = held
    vt_ref, km_ref, kn_ref, x_ref, wq_ref, wk_ref, wv_ref, sems, out_sems = refs
    loads = copies_of(sources, (x_ref, wq_ref, wk_ref, wv_ref), sems)
    stores = copies_of(held, outs, out_sems)
    start(loads[:2])
    starts, ends = survey(nq, seq, counts_ref, position_ref, meta_ref, brow_ref)
    meta = Meta(meta_ref, nq)
    wait(loads[:2])
    start(loads[2:])
    norm_ref[...] = jnp.zeros_like(norm_ref)
    kn_ref[...] = jnp.zeros_like(kn_ref)

    def make_query(i, carry):
        q0 = pl.multiple_of(i * T, T)
        q = (dot(x_ref[pl.ds(q0, T), :], wq_ref[...]) + bq_ref[...]) * (SCALE * LOG2E)
        low = q.astype(BF16)
        q_ref[pl.ds(q0, T), :] = low
        qt_ref[:, pl.ds(q0, T)] = low.T
        qm_ref[i] = query_mask(starts, ends, meta.own + q0)
        keep_norms(norm_ref, q)
        return carry

    lax.fori_loop(0, nq, make_query, 0)
    start(stores[:2] + stores[8:])
    wait(loads[2:])
    for rows, tile in ((x_ref, meta.own_tile), (xp_ref, meta.partner_tile)):
        project_keys(
            meta, brow_ref, meta.chip + tile * T, tile, rows, wk_ref, wv_ref, bv_ref,
            k_ref, v_ref, vt_ref, km_ref, kn_ref,
        )
    blank_tile(2 * nq, k_ref, vt_ref, km_ref)
    start(stores[2:4])
    acc_ref[...] = jnp.zeros_like(acc_ref)
    total_ref[...] = jnp.zeros_like(total_ref)
    safe = bounded(norm_ref[0:1, :], kn_ref[0:1, :])
    norm_ref[1:2, :] = jnp.full((1, LANES), jnp.where(safe, 1.0, 0.0), F32)
    top_ref[...] = jnp.full(top_ref.shape, jnp.where(safe, 0.0, -BIG), F32)
    attend(
        meta, [(meta.chip, 0, 2 * nq)], qt_ref, k_ref, vt_ref, km_ref, qm_ref, acc_ref, top_ref, total_ref, safe,
        lambda q0: None,
    )
    start(stores[4:8])
    wait(stores)


def attend_far(meta, brow_ref, blocks, queries, others, wk_ref, wv_ref, bv_ref, qt_ref, norm_ref, qm_ref,
               k_ref, v_ref, att_ref, attt_ref, lse_ref, vt_ref, km_ref, kn_ref, top_ref, total_ref):
    nq = meta.nq
    kn_ref[...] = jnp.zeros_like(kn_ref)
    for copies, rows, first_row, tile in blocks:
        wait(copies)
        project_keys(
            meta, brow_ref, first_row, tile, rows, wk_ref, wv_ref, bv_ref, k_ref, v_ref, vt_ref, km_ref, kn_ref
        )
    blank_tile(2 * nq, k_ref, vt_ref, km_ref)
    blank_tile(3 * nq + 1, k_ref, vt_ref, km_ref)
    wait(queries)
    start(others)

    def finish(q0):
        qs = pl.ds(q0, T)
        for h in range(H):
            total = total_ref[h : h + 1, qs]
            lse_ref[h : h + 1, qs] = top_ref[h : h + 1, qs] + jnp.log2(total)
            att = attt_ref[head(h), qs] / total
            attt_ref[head(h), qs] = att
            att_ref[qs, head(h)] = att.T.astype(BF16)

    safe = jnp.logical_and(bounded(norm_ref[0:1, :], kn_ref[0:1, :]), jnp.max(norm_ref[1:2, :]) > 0.5)
    attend(
        meta, [(meta.side, 0, 2 * nq), (meta.forward, 2 * nq + 1, nq)], qt_ref, k_ref, vt_ref, km_ref, qm_ref,
        attt_ref, top_ref, total_ref, safe, finish,
    )


def column_sum(rows):
    return jnp.sum(rows, axis=0, keepdims=True)


def mean(rows):
    return jnp.mean(rows, axis=-1, keepdims=True)


def norm(rows):
    centre = rows - mean(rows)
    inverse = lax.rsqrt(mean(centre * centre) + EPS)
    return centre * inverse, inverse


def norm_back(grad, n, inverse):
    return inverse * (grad - mean(grad) - n * mean(grad * n))


def middle(
    nq, x_ref, cot_ref, att_ref, attt_ref, wo_ref, wu_ref, wd_ref, vectors, bup_ref,
    dfirst_ref, da_ref, dat_ref, delta_ref, small_ref, gd_ref, gu_ref, go_ref,
):
    width = x_ref.shape[1]
    hidden = wu_ref.shape[1]
    b_out, gain_one, shift_one, b_down, gain_two, shift_two = (ref[...] for ref in vectors)
    for ref in (gd_ref, gu_ref, go_ref, small_ref):
        ref[...] = jnp.zeros_like(ref)
    rows_of = lambda tiles: jnp.concatenate(tiles, axis=0)

    def row_tiles(i, carry):
        both = [pl.ds(pl.multiple_of((2 * i + n) * T, T), T) for n in range(2)]
        att = [att_ref[rs, :] for rs in both]
        branch = [dot(a, wo_ref[...]) for a in att]
        one = [norm(x_ref[rs, :].astype(F32) + b + b_out) for rs, b in zip(both, branch)]
        normed = [n * gain_one + shift_one for n, _ in one]
        normed_low = [n.astype(BF16) for n in normed]
        pre, act_low, slope = [], [], []
        for n in range(2):
            pre.append(dot(normed_low[n], wu_ref[...]) + bup_ref[...])
        for n in range(2):
            cdf = 0.5 * (1.0 + lax.erf(pre[n] * math.sqrt(0.5)))
            act_low.append((pre[n] * cdf).astype(BF16))
            slope.append(cdf + pre[n] * (jnp.exp(-0.5 * pre[n] * pre[n]) * (1.0 / math.sqrt(2.0 * math.pi))))
        down = [dot(act, wd_ref[...]) for act in act_low]
        two = [norm(n + d + b_down) for n, d in zip(normed, down)]
        cot = [cot_ref[rs, :].astype(F32) for rs in both]
        for rs, (n, _) in zip(both, two):
            cot_ref[rs, :] = (n * gain_two + shift_two).astype(BF16)
        d_sum = [norm_back(c * gain_two, n, inverse) for c, (n, inverse) in zip(cot, two)]
        d_ffn = [d.astype(BF16) for d in d_sum]
        d_act = [dot(d, wd_ref[...], NT) for d in d_ffn]
        gd_ref[...] += dot(rows_of(act_low), rows_of(d_ffn), TN)
        d_pre = [(d * s).astype(BF16) for d, s in zip(d_act, slope)]
        d_normed = [a + dot(d, wu_ref[...], NT) for a, d in zip(d_sum, d_pre)]
        gu_ref[...] += dot(rows_of(normed_low), rows_of(d_pre), TN)
        d_first = [norm_back(d * gain_one, n, inverse) for d, (n, inverse) in zip(d_normed, one)]
        d_branch = [d.astype(BF16) for d in d_first]
        d_att = [dot(d, wo_ref[...], NT).astype(BF16) for d in d_branch]
        go_ref[...] += dot(rows_of(att), rows_of(d_branch), TN)
        for rs, d, a in zip(both, d_first, d_att):
            dfirst_ref[rs, :] = d
            da_ref[rs, :] = a
            turned = a.T
            dat_ref[:, rs] = turned
            for h in range(H):
                delta_ref[h : h + 1, rs] = column_sum(turned[head(h), :].astype(F32) * attt_ref[head(h), rs])
        pair_sum = lambda rows: column_sum(rows[0].astype(F32) + rows[1].astype(F32))
        up = pair_sum(d_pre)
        sums = [
            pair_sum(d_branch),
            pair_sum([d * n for d, (n, _) in zip(d_normed, one)]),
            pair_sum(d_normed),
            pair_sum(d_ffn),
            pair_sum([c * n for c, (n, _) in zip(cot, two)]),
            pair_sum(cot),
        ]
        for at in range(0, hidden, width):
            sums.append(up[:, at : at + width])
        small_ref[...] += jnp.concatenate(sums, axis=0)
        return carry

    lax.fori_loop(0, nq // 2, row_tiles, 0)


def attend_back(
    meta, brow_ref, start, tile, k_ref, v_ref, q_ref, qt_ref, da_ref, dat_ref, lse_ref, delta_ref, qm_ref,
    kt_ref, km_ref, dk_ref, dv_ref, dq_ref,
):
    nq = meta.nq
    first, last = tile_range(*meta.all_keys, start, nq)

    def rows_at(t):
        return pl.ds(pl.multiple_of((tile + t) * T, T), T)

    def blank(t, carry):
        for ref in (k_ref, v_ref):
            ref[rows_at(t), :] = jnp.zeros((T, ref.shape[1]), BF16)
        return carry

    def key_tile(t, carry):
        ks = rows_at(t)
        row = start + t * T
        q_first = sum((meta.hi(i) <= row).astype(jnp.int32) for i in range(nq))
        q_last = sum((meta.lo(i) < row + T).astype(jnp.int32) for i in range(nq))
        km_ref[...] = key_mask(brow_ref, row)
        kt_ref[...] = k_ref[ks, :].T
        dk_ref[...] = jnp.zeros_like(dk_ref)
        dv_ref[...] = jnp.zeros_like(dv_ref)

        def query_tile(i, inner):
            qs = pl.ds(pl.multiple_of(i * T, T), T)
            ps, ds, sums = [], [], []

            def products(h):
                sums.append((dot(ps[h], da_ref[qs, head(h)]), dot(ds[h], q_ref[qs, head(h)]), dot(kt_ref[head(h), :], ds[h])))

            for h in range(H):
                kx = jnp.concatenate([k_ref[ks, head(h)], km_ref[...]], axis=1)
                qx = jnp.concatenate([qt_ref[head(h), qs], qm_ref[i]], axis=0)
                p = jnp.exp2(dot(kx, qx) - lse_ref[h : h + 1, qs])
                ps.append(p.astype(BF16))
                dp = dot(v_ref[ks, head(h)], dat_ref[head(h), qs])
                ds.append((p * (dp - delta_ref[h : h + 1, qs])).astype(BF16))
                if h >= 2:
                    products(h - 2)
            products(H - 2)
            products(H - 1)
            dv_ref[...] += jnp.concatenate([out[0] for out in sums], axis=1)
            dk_ref[...] += jnp.concatenate([out[1] for out in sums], axis=1)
            dq_ref[:, qs] += jnp.concatenate([out[2] for out in sums], axis=0)
            return inner

        lax.fori_loop(q_first, q_last, query_tile, 0)
        k_ref[ks, :] = (dk_ref[...] * LN2).astype(BF16)
        v_ref[ks, :] = dv_ref[...].astype(BF16)
        return carry

    lax.fori_loop(0, first, blank, 0)
    lax.fori_loop(first, last, key_tile, 0)
    lax.fori_loop(last, nq, blank, 0)


def layer_kernel(
    nq,
    meta_ref, brow_ref, bv_ref, bup_ref, norm_ref, qm_ref, xw_ref, *refs,
):
    vectors, refs = refs[:6], refs[6:]
    count = 18
    sources, refs = refs[:count], refs[count:]
    layer_out, ig_out, pn_out, pf_out, pw_out, pp_out, keep_out, send_out = refs[:8]
    refs = refs[8:]
    staged, refs = refs[:count], refs[count:]
    sems, out_sems, grads_ref, ig_ref, k_ref, v_ref, vt_ref, km_ref, kn_ref, lse_ref, delta_ref, small_ref = refs[:12]
    att_ref, da_ref, dat_ref, gd_ref, gu_ref, go_ref, sum_ref = refs[12:19]
    kt_ref, mask_ref, dk_ref, dv_ref = refs[19:]
    loads = copies_of(sources, staged, sems)
    start(loads[:4])
    wk_ref, wv_ref, xn_ref, xf_ref, qt_ref, top_ref, total_ref, attt_ref = staged[:8]
    wo_ref, x_ref, wu_ref, wd_ref, cot_ref, q_ref, kc_ref, vc_ref, xp_ref, wq_ref = staged[8:]
    stores = []

    def store(source, target):
        copy = pltpu.make_async_copy(source, target, out_sems.at[len(stores)])
        copy.start()
        stores.append(copy)

    meta = Meta(meta_ref, nq)
    near_start = meta.side + meta.near_tile * T
    far_start = meta.side + meta.far_tile * T
    wait(loads[:2])
    start(loads[4:8])
    attend_far(
        meta, brow_ref,
        (
            ([], xw_ref, meta.forward, 2 * nq + 1),
            (loads[2:3], xn_ref, near_start, meta.near_tile),
            (loads[3:4], xf_ref, far_start, meta.far_tile),
        ),
        loads[4:8],
        loads[8:],
        wk_ref, wv_ref, bv_ref, qt_ref, norm_ref, qm_ref,
        k_ref, v_ref, att_ref, attt_ref, lse_ref, vt_ref, km_ref, kn_ref, top_ref, total_ref,
    )
    wait(loads[8:13])
    middle(
        nq, x_ref, cot_ref, att_ref, attt_ref, wo_ref, wu_ref, wd_ref, vectors, bup_ref,
        ig_ref, da_ref, dat_ref, delta_ref, small_ref, gd_ref, gu_ref, go_ref,
    )
    store(cot_ref, layer_out)
    hidden, width = wd_ref.shape
    shard = x_ref.shape[0]
    grads_ref[0:hidden, :] = gd_ref[...].astype(BF16)
    for part in range(hidden // width):
        at = hidden + part * width
        grads_ref[at : at + width, :] = gu_ref[:, part * width : (part + 1) * width].astype(BF16)
    base = 2 * hidden + width
    grads_ref[base - width : base, :] = go_ref[...].astype(BF16)
    half = grads_ref.shape[0] // 2
    assert half <= base
    first_core = meta.own_tile == 0

    def store_half(source, stays):
        copies = [pltpu.make_async_copy(source, target, out_sems.at[len(stores)]) for target in (keep_out, send_out)]
        pl.when(stays)(copies[0].start)
        pl.when(jnp.logical_not(stays))(copies[1].start)
        stores.append(copies[0])

    store_half(grads_ref.at[0:half, :], first_core)

    wait(loads[13:])
    xt_ref = vt_ref.at[:, 0:shard]
    dq_ref = attt_ref
    dwk_ref = gd_ref.at[0:width, :]
    dwv_ref = gd_ref.at[width : 2 * width, :]
    wkv_ref = wd_ref
    wkv_ref[0:width, :] = wk_ref[...].T
    wkv_ref[width : 2 * width, :] = wv_ref[...].T
    wo_ref[...] = wq_ref[...].T
    for ref in (dq_ref, dwk_ref, dwv_ref, sum_ref):
        ref[...] = jnp.zeros_like(ref)
    for rows, part_ref, out, first_row, tile, keys_ref, values_ref in (
        (xn_ref, xn_ref, pn_out, near_start, meta.near_tile, k_ref, v_ref),
        (xf_ref, xf_ref, pf_out, far_start, meta.far_tile, k_ref, v_ref),
        (xw_ref, att_ref, pw_out, meta.forward, 2 * nq + 1, k_ref, v_ref),
        (xp_ref, xp_ref, pp_out, meta.chip + meta.partner_tile * T, meta.partner_tile, kc_ref, vc_ref),
        (x_ref, None, None, meta.own, meta.own_tile, kc_ref, vc_ref),
    ):
        first, last = tile_range(*meta.all_keys, first_row, nq)

        def work(rows=rows, part_ref=part_ref, out=out, first_row=first_row, tile=tile, keys_ref=keys_ref, values_ref=values_ref):
            attend_back(
                meta, brow_ref, first_row, tile, keys_ref, values_ref, q_ref, qt_ref, da_ref, dat_ref,
                lse_ref, delta_ref, qm_ref, kt_ref, mask_ref, dk_ref, dv_ref, dq_ref,
            )
            block = pl.ds(pl.multiple_of(tile * T, T), shard)
            xt_ref[...] = rows[...].T
            dwk_ref[...] += dot(xt_ref[...], keys_ref[block, :])
            dwv_ref[...] += dot(xt_ref[...], values_ref[block, :])
            sum_ref[0:1, :] += column_sum(values_ref[block, :].astype(F32))

            def input_tile(t, carry):
                rs = pl.ds(pl.multiple_of(2 * t * T, 2 * T), 2 * T)
                ks = pl.ds(pl.multiple_of((tile + 2 * t) * T, T), 2 * T)
                grad = dot(jnp.concatenate([keys_ref[ks, :], values_ref[ks, :]], axis=1), wkv_ref[...])
                if out is None:
                    ig_ref[rs, :] += grad
                else:
                    part_ref[rs, :] = grad.astype(BF16)
                return carry

            lax.fori_loop(0, nq // 2, input_tile, 0)

        if out is None:
            work()
        else:
            pl.when(first < last)(work)

            @pl.when(first >= last)
            def _(part_ref=part_ref):
                part_ref[...] = jnp.zeros_like(part_ref)

            store(part_ref, out)

    dwk_low = dwk_ref[...].astype(BF16)
    dwv_low = dwv_ref[...].astype(BF16)

    def query_tile(i, carry):
        qs = pl.ds(pl.multiple_of(i * T, T), T)
        dq = (dq_ref[:, qs] * SCALE).astype(BF16).T
        q_ref[qs, :] = dq
        sum_ref[1:2, :] += column_sum(dq.astype(F32))
        ig_ref[qs, :] += dot(dq, wo_ref[...])
        return carry

    lax.fori_loop(0, nq, query_tile, 0)
    store(ig_ref, ig_out)
    grads_ref[base : base + width, :] = dot(xt_ref[...], q_ref[...]).astype(BF16)
    grads_ref[base + width : base + 2 * width, :] = dwk_low
    grads_ref[base + 2 * width : base + 3 * width, :] = dwv_low
    end = base + 3 * width
    rows = jnp.concatenate([sum_ref[...], small_ref[...]], axis=0)
    grads_ref[end : end + 16, :] = rows.astype(BF16)
    grads_ref[end + 16 :, :] = jnp.zeros((grads_ref.shape[0] - end - 16, width), BF16)
    store_half(grads_ref.at[half:, :], jnp.logical_not(first_core))
    wait(stores)


def vmem(count):
    return [pl.BlockSpec(memory_space=pltpu.VMEM)] * count


VMEM_LIMIT = 60 << 20


def call(kernel, inputs, staged, outputs, scratch, flops, scalars=1, out_scalars=0, limit=VMEM_LIMIT):
    size = lambda arrays: sum(math.prod(a.shape) * jnp.dtype(a.dtype).itemsize for a in arrays)
    everything = tuple(inputs) + tuple(staged)
    smem = [pl.BlockSpec(memory_space=pltpu.SMEM)]
    hbm = [pl.BlockSpec(memory_space=pltpu.HBM)]
    return pl.pallas_call(
        kernel,
        out_shape=outputs,
        in_specs=smem * scalars + vmem(len(inputs) - scalars) + hbm * len(staged),
        out_specs=smem * out_scalars + hbm * (len(outputs) - out_scalars),
        scratch_shapes=scratch,
        compiler_params=pltpu.CompilerParams(vmem_limit_bytes=limit),
        cost_estimate=pl.CostEstimate(
            flops=flops, bytes_accessed=size(everything) + size(outputs), transcendentals=0
        ),
    )(*everything)


def struct(shape, dtype):
    return jax.ShapeDtypeStruct(shape, dtype)


def after(value, other):
    return lax.optimization_barrier((value, other))[0]


class Summing:
    def __init__(self, dp, seq):
        dp_masks = [seq * (1 << j) for j in range(dp.bit_length() - 1)]
        seq_masks = [1 << j for j in range(seq.bit_length() - 1)]
        self.order = [(dp_masks[j], dp_masks[(j + 1) % len(dp_masks)]) for j in range(len(dp_masks))]
        self.dp_steps = len(self.order)
        self.order += [(mask, mask) for mask in seq_masks[1:]]
        self.devices = dp * seq
        core = lax.axis_index("seq") % 2
        index = lax.axis_index("dp") * seq + lax.axis_index("seq")
        self.bits = [jnp.where(core == 0, index // even, index // odd) % 2 for even, odd in self.order]

    def exchange(self, rows, even=1, odd=1):
        pairs = [(i, i ^ (even if i % 2 == 0 else odd)) for i in range(self.devices)]
        return lax.ppermute(rows, ("dp", "seq"), pairs)

    def halve(self, rows, number, other=None):
        half = rows.shape[0] // 2
        bit = self.bits[number]
        mine = lax.dynamic_slice_in_dim(rows, bit * half, half, 0)
        got = self.exchange(lax.dynamic_slice_in_dim(rows, (1 - bit) * half, half, 0), *self.order[number])
        return (mine if other is None else after(mine, other)) + got

    def whole(self, rows):
        return rows + self.exchange(rows, *self.order[-1])

    def double(self, rows, number, other=None):
        got = self.exchange(rows, *self.order[number])
        half = rows.shape[0]
        if other is not None:
            rows = after(rows, other)
        both = jnp.zeros((2 * half, rows.shape[1]), rows.dtype)
        both = lax.dynamic_update_slice_in_dim(both, rows, self.bits[number] * half, 0)
        return lax.dynamic_update_slice_in_dim(both, got, (1 - self.bits[number]) * half, 0)


def widen_kernel(bias_rows, core_ref, mine_one, mine_two, other_one, other_two, *refs):
    count = 6 + len(bias_rows)
    outs, wide, sems = refs[:count], refs[count : 2 * count], refs[2 * count]
    width = mine_one.shape[1]
    hidden = wide[0].shape[0]
    spans = [(0, hidden, 0, 0)]
    spans += [(hidden + at, width, 1, at) for at in range(0, hidden, width)]
    spans += [(2 * hidden + n * width, width, 2 + n, 0) for n in range(4)]
    copies = copies_of(wide, outs, sems)

    def write(*sources):
        bases = [sum(ref.shape[0] for ref in sources[:n]) for n in range(4)]
        for first_row, rows, number, column in spans:
            for source, base in zip(sources, bases):
                first, last = max(first_row, base), min(first_row + rows, base + source.shape[0])
                if first < last:
                    wide[number][first - first_row : last - first_row, column : column + width] = source[
                        first - base : last - base, :
                    ].astype(F32)
            if column + width == wide[number].shape[1]:
                copies[number].start()
        at = 2 * hidden + 4 * width - bases[3]
        vectors = sources[3][at : at + 16, :].astype(F32)
        for number, rows in enumerate(bias_rows):
            for part, row in enumerate(rows):
                wide[6 + number][:, part * width : (part + 1) * width] = vectors[row : row + 1, :]
            copies[6 + number].start()

    @pl.when(core_ref[0] == 0)
    def _():
        write(mine_one, mine_two, other_one, other_two)

    @pl.when(core_ref[0] != 0)
    def _():
        write(other_one, other_two, mine_one, mine_two)

    wait(copies)


def shards(
    tokens, counts, w_query, b_query, w_key, w_value, b_value, w_out, b_out, gain_one, shift_one,
    w_up, b_up, w_down, b_down, gain_two, shift_two, cotangent,
):
    shard, width = tokens.shape
    hidden = w_up.shape[1]
    nq = shard // T
    seq = lax.axis_size("seq")
    dp = lax.axis_size("dp")
    position = lax.axis_index("seq")

    def swap(rows):
        return lax.ppermute(rows, "seq", [(i, i ^ 1) for i in range(seq)])

    def near(rows):
        pairs = [(i, i + 1) for i in range(1, seq - 1, 2)]
        return lax.ppermute(rows, "seq", pairs + [(b, a) for a, b in pairs])

    def far(rows, back=False):
        pairs = [(i, i + 2) for i in range(0, seq - 2, 2)] + [(i, i - 2) for i in range(3, seq, 2)]
        return lax.ppermute(rows, "seq", [(b, a) for a, b in pairs] if back else pairs)

    x_partner = swap(tokens)
    x_near = near(tokens)
    x_far = far(tokens)

    core = position % 2
    row = lambda v: v.reshape(1, -1)
    tile_mask = struct((nq, LANES, T), BF16)
    stats = struct((8, shard), F32)

    def keys_scratch(tiles):
        return [
            pltpu.VMEM((width, tiles * T), BF16), pltpu.VMEM((tiles * T, LANES), BF16), pltpu.VMEM((8, LANES), F32)
        ]

    unit = 2 * shard * width * width
    chip_tiles, far_tiles = 2 * nq + 1, 3 * nq + 2
    keys = lambda tiles: struct((tiles * T, width), BF16)
    block = pltpu.VMEM((shard, width), BF16)
    weight = pltpu.VMEM((width, width), BF16)
    wide = pltpu.VMEM((width, shard), F32)
    square = pltpu.VMEM((width, width), F32)
    stat = pltpu.VMEM((8, shard), F32)
    part = struct((shard, width), BF16)
    meta, q, qt, k_chip, v_chip, top, total, acc, norms, qm, bounds = call(
        functools.partial(attend_chip_kernel, nq, seq),
        (counts, position.reshape(1).astype(jnp.int32), row(b_query), row(b_value), x_partner),
        (tokens, w_query, w_key, w_value),
        (
            struct((2 * nq + 5,), jnp.int32),
            part, struct((width, shard), BF16), keys(chip_tiles), keys(chip_tiles), stats, stats,
            struct((width, shard), F32), struct((8, LANES), F32), tile_mask, struct((8, LANES), jnp.int32),
        ),
        [
            block, pltpu.VMEM((width, shard), BF16), pltpu.VMEM((chip_tiles * T, width), BF16),
            pltpu.VMEM((chip_tiles * T, width), BF16), stat, stat, wide, pltpu.VMEM((8, LANES), F32),
            pltpu.VMEM((nq, LANES, T), BF16), pltpu.VMEM((8, LANES), jnp.int32),
        ]
        + keys_scratch(chip_tiles)
        + [block, weight, weight, weight, pltpu.SemaphoreType.DMA((4,)), pltpu.SemaphoreType.DMA((10,))],
        13 * unit,
        scalars=2,
        out_scalars=1,
    )
    x_forward = swap(after(x_near, norms))

    granule = 8 * dp * seq // 2
    grad_rows = (2 * hidden + 4 * width + 16 + granule - 1) // granule * granule
    vectors = [row(v) for v in (b_out, gain_one, shift_one, b_down, gain_two, shift_two)]
    layer, input_grad, p_near, p_far, p_forward, p_partner, keep, send = call(
        functools.partial(layer_kernel, nq),
        (meta, bounds, row(b_value), row(b_up), norms, qm, x_forward, *vectors),
        (
            w_key, w_value, x_near, x_far, qt, top, total, acc,
            w_out, tokens, w_up, w_down, cotangent, q, k_chip, v_chip, x_partner, w_query,
        ),
        (
            part, struct((shard, width), F32), part, part, part, part,
            struct((grad_rows // 2, width), BF16), struct((grad_rows // 2, width), BF16),
        ),
        [
            weight, weight, block, block, pltpu.VMEM((width, shard), BF16), stat, stat, wide,
            weight, block, pltpu.VMEM((width, hidden), BF16), pltpu.VMEM((hidden, width), BF16), block, block,
            pltpu.VMEM((chip_tiles * T, width), BF16), pltpu.VMEM((chip_tiles * T, width), BF16), block, weight,
            pltpu.SemaphoreType.DMA((18,)), pltpu.SemaphoreType.DMA((8,)),
            pltpu.VMEM((grad_rows, width), BF16), pltpu.VMEM((shard, width), F32),
            pltpu.VMEM((far_tiles * T, width), BF16), pltpu.VMEM((far_tiles * T, width), BF16),
        ]
        + keys_scratch(far_tiles)
        + [stat, stat, pltpu.VMEM((8, width), F32)]
        + [block, block, pltpu.VMEM((width, shard), BF16)]
        + [pltpu.VMEM((hidden, width), F32), pltpu.VMEM((width, hidden), F32), square]
        + [pltpu.VMEM((8, width), F32)]
        + [
            pltpu.VMEM((width, T), BF16), pltpu.VMEM((T, LANES), BF16),
            pltpu.VMEM((T, width), F32), pltpu.VMEM((T, width), F32),
        ],
        60 * unit,
    )
    summing = Summing(dp, seq)
    p_forward = swap(p_forward)
    grads = keep + summing.exchange(send)
    p_far = far(after(p_far, grads), back=True)
    p_partner = swap(after(p_partner, grads))
    p_near = p_near + p_forward
    unit = 8 << (len(summing.order) - 1)
    lead = (grad_rows // 2 // unit + 1) // 2 * unit
    one, two = grads[:lead], grads[lead:]
    dp_steps = summing.dp_steps
    steps = list(range(len(summing.order) - 1))
    others = {dp_steps: p_far}
    for number in steps:
        one = summing.halve(one, number, others.get(number))
        if number == 0:
            two = after(two, one)
    for number in steps:
        two = summing.halve(two, number)
    one, two = summing.whole(one), summing.whole(two)
    for number in steps[dp_steps:][::-1]:
        one, two = summing.double(one, number), summing.double(two, number)
    p_near = near(after(p_near, two))
    for number in steps[:dp_steps][::-1]:
        one = summing.double(one, number)
        two = summing.double(two, number, p_near if number == 0 else None)
    mine = (one, two)
    other = tuple(summing.exchange(rows) for rows in mine)
    input_grad = input_grad + p_partner.astype(F32) + p_far.astype(F32) + p_near.astype(F32)
    bias_rows = [(0,), (1,)] + [(n,) for n in range(8, 14)] + [tuple(range(14, 14 + hidden // width))]
    shapes = [(hidden, width), (width, hidden)] + [(width, width)] * 4
    shapes += [(1, len(rows) * width) for rows in bias_rows]
    wide_grads = call(
        functools.partial(widen_kernel, bias_rows),
        (core.reshape(1).astype(jnp.int32), *mine, *other),
        (),
        [struct(shape, F32) for shape in shapes],
        [pltpu.VMEM(shape, F32) for shape in shapes] + [pltpu.SemaphoreType.DMA((len(shapes),))],
        0,
        limit=20 << 20,
    )
    g_w_down, g_w_up, g_w_out, g_w_query, g_w_key, g_w_value = wide_grads[:6]
    g_b_value, g_b_query, g_b_out, g_gain_one, g_shift_one, g_b_down, g_gain_two, g_shift_two, g_b_up = (
        v.reshape(-1) for v in wide_grads[6:]
    )
    return (
        layer, input_grad, g_w_query, g_b_query, g_w_key, g_w_value, g_b_value, g_w_out, g_b_out,
        g_gain_one, g_shift_one, g_w_up, g_b_up, g_w_down, g_b_down, g_gain_two, g_shift_two,
    )


def solution(mesh):
    rows = P(("dp", "seq"), None)
    return jax.shard_map(
        shards,
        mesh=mesh,
        in_specs=(rows, P("dp", None)) + (P(),) * 15 + (rows,),
        out_specs=(rows, rows) + (P(),) * 15,
        check_vma=False,
    )
```
